256 devices in a mesh: dom: 128 (over x, z, y), edge: 2 (over core).
Axes of the slice: x: 4, y: 4, z: 8, core: 2. Of those that a mesh axis runs over, the one named last changes fastest.
Arguments:
- node_feats: bfloat16 [131072, 128], P('dom'), may hold values from -6 to 6
- hub_feats: bfloat16 [4096, 128], P('dom'), may hold values from -6 to 6
- w_self: bfloat16 [128, 128], replicated, may hold values from -0.5 to 0.5
- w_neigh: bfloat16 [128, 128], replicated, may hold values from -0.75 to 0.75
- bias: float32 [128], replicated, may hold values from -4 to 4
- cotangent: bfloat16 [131072, 128], P('dom'), may hold values from -6 to 6
- send_count: int32 [128, 128], P('dom'), may hold values from 0 to 128, as said below
- send_rows: int32 [128, 128, 128], P('dom'), may hold values from 0 to 1023, as said below
- edge_src: int32 [128, 2, 8192], P('dom', 'edge'), may hold values from 0 to 21503, as said below
- edge_dst: int32 [128, 2, 8192], P('dom', 'edge'), may hold values from 0 to 1023
- edge_count: int32 [128, 2], P('dom', 'edge'), may hold values from 2048 to 8192, as said below
Outputs:
- layer_out: bfloat16 [131072, 128], P('dom')
- grad_feats: float32 [131072, 128], P('dom')
- grad_hubs: float32 [4096, 128], P('dom')
- grad_self: float32 [128, 128], replicated
- grad_neigh: float32 [128, 128], replicated
- grad_bias: float32 [128], replicated
The draws below stay inside these ranges and needn't reach their ends.
Inputs may be any that keep to these rules, and one draw needn't show every extreme that they name: send_count[p, p] is 0; otherwise at least 32; every partition p sends exactly 128 rows to partition (p + 1) mod 128. `send_rows`: rows of the sending partition; rows may repeat within a block. `edge_src`: every slot names a row of the source table: an own node, a live slot of a block from another partition, or a hub; slots at or beyond edge_count are ignored. `edge_count`: in every partition one of the two halves is full with 8192 live slots.
All inputs are finite; a program needn't handle non-finite values.
Results may differ from the reference program's by a relative error of at most 0.008.
Values may be sent and summed in bfloat16 or wider, within the bound.
No kernel may reach another device: no remote copies, remote signals or barrier semaphores. Data moves between devices by JAX's collectives and lax.ppermute only.
A program may use at most 128 MiB of HBM per device.

```python
import jax
import jax.numpy as jnp
from jax import lax

F = 128
H = 128
NLOC = 1024
EDGE_DEV = 8192
BR = 128
HUBS = 4096
NODES = 131072
N_DOM = 128


def counts_table(key):
    key = jax.random.fold_in(key, 101)
    counts = jax.random.randint(key, (N_DOM, N_DOM), BR // 4, BR + 1)
    indices = jnp.arange(N_DOM, dtype=jnp.int32)
    counts = jnp.where(indices[None, :] == (indices[:, None] + 1) % N_DOM, BR, counts)
    counts = jnp.where(indices[:, None] == indices[None, :], 0, counts)
    return counts.astype(jnp.int32)


def draw_send_count(key, part):
    return counts_table(key)


def draw_send_rows(key, part):
    key = jax.random.fold_in(key, 3)
    return jax.random.randint(key, (N_DOM, N_DOM, BR), 0, NLOC).astype(jnp.int32)


def draw_edge_src(key, part):
    counts = counts_table(key)
    key = jax.random.fold_in(key, 5)
    key_kind, key_local, key_peer, key_slot, key_hub = jax.random.split(key, 5)
    shape = (N_DOM, 2, EDGE_DEV)
    choose = jax.random.randint(key_kind, shape, 0, 20)
    local_pick = jax.random.randint(key_local, shape, 0, NLOC)
    receiver = jnp.arange(N_DOM, dtype=jnp.int32)[:, None, None]
    sender = (receiver + 1 + jax.random.randint(key_peer, shape, 0, N_DOM - 1)) % N_DOM
    pair_count = counts[sender, receiver]
    slot_pick = jax.random.randint(key_slot, shape, 0, 1 << 20) % pair_count
    boundary_pick = NLOC + sender * BR + slot_pick
    hub_pick = NLOC + N_DOM * BR + jax.random.randint(key_hub, shape, 0, HUBS)
    picked = jnp.where(choose < 10, local_pick, jnp.where(choose < 17, boundary_pick, hub_pick))
    return picked.astype(jnp.int32)


def draw_edge_dst(key, part):
    key = jax.random.fold_in(key, 7)
    return jax.random.randint(key, (N_DOM, 2, EDGE_DEV), 0, NLOC).astype(jnp.int32)


def draw_edge_count(key, part):
    key = jax.random.fold_in(key, 11)
    key_full, key_other = jax.random.split(key)
    full_half = jax.random.randint(key_full, (N_DOM,), 0, 2)
    other = jax.random.randint(key_other, (N_DOM,), EDGE_DEV // 4, EDGE_DEV + 1)
    halves = jnp.arange(2, dtype=jnp.int32)[None, :]
    return jnp.where(halves == full_half[:, None], EDGE_DEV, other[:, None]).astype(jnp.int32)


def level_of(stream_key, shape, cuts, smallest, largest):
    factor_of, own = 1.0, jax.random.fold_in(stream_key, 6)
    for axis_at, parts in cuts:
        heights = jnp.exp(jax.random.uniform(jax.random.fold_in(own, axis_at), (parts,), jnp.float32, smallest / len(cuts), largest / len(cuts)))
        factor_of = factor_of * jnp.repeat(heights, shape[axis_at] // parts).reshape([-1 if axis == axis_at else 1 for axis in range(len(shape))])
    return factor_of


def bell_draw(rng, shape, width, limit, cuts=(), kind=jnp.bfloat16):
    entries = jax.random.normal(rng, shape, jnp.float32) * width
    if len(cuts) > 0:
        entries = level_of(rng, shape, cuts, -0.22, 0.18) * entries
    return jnp.clip(entries, min=-limit, max=limit).astype(kind)


def setup_inputs(seed: int = 0) -> dict:
    keys = jax.random.split(jax.random.key(seed), 12)
    return {
        "node_feats": bell_draw(keys[0], (NODES, F), 1.0, 6.0, ((0, 128),)),
        "hub_feats": bell_draw(keys[1], (HUBS, F), 1.0, 6.0, ((0, 128),)),
        "w_self": bell_draw(keys[2], (F, H), F ** -0.5, 0.5),
        "w_neigh": bell_draw(keys[3], (F, H), (F // 2) ** -0.5, 0.75),
        "bias": bell_draw(keys[4], (H,), 1.0, 4.0, (), jnp.float32),
        "cotangent": bell_draw(keys[5], (NODES, H), 1.0, 6.0, ((0, 128),)),
        "send_count": draw_send_count(jax.random.fold_in(keys[11], 71), 0),
        "send_rows": draw_send_rows(jax.random.fold_in(keys[11], 71), 0),
        "edge_src": draw_edge_src(jax.random.fold_in(keys[11], 71), 0),
        "edge_dst": draw_edge_dst(jax.random.fold_in(keys[11], 71), 0),
        "edge_count": draw_edge_count(jax.random.fold_in(keys[11], 71), 0),
    }


def silu_slope(value):
    sig = jax.nn.sigmoid(value)
    return sig * (1.0 + value * (1.0 - sig))


def reference(node_feats, hub_feats, w_self, w_neigh, bias, cotangent, send_count, send_rows, edge_src, edge_dst, edge_count):
    table_len = NLOC + N_DOM * BR + HUBS
    slot_ids = jnp.arange(BR, dtype=jnp.int32)
    peer_ids = jnp.arange(N_DOM, dtype=jnp.int32)
    edge_ids = jnp.arange(EDGE_DEV, dtype=jnp.int32)

    def source_of(peer):
        send_idx = send_rows[:, peer, :]
        live_mask = slot_ids[None, :] < send_count[:, peer][:, None]
        received = node_feats[(peer_ids[:, None] * NLOC + send_idx).astype(jnp.int32)]
        received = jnp.where(live_mask[:, :, None], received, jnp.zeros((), jnp.bfloat16))
        own_rows = lax.dynamic_slice_in_dim(node_feats, (peer * NLOC).astype(jnp.int32), NLOC, 0)
        return jnp.concatenate([own_rows, received.reshape(N_DOM * BR, F), hub_feats], axis=0)

    def forward_part(peer):
        source_table = source_of(peer)
        live_mask = (edge_ids[None, :] < edge_count[peer][:, None]).reshape(-1).astype(jnp.float32)
        values = source_table[edge_src[peer].reshape(-1)].astype(jnp.float32) * live_mask[:, None]
        totals = jax.ops.segment_sum(values, edge_dst[peer].reshape(-1), NLOC)
        degree = jax.ops.segment_sum(live_mask, edge_dst[peer].reshape(-1), NLOC)
        return totals, degree

    totals, degree = lax.map(forward_part, peer_ids)
    totals = totals.reshape(NODES, F)
    divisor = jnp.maximum(degree.reshape(NODES), 1.0)[:, None]
    aggregate = (totals / divisor).astype(jnp.bfloat16)
    preact = jnp.dot(node_feats, w_self, preferred_element_type=jnp.float32) + jnp.dot(aggregate, w_neigh, preferred_element_type=jnp.float32) + bias
    layer_out = jax.nn.silu(preact).astype(jnp.bfloat16)
    grad_pre = (cotangent.astype(jnp.float32) * silu_slope(preact)).astype(jnp.bfloat16)
    dims = (((0,), (0,)), ((), ()))
    grad_self = lax.dot_general(node_feats, grad_pre, dims, preferred_element_type=jnp.float32)
    grad_neigh = lax.dot_general(aggregate, grad_pre, dims, preferred_element_type=jnp.float32)
    grad_bias = jnp.sum(grad_pre.astype(jnp.float32), axis=0)
    grad_sum = (jnp.dot(grad_pre, w_neigh.T, preferred_element_type=jnp.float32) / divisor).astype(jnp.bfloat16)
    grad_input = jnp.dot(grad_pre, w_self.T, preferred_element_type=jnp.float32)

    def backward_part(carry, peer):
        node_acc, hub_acc = carry
        grad_rows = lax.dynamic_slice_in_dim(grad_sum, (peer * NLOC).astype(jnp.int32), NLOC, 0)
        local_acc = jnp.zeros((NLOC, F), jnp.float32)
        bound_acc = jnp.zeros((N_DOM * BR, F), jnp.float32)
        send_idx = (peer_ids[:, None] * NLOC + send_rows[:, peer, :]).reshape(-1).astype(jnp.int32)
        live_slots = (slot_ids[None, :] < send_count[:, peer][:, None]).reshape(-1, 1).astype(jnp.float32)
        for half_idx in range(2):
            live_mask = (edge_ids < edge_count[peer, half_idx]).astype(jnp.float32)
            values = grad_rows[edge_dst[peer, half_idx]].astype(jnp.float32) * live_mask[:, None]
            table_grad = jax.ops.segment_sum(values, edge_src[peer, half_idx], table_len)
            local_acc = local_acc + table_grad[:NLOC]
            hub_acc = hub_acc + table_grad[NLOC + N_DOM * BR:]
            bound_acc = bound_acc + table_grad[NLOC:NLOC + N_DOM * BR]
        bound_b = lax.optimization_barrier(bound_acc.astype(jnp.bfloat16))
        node_acc = node_acc.at[send_idx].add(bound_b.astype(jnp.float32) * live_slots)
        start = (peer * NLOC).astype(jnp.int32)
        old_rows = lax.dynamic_slice_in_dim(node_acc, start, NLOC, 0)
        node_acc = lax.dynamic_update_slice_in_dim(node_acc, old_rows + local_acc, start, 0)
        return (node_acc, hub_acc), None

    init = (jnp.zeros((NODES, F), jnp.float32), jnp.zeros((HUBS, F), jnp.float32))
    (node_acc, hub_acc), _ = lax.scan(backward_part, init, peer_ids)
    grad_feats = grad_input + node_acc
    return layer_out, grad_feats, hub_acc, grad_self, grad_neigh, grad_bias
```

```python
import functools

import jax
import jax.numpy as jnp
from jax import lax
from jax.experimental import pallas as pl
from jax.experimental.pallas import tpu as pltpu
from jax.sharding import PartitionSpec as P

F32 = jnp.float32
BF16 = jnp.bfloat16
VMEM = pltpu.VMEM
SMEM = pltpu.SMEM
SWAP = [(0, 1), (1, 0)]
CHUNK = 256
DST_BITS = 10
PAD = 1 << 30
DEAD = 1 << 26
HALF_BIT = 24


def params(mib=40):
    return pltpu.CompilerParams(vmem_limit_bytes=mib * 1024 * 1024)


def vspec():
    return pl.BlockSpec(memory_space=VMEM)


def sspec():
    return pl.BlockSpec(memory_space=SMEM)


def columns_of(row):
    parts = []
    for at in range(0, row.shape[1], 128):
        parts.append(jnp.broadcast_to(row[:, at : at + 128], (128, 128)).T)
    return jnp.concatenate(parts, axis=0)


def onehot_of_columns(col, width):
    lane = lax.broadcasted_iota(jnp.int32, col.shape, 1)
    parts = [
        jnp.where(col == lane + at, 1.0, 0.0).astype(BF16) for at in range(0, width, 128)
    ]
    return jnp.concatenate(parts, axis=1)


def onehot_of_rows(row, height):
    sub = lax.broadcasted_iota(jnp.int32, (height, row.shape[1]), 0)
    return jnp.where(sub == row, 1.0, 0.0).astype(BF16)


def dot(a, b):
    return jnp.dot(a, b, preferred_element_type=F32)


def dot_nt(a, b):
    return lax.dot_general(a, b, (((1,), (1,)), ((), ())), preferred_element_type=F32)


def dot_tn(a, b):
    return lax.dot_general(a, b, (((0,), (0,)), ((), ())), preferred_element_type=F32)


def outgoing_kernel(slots, idx_ref, feat_ref, hub_ref, out_ref):
    step = pl.program_id(0)
    peers = out_ref.shape[0]
    hubs = hub_ref.shape[0]
    rows = feat_ref.shape[0]
    for pair in range(peers // 4):
        at = step * (peers // 2) + pair * 2
        idx = [idx_ref[pl.ds(at + k, 1), :] for k in range(2)]
        hot = onehot_of_columns(columns_of(jnp.concatenate(idx, axis=1)), rows)
        picked = dot(hot, feat_ref[...]).astype(BF16)
        for k in range(4):
            out_ref[pair * 4 + k, :slots, :] = picked[k * slots : (k + 1) * slots]
            out_ref[pair * 4 + k, slots:, :] = hub_ref[...]


def outgoing(idx, feats, hub_rows, slots, step_peers=8):
    peers = idx.shape[0] * idx.shape[1] // slots
    hubs, width = hub_rows.shape
    return pl.pallas_call(
        functools.partial(outgoing_kernel, slots),
        grid=(peers // step_peers,),
        in_specs=[
            pl.BlockSpec(idx.shape, lambda i: (0, 0)),
            pl.BlockSpec(feats.shape, lambda i: (0, 0)),
            pl.BlockSpec(hub_rows.shape, lambda i: (0, 0)),
        ],
        out_specs=pl.BlockSpec((step_peers, slots + hubs, width), lambda i: (i, 0, 0)),
        out_shape=jax.ShapeDtypeStruct((peers, slots + hubs, width), BF16),
        compiler_params=params(),
        name="outgoing_rows",
    )(idx, feats, hub_rows)


def own_forward_kernel(count_ref, every_ref, keys_ref, own_ref, sum_ref, deg_ref):
    nodes = sum_ref.shape[0]
    own_rows = own_ref.shape[0]
    deg_ref[...] = jnp.zeros_like(deg_ref)
    sum_ref[...] = jnp.zeros_like(sum_ref)

    def degrees(c, _):
        key = every_ref[pl.ds(c, 1), :]
        dst = key & (nodes - 1)
        high = jnp.where(key < DEAD, dst >> 7, deg_ref.shape[0])
        deg_ref[...] += dot_nt(
            onehot_of_rows(high, deg_ref.shape[0]), onehot_of_rows(dst & 127, 128)
        )
        return 0

    lax.fori_loop(0, every_ref.shape[0], degrees, 0)

    def chunk(c, _):
        key = keys_ref[pl.ds(c, 1), :]
        hot = onehot_of_columns(columns_of(key >> DST_BITS), own_rows)
        values = dot(hot, own_ref[...]).astype(BF16)
        sum_ref[...] += dot(onehot_of_rows(key & (nodes - 1), nodes), values)
        return 0

    lax.fori_loop(0, pl.cdiv(count_ref[0], CHUNK), chunk, 0)


def own_forward(counts, every, keys, own, nodes):
    return pl.pallas_call(
        own_forward_kernel,
        in_specs=[sspec(), vspec(), vspec(), vspec()],
        out_specs=[vspec(), vspec()],
        out_shape=[
            jax.ShapeDtypeStruct((nodes, own.shape[1]), F32),
            jax.ShapeDtypeStruct((16, 128), F32),
        ],
        compiler_params=params(),
        name="own_forward",
    )(counts, every, keys, own)


def received_forward_kernel(
    own_rows, count_ref, low_ref, high_ref, keys_ref, table_ref, base_ref, sum_ref, values_ref
):
    nodes = sum_ref.shape[0]
    blocks = table_ref.shape[0] // CHUNK
    sum_ref[...] = base_ref[...]

    def chunk(c, _):
        key = keys_ref[pl.ds(c, 1), :]
        col = columns_of((key >> DST_BITS) - own_rows)
        values_ref[...] = jnp.zeros_like(values_ref)

        def block(b, _):
            hot = onehot_of_columns(col - b * CHUNK, CHUNK)
            start = pl.multiple_of(b * CHUNK, CHUNK)
            values_ref[...] += dot(hot, table_ref[pl.ds(start, CHUNK), :])
            return 0

        first = jnp.maximum(low_ref[c] - own_rows, 0) // CHUNK
        last = jnp.minimum(jnp.maximum(high_ref[c] - own_rows, 0) // CHUNK, blocks - 1)
        lax.fori_loop(first, last + 1, block, 0)
        sum_ref[...] += dot(
            onehot_of_rows(key & (nodes - 1), nodes), values_ref[...].astype(BF16)
        )
        return 0

    lax.fori_loop(count_ref[0] // CHUNK, pl.cdiv(count_ref[1], CHUNK), chunk, 0)


def received_forward(counts, low, high, keys, table, base, own_rows):
    return pl.pallas_call(
        functools.partial(received_forward_kernel, own_rows),
        in_specs=[sspec(), sspec(), sspec(), vspec(), vspec(), vspec()],
        out_specs=vspec(),
        out_shape=jax.ShapeDtypeStruct(base.shape, F32),
        scratch_shapes=[VMEM((CHUNK, base.shape[1]), F32)],
        compiler_params=params(),
        name="received_forward",
    )(counts, low, high, keys, table, base)


def dense_kernel(
    half_ref,
    mine_ref,
    other_ref,
    deg_ref,
    feat_ref,
    cot_ref,
    w_self_ref,
    w_neigh_ref,
    bias_ref,
    out_ref,
    grad_sum_ref,
    grad_input_ref,
    grad_w_ref,
    left_ref,
    pre_ref,
):
    nodes = feat_ref.shape[0]
    grad_bias = jnp.zeros((8, 128), F32)
    for at in range(0, nodes, 128):
        span = pl.ds(at, 128)
        h = at // 128
        divisor = jnp.maximum(columns_of(deg_ref[h : h + 1, :]), 1.0)
        feats = feat_ref[span, :]
        aggregate = ((mine_ref[span, :] + other_ref[span, :]) / divisor).astype(BF16)
        preact = dot(feats, w_self_ref[...]) + dot(aggregate, w_neigh_ref[...]) + bias_ref[...]
        sig = jax.nn.sigmoid(preact)
        out_ref[span, :] = (preact * sig).astype(BF16)
        slope = sig * (1.0 + preact * (1.0 - sig))
        grad_pre = (cot_ref[span, :].astype(F32) * slope).astype(BF16)
        pre_ref[span, :] = grad_pre
        grad_sum_ref[span, :] = (dot_nt(grad_pre, w_neigh_ref[...]) / divisor).astype(BF16)
        grad_input_ref[span, :] = dot_nt(grad_pre, w_self_ref[...])
        left_ref[span, :] = jnp.where(half_ref[0] == 0, feats.astype(F32), aggregate.astype(F32)).astype(BF16)
        wide = grad_pre.astype(F32)
        for r in range(0, 128, 8):
            grad_bias = grad_bias + wide[r : r + 8]
    grad_w_ref[:128, :] = dot_tn(left_ref[...], pre_ref[...])
    grad_w_ref[128:136, :] = jnp.broadcast_to(
        jnp.sum(grad_bias, axis=0, keepdims=True), (8, 128)
    )


def dense(half, mine, other, deg, feats, cot, w_self, w_neigh, bias):
    nodes, width = feats.shape
    return pl.pallas_call(
        dense_kernel,
        in_specs=[sspec()] + [vspec()] * 8,
        out_specs=[vspec()] * 4,
        out_shape=[
            jax.ShapeDtypeStruct((nodes, width), BF16),
            jax.ShapeDtypeStruct((nodes, width), BF16),
            jax.ShapeDtypeStruct((nodes, width), F32),
            jax.ShapeDtypeStruct((136, width), F32),
        ],
        scratch_shapes=[VMEM((nodes, width), BF16), VMEM((nodes, width), BF16)],
        compiler_params=params(),
        name="dense_part",
    )(half, mine, other, deg, feats, cot, w_self, w_neigh, bias)


def received_backward_kernel(
    own_rows, count_ref, low_ref, high_ref, keys_ref, grad_ref, out_ref, acc_ref, values_ref
):
    nodes = grad_ref.shape[0]
    blocks = acc_ref.shape[0] // CHUNK

    def clear(b, _):
        acc_ref[pl.ds(pl.multiple_of(b * CHUNK, CHUNK), CHUNK), :] = jnp.zeros(
            (CHUNK, acc_ref.shape[1]), F32
        )
        return 0

    lax.fori_loop(0, blocks, clear, 0)

    def chunk(c, _):
        key = keys_ref[pl.ds(c, 1), :]
        row = (key >> DST_BITS) - own_rows
        hot = onehot_of_columns(columns_of(key & (nodes - 1)), nodes)
        values_ref[...] = dot(hot, grad_ref[...]).astype(BF16)

        def block(b, _):
            start = pl.multiple_of(b * CHUNK, CHUNK)
            acc_ref[pl.ds(start, CHUNK), :] += dot(
                onehot_of_rows(row - b * CHUNK, CHUNK), values_ref[...]
            )
            return 0

        first = jnp.maximum(low_ref[c] - own_rows, 0) // CHUNK
        last = jnp.minimum(jnp.maximum(high_ref[c] - own_rows, 0) // CHUNK, blocks - 1)
        lax.fori_loop(first, last + 1, block, 0)
        return 0

    lax.fori_loop(count_ref[0] // CHUNK, pl.cdiv(count_ref[1], CHUNK), chunk, 0)

    def finish(b, _):
        span = pl.ds(pl.multiple_of(b * CHUNK, CHUNK), CHUNK)
        out_ref[span, :] = acc_ref[span, :].astype(BF16)
        return 0

    lax.fori_loop(0, blocks, finish, 0)


def received_backward(counts, low, high, keys, grad_sum, own_rows, table_rows):
    width = grad_sum.shape[1]
    return pl.pallas_call(
        functools.partial(received_backward_kernel, own_rows),
        in_specs=[sspec(), sspec(), sspec(), vspec(), vspec()],
        out_specs=vspec(),
        out_shape=jax.ShapeDtypeStruct((table_rows, width), BF16),
        scratch_shapes=[VMEM((table_rows, width), F32), VMEM((CHUNK, width), BF16)],
        compiler_params=params(),
        name="received_backward",
    )(counts, low, high, keys, grad_sum)


def own_backward_kernel(count_ref, keys_ref, grad_ref, out_ref):
    nodes = grad_ref.shape[0]
    own_rows = out_ref.shape[0]
    out_ref[...] = jnp.zeros_like(out_ref)

    def chunk(c, _):
        key = keys_ref[pl.ds(c, 1), :]
        hot = onehot_of_columns(columns_of(key & (nodes - 1)), nodes)
        values = dot(hot, grad_ref[...]).astype(BF16)
        out_ref[...] += dot(onehot_of_rows(key >> DST_BITS, own_rows), values)
        return 0

    lax.fori_loop(0, pl.cdiv(count_ref[0], CHUNK), chunk, 0)


def own_backward(counts, keys, grad_sum, own_rows):
    return pl.pallas_call(
        own_backward_kernel,
        in_specs=[sspec(), vspec(), vspec()],
        out_specs=vspec(),
        out_shape=jax.ShapeDtypeStruct((own_rows, grad_sum.shape[1]), F32),
        compiler_params=params(),
        name="own_backward",
    )(counts, keys, grad_sum)


def returned_kernel(slots, half_ref, idx_ref, back_ref, own_ref, part_ref, hub_ref):
    nodes = part_ref.shape[0]
    own_rows = own_ref.shape[0]
    peers = back_ref.shape[0]
    width = back_ref.shape[2]
    part_ref[...] = jnp.zeros_like(part_ref)
    part_ref[pl.ds(pl.multiple_of(half_ref[0] * own_rows, own_rows), own_rows), :] = own_ref[...]
    hub_ref[...] = jnp.zeros_like(hub_ref)

    def step(s, _):
        idx = jnp.concatenate([idx_ref[pl.ds(s * 4 + k, 1), :] for k in range(4)], axis=1)
        rows = back_ref[pl.ds(s * 8, 8), :slots, :].reshape(8 * slots, width)
        part_ref[...] += dot(onehot_of_rows(idx, nodes), rows)
        for k in range(8):
            hub_ref[...] += back_ref[s * 8 + k, slots:, :].astype(F32)
        return 0

    lax.fori_loop(0, peers // 8, step, 0)


def returned_sum(half, idx, back, own, nodes, slots):
    width = back.shape[2]
    return pl.pallas_call(
        functools.partial(returned_kernel, slots),
        in_specs=[sspec(), vspec(), vspec(), vspec()],
        out_specs=[vspec(), vspec()],
        out_shape=[
            jax.ShapeDtypeStruct((nodes, width), F32),
            jax.ShapeDtypeStruct((back.shape[1] - slots, width), F32),
        ],
        compiler_params=params(),
        name="returned_sum",
    )(half, idx, back, own)


def tree_sum(value, masks, size):
    parts = [value] + [
        lax.ppermute(value, "dom", [(i, i ^ m) for i in range(size)]) for m in masks
    ]
    while len(parts) > 1:
        parts = [parts[i] + parts[i + 1] for i in range(0, len(parts), 2)]
    return parts[0]


def body(
    node_feats,
    hub_feats,
    w_self,
    w_neigh,
    bias,
    cotangent,
    send_count,
    send_rows,
    edge_src,
    edge_dst,
    edge_count,
):
    num_dom = lax.axis_size("dom")
    half = lax.axis_index("edge")
    nodes, width = node_feats.shape
    block_rows = send_rows.shape[2]
    hubs = hub_feats.shape[0]
    slots, half_hubs, own_rows = block_rows // 2, hubs // 2, nodes // 2
    per_peer = slots + half_hubs
    half_scalar = half.astype(jnp.int32).reshape(1)

    slot_ids = jnp.arange(block_rows, dtype=jnp.int32)[None, :]
    idx_all = jnp.where(slot_ids < send_count[0][:, None], send_rows[0], nodes + 1024)
    idx = jnp.where(half == 0, idx_all[:, 0::2], idx_all[:, 1::2])
    idx = idx.reshape(num_dom * slots // 128, 128)
    hub_half = lax.dynamic_slice_in_dim(hub_feats, half * half_hubs, half_hubs, 0)
    own_half = lax.dynamic_slice_in_dim(node_feats, half * own_rows, own_rows, 0)
    out_rows = outgoing(idx, node_feats, hub_half, slots)
    table = lax.all_to_all(out_rows, "dom", split_axis=0, concat_axis=0, tiled=True)

    src = edge_src.reshape(-1)
    dst = edge_dst.reshape(-1)
    edges = src.shape[0]
    live = jnp.arange(edges, dtype=jnp.int32) < edge_count.reshape(())
    slot = src - nodes
    hub = slot - num_dom * block_rows
    is_own, is_hub = src < nodes, hub >= 0
    peer = slot // block_rows
    place = slot % block_rows
    row = jnp.where(
        is_own,
        src % own_rows,
        own_rows
        + jnp.where(
            is_hub,
            (hub // hubs) * per_peer + slots + hub % half_hubs,
            peer * per_peer + place // 2,
        ),
    )
    side = jnp.where(is_own, src // own_rows, jnp.where(is_hub, (hub % hubs) // half_hubs, place % 2))
    key = (side << HALF_BIT) + (row << DST_BITS) + dst
    key = jnp.where(live, key, DEAD)
    key, _ = lax.optimization_barrier((key, out_rows))
    key_other = lax.ppermute(key, "edge", SWAP)
    every = jnp.concatenate([key, key_other])
    mine = jnp.where((every >> HALF_BIT) == half, every & ((1 << HALF_BIT) - 1), PAD)
    keys = lax.sort(mine).reshape(-1, CHUNK)
    every = every.reshape(-1, CHUNK)
    counts = jnp.stack(
        [
            jnp.sum((keys < (own_rows << DST_BITS)).astype(jnp.int32)),
            jnp.sum((keys < PAD).astype(jnp.int32)),
        ]
    )
    low = keys[:, 0] >> DST_BITS
    high = jnp.max(jnp.where(keys < PAD, keys, 0), axis=1) >> DST_BITS

    own_sum, degree = own_forward(counts, every, keys, own_half, nodes)
    neigh = received_forward(
        counts, low, high, keys, table.reshape(num_dom * per_peer, width), own_sum, own_rows
    )
    neigh_other = lax.ppermute(neigh, "edge", SWAP)
    layer_out, grad_sum, grad_input, grad_w = dense(
        half_scalar,
        neigh,
        neigh_other,
        degree,
        node_feats,
        cotangent,
        w_self,
        w_neigh,
        bias.reshape(1, width),
    )
    row_grads = received_backward(
        counts, low, high, keys, grad_sum, own_rows, num_dom * per_peer
    )
    back = lax.all_to_all(
        row_grads.reshape(num_dom, per_peer, width), "dom", split_axis=0, concat_axis=0, tiled=True
    )
    own_grads = own_backward(counts, keys, grad_sum, own_rows)

    bits = num_dom.bit_length() - 1
    for b in range(bits):
        grad_w = tree_sum(grad_w, [1 << b], num_dom)
    grad_w_other = lax.ppermute(grad_w[:128], "edge", SWAP)
    grad_self = jnp.where(half == 0, grad_w[:128], grad_w_other)
    grad_neigh = jnp.where(half == 0, grad_w_other, grad_w[:128])
    grad_bias = grad_w[128]

    part, hub_part = returned_sum(half_scalar, idx, back, own_grads, nodes, slots)
    part_other = lax.ppermute(part, "edge", SWAP)
    hub_other = lax.ppermute(hub_part, "edge", SWAP)
    grad_feats = grad_input + (part + part_other)
    grad_hubs = jnp.where(
        half == 0,
        jnp.concatenate([hub_part, hub_other]),
        jnp.concatenate([hub_other, hub_part]),
    )
    return (layer_out, grad_feats, grad_hubs, grad_self, grad_neigh, grad_bias)


def solution(mesh):
    placed = (
        P("dom", None),
        P("dom", None),
        P(),
        P(),
        P(),
        P("dom", None),
        P("dom", None),
        P("dom", None, None),
        P("dom", "edge", None),
        P("dom", "edge", None),
        P("dom", "edge"),
    )
    return jax.shard_map(
        body,
        mesh=mesh,
        in_specs=placed,
        out_specs=(P("dom", None), P("dom", None), P("dom", None), P(), P(), P()),
        check_vma=False,
    )
```

```python
import functools

import jax
import jax.numpy as jnp
import numpy as np
from jax import lax
from jax.experimental import pallas as pl
from jax.experimental.pallas import tpu as pltpu
from jax.sharding import PartitionSpec as P

F32 = jnp.float32
BF16 = jnp.bfloat16
VMEM = pltpu.VMEM
SMEM = pltpu.SMEM
SWAP = [(0, 1), (1, 0)]
CHUNK = 256
DST_BITS = 10
PAD = 1 << 30
DEAD = 1 << 26
HALF_BIT = 24


def params(mib=40):
    return pltpu.CompilerParams(vmem_limit_bytes=mib * 1024 * 1024)


def vspec():
    return pl.BlockSpec(memory_space=VMEM)


def sspec():
    return pl.BlockSpec(memory_space=SMEM)


def columns_of(row):
    parts = []
    for at in range(0, row.shape[1], 128):
        parts.append(jnp.broadcast_to(row[:, at : at + 128], (128, 128)).T)
    return jnp.concatenate(parts, axis=0)


def onehot_of_columns(col, width):
    lane = lax.broadcasted_iota(jnp.int32, col.shape, 1)
    parts = [
        jnp.where(col == lane + at, 1.0, 0.0).astype(BF16) for at in range(0, width, 128)
    ]
    return jnp.concatenate(parts, axis=1)


def onehot_of_rows(row, height):
    sub = lax.broadcasted_iota(jnp.int32, (height, row.shape[1]), 0)
    return jnp.where(sub == row, 1.0, 0.0).astype(BF16)


def dot(a, b):
    return jnp.dot(a, b, preferred_element_type=F32)


def dot_nt(a, b):
    return lax.dot_general(a, b, (((1,), (1,)), ((), ())), preferred_element_type=F32)


def dot_tn(a, b):
    return lax.dot_general(a, b, (((0,), (0,)), ((), ())), preferred_element_type=F32)


def outgoing_kernel(slots, idx_ref, feat_ref, out_ref):
    step = pl.program_id(0)
    peers = out_ref.shape[0]
    rows = feat_ref.shape[0]
    for pair in range(peers // 4):
        at = step * (peers // 2) + pair * 2
        idx = [idx_ref[pl.ds(at + k, 1), :] for k in range(2)]
        hot = onehot_of_columns(columns_of(jnp.concatenate(idx, axis=1)), rows)
        picked = dot(hot, feat_ref[...]).astype(BF16)
        for k in range(4):
            out_ref[pair * 4 + k, :, :] = picked[k * slots : (k + 1) * slots]


def outgoing(idx, feats, slots, step_peers=8):
    peers = idx.shape[0] * idx.shape[1] // slots
    width = feats.shape[1]
    return pl.pallas_call(
        functools.partial(outgoing_kernel, slots),
        grid=(peers // step_peers,),
        in_specs=[
            pl.BlockSpec(idx.shape, lambda i: (0, 0)),
            pl.BlockSpec(feats.shape, lambda i: (0, 0)),
        ],
        out_specs=pl.BlockSpec((step_peers, slots, width), lambda i: (i, 0, 0)),
        out_shape=jax.ShapeDtypeStruct((peers, slots, width), BF16),
        compiler_params=params(),
        name="outgoing_rows",
    )(idx, feats)


def over_windows(c, low_ref, high_ref, rows, window, visit):
    low = low_ref[c] // 128 * 128

    def step(w, _):
        base = low + w * window
        visit(pl.multiple_of(jnp.minimum(base, rows - window), 128), base)
        return 0

    lax.fori_loop(0, (high_ref[c] - low) // window + 1, step, 0)


def gather_add(c, offset, window, low_ref, high_ref, keys_ref, table_ref, sum_ref, values_ref):
    nodes = sum_ref.shape[0]
    key = keys_ref[pl.ds(c, 1), :]
    row = (key >> DST_BITS) - offset
    values_ref[...] = jnp.zeros_like(values_ref)

    def visit(start, base):
        hot = onehot_of_columns(columns_of(jnp.where(row >= base, row - start, -1)), window)
        values_ref[...] += dot(hot, table_ref[pl.ds(start, window), :])

    over_windows(c, low_ref, high_ref, table_ref.shape[0], window, visit)
    sum_ref[...] += dot(onehot_of_rows(key & (nodes - 1), nodes), values_ref[...].astype(BF16))


def spread_add(c, offset, window, low_ref, high_ref, keys_ref, grad_ref, acc_ref):
    nodes = grad_ref.shape[0]
    key = keys_ref[pl.ds(c, 1), :]
    row = (key >> DST_BITS) - offset
    hot = onehot_of_columns(columns_of(key & (nodes - 1)), nodes)
    values = dot(hot, grad_ref[...]).astype(BF16)

    def visit(start, base):
        hot = onehot_of_rows(jnp.where(row >= base, row - start, -1), window)
        acc_ref[pl.ds(start, window), :] += dot(hot, values)

    over_windows(c, low_ref, high_ref, acc_ref.shape[0], window, visit)


def near_forward_kernel(
    window, count_ref, low_ref, high_ref, every_ref, keys_ref, table_ref, sum_ref, deg_ref, values_ref
):
    nodes = sum_ref.shape[0]
    deg_ref[...] = jnp.zeros_like(deg_ref)
    sum_ref[...] = jnp.zeros_like(sum_ref)

    def degrees(c, _):
        key = every_ref[pl.ds(c, 1), :]
        dst = key & (nodes - 1)
        high = jnp.where(key < DEAD, dst >> 7, deg_ref.shape[0])
        deg_ref[...] += dot_nt(
            onehot_of_rows(high, deg_ref.shape[0]), onehot_of_rows(dst & 127, 128)
        )
        return 0

    lax.fori_loop(0, every_ref.shape[0], degrees, 0)

    def chunk(c, _):
        gather_add(c, 0, window, low_ref, high_ref, keys_ref, table_ref, sum_ref, values_ref)
        return 0

    lax.fori_loop(0, pl.cdiv(count_ref[0], CHUNK), chunk, 0)


def near_forward(counts, low, high, every, keys, table, nodes, window=640):
    width = table.shape[1]
    return pl.pallas_call(
        functools.partial(near_forward_kernel, min(window, table.shape[0])),
        in_specs=[sspec(), sspec(), sspec(), vspec(), vspec(), vspec()],
        out_specs=[vspec(), vspec()],
        out_shape=[
            jax.ShapeDtypeStruct((nodes, width), F32),
            jax.ShapeDtypeStruct((16, 128), F32),
        ],
        scratch_shapes=[VMEM((CHUNK, width), F32)],
        compiler_params=params(),
        name="near_forward",
    )(counts, low, high, every, keys, table)


def far_forward_kernel(
    offset, window, count_ref, low_ref, high_ref, keys_ref, table_ref, base_ref, sum_ref, values_ref
):
    sum_ref[...] = base_ref[...]

    def chunk(c, _):
        gather_add(c, offset, window, low_ref, high_ref, keys_ref, table_ref, sum_ref, values_ref)
        return 0

    lax.fori_loop(count_ref[0] // CHUNK, pl.cdiv(count_ref[1], CHUNK), chunk, 0)


def far_forward(counts, low, high, keys, table, base, offset, window=1280):
    return pl.pallas_call(
        functools.partial(far_forward_kernel, offset, min(window, table.shape[0])),
        in_specs=[sspec(), sspec(), sspec(), vspec(), vspec(), vspec()],
        out_specs=vspec(),
        out_shape=jax.ShapeDtypeStruct(base.shape, F32),
        scratch_shapes=[VMEM((CHUNK, base.shape[1]), F32)],
        compiler_params=params(),
        name="far_forward",
    )(counts, low, high, keys, table, base)


def dense_kernel(
    half_ref,
    mine_ref,
    other_ref,
    deg_ref,
    feat_ref,
    cot_ref,
    w_self_ref,
    w_neigh_ref,
    bias_ref,
    out_ref,
    grad_sum_ref,
    grad_input_ref,
    grad_w_ref,
    left_ref,
    pre_ref,
):
    nodes = feat_ref.shape[0]
    grad_bias = jnp.zeros((8, 128), F32)
    for at in range(0, nodes, 128):
        span = pl.ds(at, 128)
        h = at // 128
        divisor = jnp.maximum(columns_of(deg_ref[h : h + 1, :]), 1.0)
        feats = feat_ref[span, :]
        aggregate = ((mine_ref[span, :] + other_ref[span, :]) / divisor).astype(BF16)
        preact = dot(feats, w_self_ref[...]) + dot(aggregate, w_neigh_ref[...]) + bias_ref[...]
        sig = jax.nn.sigmoid(preact)
        out_ref[span, :] = (preact * sig).astype(BF16)
        slope = sig * (1.0 + preact * (1.0 - sig))
        grad_pre = (cot_ref[span, :].astype(F32) * slope).astype(BF16)
        pre_ref[span, :] = grad_pre
        grad_sum_ref[span, :] = (dot_nt(grad_pre, w_neigh_ref[...]) / divisor).astype(BF16)
        grad_input_ref[span, :] = dot_nt(grad_pre, w_self_ref[...])
        left_ref[span, :] = jnp.where(half_ref[0] == 0, feats.astype(F32), aggregate.astype(F32)).astype(BF16)
        wide = grad_pre.astype(F32)
        for r in range(0, 128, 8):
            grad_bias = grad_bias + wide[r : r + 8]
    grad_w_ref[:128, :] = dot_tn(left_ref[...], pre_ref[...])
    grad_w_ref[128:, :] = jnp.broadcast_to(
        jnp.sum(grad_bias, axis=0, keepdims=True), (grad_w_ref.shape[0] - 128, 128)
    )


def dense(half, mine, other, deg, feats, cot, w_self, w_neigh, bias):
    nodes, width = feats.shape
    return pl.pallas_call(
        dense_kernel,
        in_specs=[sspec()] + [vspec()] * 8,
        out_specs=[vspec()] * 4,
        out_shape=[
            jax.ShapeDtypeStruct((nodes, width), BF16),
            jax.ShapeDtypeStruct((nodes, width), BF16),
            jax.ShapeDtypeStruct((nodes, width), F32),
            jax.ShapeDtypeStruct((192, width), F32),
        ],
        scratch_shapes=[VMEM((nodes, width), BF16), VMEM((nodes, width), BF16)],
        compiler_params=params(),
        name="dense_part",
    )(half, mine, other, deg, feats, cot, w_self, w_neigh, bias)


def far_backward_kernel(
    offset, window, count_ref, low_ref, high_ref, keys_ref, grad_ref, out_ref, acc_ref
):
    rows = acc_ref.shape[0]
    block = min(512, rows)

    def clear(b, _):
        span = pl.ds(pl.multiple_of(b * block, block), block)
        acc_ref[span, :] = jnp.zeros((block, acc_ref.shape[1]), F32)
        return 0

    lax.fori_loop(0, rows // block, clear, 0)

    def chunk(c, _):
        spread_add(c, offset, window, low_ref, high_ref, keys_ref, grad_ref, acc_ref)
        return 0

    lax.fori_loop(count_ref[0] // CHUNK, pl.cdiv(count_ref[1], CHUNK), chunk, 0)

    def finish(b, _):
        span = pl.ds(pl.multiple_of(b * block, block), block)
        out_ref[span, :] = acc_ref[span, :].astype(BF16)
        return 0

    lax.fori_loop(0, rows // block, finish, 0)


def far_backward(counts, low, high, keys, grad_sum, offset, rows, window=1280):
    width = grad_sum.shape[1]
    return pl.pallas_call(
        functools.partial(far_backward_kernel, offset, min(window, rows)),
        in_specs=[sspec(), sspec(), sspec(), vspec(), vspec()],
        out_specs=vspec(),
        out_shape=jax.ShapeDtypeStruct((rows, width), BF16),
        scratch_shapes=[VMEM((rows, width), F32)],
        compiler_params=params(),
        name="far_backward",
    )(counts, low, high, keys, grad_sum)


def near_backward_kernel(window, count_ref, low_ref, high_ref, keys_ref, grad_ref, out_ref):
    out_ref[...] = jnp.zeros_like(out_ref)

    def chunk(c, _):
        spread_add(c, 0, window, low_ref, high_ref, keys_ref, grad_ref, out_ref)
        return 0

    lax.fori_loop(0, pl.cdiv(count_ref[0], CHUNK), chunk, 0)


def near_backward(counts, low, high, keys, grad_sum, rows, window=640):
    return pl.pallas_call(
        functools.partial(near_backward_kernel, min(window, rows)),
        in_specs=[sspec(), sspec(), sspec(), vspec(), vspec()],
        out_specs=vspec(),
        out_shape=jax.ShapeDtypeStruct((rows, grad_sum.shape[1]), F32),
        compiler_params=params(),
        name="near_backward",
    )(counts, low, high, keys, grad_sum)


def returned_kernel(half_ref, idx_ref, back_ref, near_ref, part_ref):
    nodes = part_ref.shape[0]
    own_rows = nodes // 2
    peers, slots, width = back_ref.shape
    part_ref[...] = jnp.zeros_like(part_ref)
    own_span = pl.ds(pl.multiple_of(half_ref[0] * own_rows, own_rows), own_rows)
    part_ref[own_span, :] = near_ref[:own_rows, :]

    def step(s, _):
        idx = jnp.concatenate([idx_ref[pl.ds(s * 4 + k, 1), :] for k in range(4)], axis=1)
        rows = back_ref[pl.ds(s * 8, 8), :, :].reshape(8 * slots, width)
        part_ref[...] += dot(onehot_of_rows(idx, nodes), rows)
        return 0

    lax.fori_loop(0, peers // 8, step, 0)


def returned_sum(half, idx, back, near, nodes):
    return pl.pallas_call(
        returned_kernel,
        in_specs=[sspec(), vspec(), vspec(), vspec()],
        out_specs=vspec(),
        out_shape=jax.ShapeDtypeStruct((nodes, back.shape[2]), F32),
        compiler_params=params(),
        name="returned_sum",
    )(half, idx, back, near)


def torus_of(size):
    side = 4 if size >= 64 else 2
    return side, size // (side * side), side


def groups_of(size, axis):
    sizes = torus_of(size)
    ids = np.arange(size).reshape(sizes)
    return np.moveaxis(ids, axis, -1).reshape(-1, sizes[axis]).tolist()


X_AXIS, Z_AXIS, Y_AXIS = 0, 1, 2


def exchange(blocks, axis, size):
    return lax.all_to_all(
        blocks, "dom", 0, 0, axis_index_groups=groups_of(size, axis), tiled=True
    )


def partners(size, axis):
    step, count = ((torus_of(size)[2] * torus_of(size)[1], torus_of(size)[0]) if axis == X_AXIS
                   else (1, torus_of(size)[2]))
    return [[(i, i ^ (step * j)) for i in range(size)] for j in range(1, count)]


def swap_blocks(blocks, axis, size):
    return [blocks[0]] + [
        lax.ppermute(block, "dom", pairs) for block, pairs in zip(blocks[1:], partners(size, axis))
    ]


def pair_sum(parts):
    while len(parts) > 1:
        parts = [parts[i] + parts[i + 1] for i in range(0, len(parts), 2)]
    return parts[0]


def after(value, *earlier):
    return lax.optimization_barrier((value,) + earlier)[0]


def body(
    node_feats,
    hub_feats,
    w_self,
    w_neigh,
    bias,
    cotangent,
    send_count,
    send_rows,
    edge_src,
    edge_dst,
    edge_count,
):
    num_dom = lax.axis_size("dom")
    half = lax.axis_index("edge")
    nodes, width = node_feats.shape
    block_rows = send_rows.shape[2]
    hubs = hub_feats.shape[0]
    slots, half_hubs, own_rows = block_rows // 2, hubs // 2, nodes // 2
    half_scalar = half.astype(jnp.int32).reshape(1)
    xs, zs, ys = torus_of(num_dom)
    hub_rows = num_dom * half_hubs
    near_rows, far_rows = own_rows + hub_rows, num_dom * slots

    hub_half = lax.dynamic_slice_in_dim(hub_feats, half * half_hubs, half_hubs, 0)
    hub_z = exchange(jnp.broadcast_to(hub_half[None], (zs,) + hub_half.shape), Z_AXIS, num_dom)

    slot_ids = jnp.arange(block_rows, dtype=jnp.int32)[None, :]
    idx_all = jnp.where(slot_ids < send_count[0][:, None], send_rows[0], nodes + 1024)
    idx = jnp.where(half == 0, idx_all[:, 0::2], idx_all[:, 1::2])
    idx = idx.reshape(num_dom * slots // 128, 128)
    out_rows = outgoing(idx, node_feats, slots)
    out_rows, hub_z = lax.optimization_barrier((out_rows, hub_z))
    table = lax.all_to_all(out_rows, "dom", split_axis=0, concat_axis=0, tiled=True)
    hub_z = after(hub_z.reshape(zs * half_hubs, width), out_rows)
    hub_x = jnp.concatenate(swap_blocks([hub_z] * xs, X_AXIS, num_dom))
    hub_y = jnp.concatenate(swap_blocks([hub_x] * ys, Y_AXIS, num_dom))
    own_half = lax.dynamic_slice_in_dim(node_feats, half * own_rows, own_rows, 0)
    near_table = jnp.concatenate([own_half, hub_y.reshape(hub_rows, width)])

    src = edge_src.reshape(-1)
    dst = edge_dst.reshape(-1)
    edges = src.shape[0]
    live = jnp.arange(edges, dtype=jnp.int32) < edge_count.reshape(())
    slot = src - nodes
    hub = slot - num_dom * block_rows
    is_own, is_hub = src < nodes, hub >= 0
    master = hub // hubs
    me = lax.axis_index("dom")
    far_y, far_x = (master ^ me) & (ys - 1), (master ^ me) // (ys * zs)
    master_place = (far_y * xs + far_x) * zs + (master // ys) % zs
    row = jnp.where(
        is_own,
        src % own_rows,
        jnp.where(
            is_hub,
            own_rows + master_place * half_hubs + hub % half_hubs,
            near_rows + slot // 2,
        ),
    )
    side = jnp.where(is_own, src // own_rows, jnp.where(is_hub, (hub % hubs) // half_hubs, slot % 2))
    key = (side << HALF_BIT) + (row << DST_BITS) + dst
    key = after(jnp.where(live, key, DEAD), out_rows)
    key_other = lax.ppermute(key, "edge", SWAP)
    every = jnp.concatenate([key, key_other])
    mine = jnp.where((every >> HALF_BIT) == half, every & ((1 << HALF_BIT) - 1), PAD)
    keys = lax.sort(mine).reshape(-1, CHUNK)
    every = every.reshape(-1, CHUNK)
    near_edge = keys < (near_rows << DST_BITS)
    live_edge = keys < PAD
    counts = jnp.stack([jnp.sum(near_edge.astype(jnp.int32)), jnp.sum(live_edge.astype(jnp.int32))])
    near_low = jnp.minimum(keys[:, 0] >> DST_BITS, near_rows - 1)
    near_high = jnp.max(jnp.where(near_edge, keys, 0), axis=1) >> DST_BITS
    far_low = jnp.min(jnp.where(near_edge, PAD, keys), axis=1) >> DST_BITS
    far_low = jnp.minimum(far_low - near_rows, far_rows - 1)
    far_high = jnp.max(jnp.where(live_edge, keys, 0), axis=1) >> DST_BITS
    far_high = jnp.maximum(far_high - near_rows, 0)

    near_sum, degree = near_forward(counts, near_low, near_high, every, keys, near_table, nodes)
    neigh = far_forward(
        counts, far_low, far_high, keys, table.reshape(far_rows, width), near_sum, near_rows
    )
    neigh_other = lax.ppermute(neigh, "edge", SWAP)
    layer_out, grad_sum, grad_input, grad_w = dense(
        half_scalar,
        neigh,
        neigh_other,
        degree,
        node_feats,
        cotangent,
        w_self,
        w_neigh,
        bias.reshape(1, width),
    )
    share = grad_w.shape[0] // zs
    grad_w = exchange(grad_w.reshape(zs, share, width), Z_AXIS, num_dom)
    row_grads = far_backward(counts, far_low, far_high, keys, grad_sum, near_rows, far_rows)
    row_grads, grad_w = lax.optimization_barrier((row_grads, grad_w))
    back = lax.all_to_all(
        row_grads.reshape(num_dom, slots, width), "dom", split_axis=0, concat_axis=0, tiled=True
    )
    near_grads = near_backward(
        counts, near_low, near_high, after(keys, row_grads), grad_sum, near_rows
    )

    grad_w = jnp.sum(grad_w, axis=0)
    hub_part = near_grads[own_rows:]
    for axis, parts in ((Y_AXIS, ys), (X_AXIS, xs)):
        blocks = jnp.split(hub_part, parts)
        kept = blocks[0].shape[0]
        both = pair_sum(
            swap_blocks([jnp.concatenate([block, grad_w]) for block in blocks], axis, num_dom)
        )
        hub_part, grad_w = both[:kept], both[kept:]
    hub_part = hub_part.reshape(zs, half_hubs, width)
    both = jnp.concatenate([hub_part, jnp.broadcast_to(grad_w[None], (zs,) + grad_w.shape)], axis=1)
    both = exchange(after(both, back), Z_AXIS, num_dom)
    hub_part = jnp.sum(both[:, :half_hubs], axis=0)
    grad_w = both[:, half_hubs:].reshape(zs * share, width)

    part = returned_sum(half_scalar, idx, back, near_grads, nodes)
    part_other = lax.ppermute(part, "edge", SWAP)
    small = jnp.concatenate([grad_w[:width], hub_part])
    small_other = lax.ppermute(small, "edge", SWAP)
    first = jnp.where(half == 0, small, small_other)
    second = jnp.where(half == 0, small_other, small)
    grad_self, grad_neigh, grad_bias = first[:width], second[:width], grad_w[width]
    grad_hubs = jnp.concatenate([first[width:], second[width:]])
    grad_feats = grad_input + (part + part_other)
    return (layer_out, grad_feats, grad_hubs, grad_self, grad_neigh, grad_bias)


def solution(mesh):
    placed = (
        P("dom", None),
        P("dom", None),
        P(),
        P(),
        P(),
        P("dom", None),
        P("dom", None),
        P("dom", None, None),
        P("dom", "edge", None),
        P("dom", "edge", None),
        P("dom", "edge"),
    )
    return jax.shard_map(
        body,
        mesh=mesh,
        in_specs=placed,
        out_specs=(P("dom", None), P("dom", None), P("dom", None), P(), P(), P()),
        check_vma=False,
    )
```

```python
import functools

import jax
import jax.numpy as jnp
import numpy as np
from jax import lax
from jax.experimental import pallas as pl
from jax.experimental.pallas import tpu as pltpu
from jax.sharding import PartitionSpec as P

F32 = jnp.float32
BF16 = jnp.bfloat16
I16 = jnp.int16
VMEM = pltpu.VMEM
SMEM = pltpu.SMEM
SWAP = [(0, 1), (1, 0)]
CHUNK = 256
UNROLL = 4
DST_BITS = 10
PAD = 1 << 30
DEAD = 1 << 26
HALF_BIT = 24
META = NEAR_LOW, NEAR_HIGH, FAR_LOW, FAR_HIGH, COUNTS = 0, 1, 2, 3, 4


def params(mib=40):
    return pltpu.CompilerParams(vmem_limit_bytes=mib * 1024 * 1024)


def vspec():
    return pl.BlockSpec(memory_space=VMEM)


def sspec():
    return pl.BlockSpec(memory_space=SMEM)


def columns_of(row):
    parts = []
    for at in range(0, row.shape[1], 128):
        parts.append(jnp.broadcast_to(row[:, at : at + 128], (128, 128)).T)
    return jnp.concatenate(parts, axis=0)


def onehot_of_columns(col, width):
    lane = lax.broadcasted_iota(jnp.int32, col.shape, 1).astype(I16)
    col = col.astype(I16)
    one, zero = jnp.ones((), BF16), jnp.zeros((), BF16)
    parts = [jnp.where(col == lane + I16(at), one, zero) for at in range(0, width, 128)]
    return parts[0] if len(parts) == 1 else jnp.concatenate(parts, axis=1)


def onehot_of_rows(row, height):
    sub = lax.broadcasted_iota(jnp.int32, (height, row.shape[1]), 0).astype(I16)
    return jnp.where(sub == row.astype(I16), jnp.ones((), BF16), jnp.zeros((), BF16))


def dot(a, b):
    return jnp.dot(a, b, preferred_element_type=F32)


def dot_nt(a, b):
    return lax.dot_general(a, b, (((1,), (1,)), ((), ())), preferred_element_type=F32)


def dot_tn(a, b):
    return lax.dot_general(a, b, (((0,), (0,)), ((), ())), preferred_element_type=F32)


def pick(col, wide):
    rows = wide.shape[0]
    both = dot(onehot_of_columns(jnp.where(col >= rows, col - rows, col), rows), wide)
    return jnp.where(col >= rows, both[:, 128:], both[:, :128])


def spread(row, col, values, rows):
    left = col.astype(I16) < I16(rows)
    zero = jnp.zeros((), BF16)
    pair = jnp.concatenate([jnp.where(left, values, zero), jnp.where(left, zero, values)], axis=1)
    return dot(onehot_of_rows(jnp.where(row >= rows, row - rows, row), rows), pair)


def join(refs_at):
    return jnp.concatenate(refs_at, axis=1)


def outgoing_kernel(idx_ref, feat_ref, out_ref, wide_ref):
    step = pl.program_id(0)
    peers, slots, width = out_ref.shape
    nodes = feat_ref.shape[0]
    lines = peers * slots // 128

    @pl.when(step == 0)
    def _():
        wide_ref[:, :width] = feat_ref[: nodes // 2, :]
        wide_ref[:, width:] = feat_ref[nodes // 2 :, :]

    row = join([idx_ref[pl.ds(step * lines + k, 1), :] for k in range(lines)])
    out_ref[...] = pick(columns_of(row), wide_ref[...]).astype(BF16).reshape(peers, slots, width)


def outgoing(idx, feats, slots, step_peers=32):
    peers = idx.shape[0] * idx.shape[1] // slots
    nodes, width = feats.shape
    step_peers = min(step_peers, peers)
    return pl.pallas_call(
        outgoing_kernel,
        grid=(peers // step_peers,),
        in_specs=[
            pl.BlockSpec(idx.shape, lambda i: (0, 0)),
            pl.BlockSpec(feats.shape, lambda i: (0, 0)),
        ],
        out_specs=pl.BlockSpec((step_peers, slots, width), lambda i: (i, 0, 0)),
        out_shape=jax.ShapeDtypeStruct((peers, slots, width), BF16),
        scratch_shapes=[VMEM((nodes // 2, 2 * width), BF16)],
        compiler_params=params(),
        name="outgoing_rows",
    )(idx, feats)


def relative(row, base, start, window):
    return jnp.where((row >= base) & (row < start + window), row - start, -1)


def window_of(meta_ref, low_at, c, w, rows, window):
    base = meta_ref[low_at, c] // 128 * 128 + w * window
    return base, pl.multiple_of(jnp.minimum(base, rows - window), 128)


def windows_of(meta_ref, low_at, c, window):
    return (meta_ref[low_at + 1, c] - meta_ref[low_at, c] // 128 * 128) // window + 1


def keys_of(keys_ref, c, end):
    at = jnp.minimum(c, keys_ref.shape[0] - 1)
    return at, jnp.where(c < end, keys_ref[pl.ds(at, 1), :], PAD)


def gather_add(first, end, offset, window, low_at, meta_ref, keys_ref, table_ref, sum_ref, values_ref):
    half_nodes = sum_ref.shape[0]
    rows = table_ref.shape[0]
    half = window // 2

    def picked(c, w, col):
        base, start = window_of(meta_ref, low_at, c, w, rows, window)
        wide = join([table_ref[pl.ds(start, half), :], table_ref[pl.ds(start + half, half), :]])
        return pick(relative((col >> DST_BITS) - offset, base, start, window), wide)

    keys, cols = [], []
    for u in range(UNROLL):
        c, key = keys_of(keys_ref, first + u, end)
        keys.append(key)
        cols.append(columns_of(key))
        values_ref[u * CHUNK : (u + 1) * CHUNK, :] = picked(c, 0, cols[u])
    for u in range(UNROLL):
        c, key = keys_of(keys_ref, first + u, end)

        def more(w, _, c=c, key=key, u=u):
            values_ref[u * CHUNK : (u + 1) * CHUNK, :] += picked(c, w, columns_of(key))
            return 0

        lax.fori_loop(1, windows_of(meta_ref, low_at, c, window), more, 0)
    nodes = 2 * half_nodes
    sum_ref[...] += spread(
        join(keys) & (nodes - 1),
        jnp.concatenate(cols, axis=0) & (nodes - 1),
        values_ref[...].astype(BF16),
        half_nodes,
    )


def spread_add(first, end, offset, window, low_at, meta_ref, keys_ref, grad_ref, acc_ref, values_ref):
    nodes = 2 * grad_ref.shape[0]
    rows = acc_ref.shape[0]
    half = window // 2

    def add(c, w, key, col, values):
        base, start = window_of(meta_ref, low_at, c, w, rows, window)
        row, col = (
            relative((k >> DST_BITS) - offset, base, start, window) for k in (key, col)
        )
        both = spread(row, col, values, half)
        acc_ref[pl.ds(start, half), :] += both[:, :128]
        acc_ref[pl.ds(start + half, half), :] += both[:, 128:]

    keys = [keys_of(keys_ref, first + u, end) for u in range(UNROLL)]
    cols = [columns_of(key) for _, key in keys]
    values = pick(jnp.concatenate(cols, axis=0) & (nodes - 1), grad_ref[...]).astype(BF16)
    values_ref[...] = values
    for u, (c, key) in enumerate(keys):
        add(c, 0, key, cols[u], values[u * CHUNK : (u + 1) * CHUNK])
    for u in range(UNROLL):
        c, key = keys_of(keys_ref, first + u, end)

        def more(w, _, c=c, key=key, u=u):
            add(c, w, key, columns_of(key), values_ref[u * CHUNK : (u + 1) * CHUNK, :])
            return 0

        lax.fori_loop(1, windows_of(meta_ref, low_at, c, window), more, 0)


def over_chunks(first, end, visit):
    def step(i, _):
        visit(first + i * UNROLL)
        return 0

    lax.fori_loop(0, pl.cdiv(end - first, UNROLL), step, 0)


def near_forward_kernel(
    window, meta_ref, every_ref, keys_ref, table_ref, sum_ref, deg_ref, values_ref
):
    nodes = 2 * sum_ref.shape[0]
    deg_ref[...] = jnp.zeros_like(deg_ref)
    sum_ref[...] = jnp.zeros_like(sum_ref)

    def degrees(c, _):
        key = join([every_ref[pl.ds(c * UNROLL + u, 1), :] for u in range(UNROLL)])
        dst = key & (nodes - 1)
        high = jnp.where(key < DEAD, dst >> 7, deg_ref.shape[0])
        deg_ref[...] += dot_nt(
            onehot_of_rows(high, deg_ref.shape[0]), onehot_of_rows(dst & 127, 128)
        )
        return 0

    lax.fori_loop(0, every_ref.shape[0] // UNROLL, degrees, 0)
    end = pl.cdiv(meta_ref[COUNTS, 0], CHUNK)
    over_chunks(
        0,
        end,
        lambda c: gather_add(
            c, end, 0, window, NEAR_LOW, meta_ref, keys_ref, table_ref, sum_ref, values_ref
        ),
    )


def near_forward(meta, every, keys, table, nodes, window=768):
    width = table.shape[1]
    return pl.pallas_call(
        functools.partial(near_forward_kernel, min(window, table.shape[0])),
        in_specs=[sspec(), vspec(), vspec(), vspec()],
        out_specs=[vspec(), vspec()],
        out_shape=[
            jax.ShapeDtypeStruct((nodes // 2, 2 * width), F32),
            jax.ShapeDtypeStruct((16, 128), F32),
        ],
        scratch_shapes=[VMEM((UNROLL * CHUNK, width), F32)],
        compiler_params=params(),
        name="near_forward",
    )(meta, every, keys, table)


def far_forward_kernel(
    offset, window, meta_ref, keys_ref, table_ref, base_ref, sum_ref, values_ref
):
    sum_ref[...] = base_ref[...]
    end = pl.cdiv(meta_ref[COUNTS, 1], CHUNK)
    over_chunks(
        meta_ref[COUNTS, 0] // CHUNK,
        end,
        lambda c: gather_add(
            c, end, offset, window, FAR_LOW, meta_ref, keys_ref, table_ref, sum_ref, values_ref
        ),
    )


def far_forward(meta, keys, table, base, offset, window=1280):
    return pl.pallas_call(
        functools.partial(far_forward_kernel, offset, min(window, table.shape[0])),
        in_specs=[sspec(), vspec(), vspec(), vspec()],
        out_specs=vspec(),
        out_shape=jax.ShapeDtypeStruct(base.shape, F32),
        scratch_shapes=[VMEM((UNROLL * CHUNK, table.shape[1]), F32)],
        compiler_params=params(),
        name="far_forward",
    )(meta, keys, table, base)


def dense_kernel(
    half_ref,
    mine_ref,
    other_ref,
    deg_ref,
    feat_ref,
    cot_ref,
    w_self_ref,
    w_neigh_ref,
    bias_ref,
    out_ref,
    grad_sum_ref,
    grad_input_ref,
    grad_w_ref,
    left_ref,
    pre_ref,
):
    nodes = feat_ref.shape[0]
    grad_bias = jnp.zeros((8, 128), F32)
    for at in range(0, nodes, 128):
        span = pl.ds(at, 128)
        h = at // 128
        divisor = jnp.maximum(columns_of(deg_ref[h : h + 1, :]), 1.0)
        feats = feat_ref[span, :]
        place = (pl.ds(at % (nodes // 2), 128), pl.ds(at // (nodes // 2) * 128, 128))
        aggregate = ((mine_ref[place] + other_ref[place]) / divisor).astype(BF16)
        preact = dot(feats, w_self_ref[...]) + dot(aggregate, w_neigh_ref[...]) + bias_ref[...]
        sig = jax.nn.sigmoid(preact)
        out_ref[span, :] = (preact * sig).astype(BF16)
        slope = sig * (1.0 + preact * (1.0 - sig))
        grad_pre = (cot_ref[span, :].astype(F32) * slope).astype(BF16)
        pre_ref[span, :] = grad_pre
        grad_sum_ref[place] = (dot_nt(grad_pre, w_neigh_ref[...]) / divisor).astype(BF16)
        grad_input_ref[span, :] = dot_nt(grad_pre, w_self_ref[...])
        left_ref[span, :] = jnp.where(half_ref[0] == 0, feats.astype(F32), aggregate.astype(F32)).astype(BF16)
        wide = grad_pre.astype(F32)
        for r in range(0, 128, 8):
            grad_bias = grad_bias + wide[r : r + 8]
    grad_w_ref[:128, :] = dot_tn(left_ref[...], pre_ref[...])
    grad_w_ref[128:, :] = jnp.broadcast_to(
        jnp.sum(grad_bias, axis=0, keepdims=True), (grad_w_ref.shape[0] - 128, 128)
    )


def dense(half, mine, other, deg, feats, cot, w_self, w_neigh, bias):
    nodes, width = feats.shape
    return pl.pallas_call(
        dense_kernel,
        in_specs=[sspec()] + [vspec()] * 8,
        out_specs=[vspec()] * 4,
        out_shape=[
            jax.ShapeDtypeStruct((nodes, width), BF16),
            jax.ShapeDtypeStruct((nodes // 2, 2 * width), BF16),
            jax.ShapeDtypeStruct((nodes, width), F32),
            jax.ShapeDtypeStruct((192, width), F32),
        ],
        scratch_shapes=[VMEM((nodes, width), BF16), VMEM((nodes, width), BF16)],
        compiler_params=params(),
        name="dense_part",
    )(half, mine, other, deg, feats, cot, w_self, w_neigh, bias)


def far_backward_kernel(offset, window, meta_ref, keys_ref, grad_ref, out_ref, acc_ref, values_ref):
    rows = acc_ref.shape[0]
    block = min(512, rows)

    def clear(b, _):
        span = pl.ds(pl.multiple_of(b * block, block), block)
        acc_ref[span, :] = jnp.zeros((block, acc_ref.shape[1]), F32)
        return 0

    lax.fori_loop(0, rows // block, clear, 0)
    end = pl.cdiv(meta_ref[COUNTS, 1], CHUNK)
    over_chunks(
        meta_ref[COUNTS, 0] // CHUNK,
        end,
        lambda c: spread_add(
            c, end, offset, window, FAR_LOW, meta_ref, keys_ref, grad_ref, acc_ref, values_ref
        ),
    )

    def finish(b, _):
        span = pl.ds(pl.multiple_of(b * block, block), block)
        out_ref[span, :] = acc_ref[span, :].astype(BF16)
        return 0

    lax.fori_loop(0, rows // block, finish, 0)


def far_backward(meta, keys, grad_sum, offset, rows, window=1280):
    width = grad_sum.shape[1] // 2
    return pl.pallas_call(
        functools.partial(far_backward_kernel, offset, min(window, rows)),
        in_specs=[sspec(), vspec(), vspec()],
        out_specs=vspec(),
        out_shape=jax.ShapeDtypeStruct((rows, width), BF16),
        scratch_shapes=[VMEM((rows, width), F32), VMEM((UNROLL * CHUNK, width), BF16)],
        compiler_params=params(),
        name="far_backward",
    )(meta, keys, grad_sum)


def near_backward_kernel(window, meta_ref, keys_ref, grad_ref, out_ref, values_ref):
    out_ref[...] = jnp.zeros_like(out_ref)
    end = pl.cdiv(meta_ref[COUNTS, 0], CHUNK)
    over_chunks(
        0,
        end,
        lambda c: spread_add(
            c, end, 0, window, NEAR_LOW, meta_ref, keys_ref, grad_ref, out_ref, values_ref
        ),
    )


def near_backward(meta, keys, grad_sum, rows, window=768):
    width = grad_sum.shape[1] // 2
    return pl.pallas_call(
        functools.partial(near_backward_kernel, min(window, rows)),
        in_specs=[sspec(), vspec(), vspec()],
        out_specs=vspec(),
        out_shape=jax.ShapeDtypeStruct((rows, width), F32),
        scratch_shapes=[VMEM((UNROLL * CHUNK, width), BF16)],
        compiler_params=params(),
        name="near_backward",
    )(meta, keys, grad_sum)


def returned_kernel(peers_step, half_ref, idx_ref, back_ref, near_ref, part_ref, acc_ref):
    nodes = part_ref.shape[0]
    own_rows = nodes // 2
    peers, slots, width = back_ref.shape
    lines = peers_step * slots // 128
    acc_ref[...] = jnp.zeros_like(acc_ref)

    def step(s, _):
        row = join([idx_ref[pl.ds(s * lines + k, 1), :] for k in range(lines)])
        rows = back_ref[pl.ds(s * peers_step, peers_step), :, :].reshape(peers_step * slots, width)
        acc_ref[...] += spread(row, columns_of(row), rows, own_rows)
        return 0

    lax.fori_loop(0, peers // peers_step, step, 0)
    part_ref[:own_rows, :] = acc_ref[:, :width]
    part_ref[own_rows:, :] = acc_ref[:, width:]
    own_span = pl.ds(pl.multiple_of(half_ref[0] * own_rows, own_rows), own_rows)
    part_ref[own_span, :] += near_ref[:own_rows, :]


def returned_sum(half, idx, back, near, nodes):
    width = back.shape[2]
    return pl.pallas_call(
        functools.partial(returned_kernel, min(32, back.shape[0])),
        in_specs=[sspec(), vspec(), vspec(), vspec()],
        out_specs=vspec(),
        out_shape=jax.ShapeDtypeStruct((nodes, width), F32),
        scratch_shapes=[VMEM((nodes // 2, 2 * width), F32)],
        compiler_params=params(),
        name="returned_sum",
    )(half, idx, back, near)


def torus_of(size):
    side = 4 if size >= 64 else 2
    return side, size // (side * side), side


def groups_of(size, axis):
    sizes = torus_of(size)
    ids = np.arange(size).reshape(sizes)
    return np.moveaxis(ids, axis, -1).reshape(-1, sizes[axis]).tolist()


X_AXIS, Z_AXIS, Y_AXIS = 0, 1, 2


def exchange(blocks, axis, size):
    return lax.all_to_all(
        blocks, "dom", 0, 0, axis_index_groups=groups_of(size, axis), tiled=True
    )


def partners(size, axis):
    step, count = ((torus_of(size)[2] * torus_of(size)[1], torus_of(size)[0]) if axis == X_AXIS
                   else (1, torus_of(size)[2]))
    return [[(i, i ^ (step * j)) for i in range(size)] for j in range(1, count)]


def swap_blocks(blocks, axis, size):
    return [blocks[0]] + [
        lax.ppermute(block, "dom", pairs) for block, pairs in zip(blocks[1:], partners(size, axis))
    ]


def pair_sum(parts):
    while len(parts) > 1:
        parts = [parts[i] + parts[i + 1] for i in range(0, len(parts), 2)]
    return parts[0]


def after(value, *earlier):
    return lax.optimization_barrier((value,) + earlier)[0]


def body(
    node_feats,
    hub_feats,
    w_self,
    w_neigh,
    bias,
    cotangent,
    send_count,
    send_rows,
    edge_src,
    edge_dst,
    edge_count,
):
    num_dom = lax.axis_size("dom")
    half = lax.axis_index("edge")
    nodes, width = node_feats.shape
    block_rows = send_rows.shape[2]
    hubs = hub_feats.shape[0]
    slots, half_hubs, own_rows = block_rows // 2, hubs // 2, nodes // 2
    half_scalar = half.astype(jnp.int32).reshape(1)
    xs, zs, ys = torus_of(num_dom)
    hub_rows = num_dom * half_hubs
    near_rows, far_rows = own_rows + hub_rows, num_dom * slots

    hub_half = lax.dynamic_slice_in_dim(hub_feats, half * half_hubs, half_hubs, 0)
    hub_z = exchange(jnp.broadcast_to(hub_half[None], (zs,) + hub_half.shape), Z_AXIS, num_dom)

    slot_ids = jnp.arange(block_rows, dtype=jnp.int32)[None, :]
    idx_all = jnp.where(slot_ids < send_count[0][:, None], send_rows[0], -1)
    idx = jnp.where(half == 0, idx_all[:, 0::2], idx_all[:, 1::2])
    idx = idx.reshape(num_dom * slots // 128, 128)
    out_rows = outgoing(idx, node_feats, slots)
    out_rows, hub_z = lax.optimization_barrier((out_rows, hub_z))
    table = lax.all_to_all(out_rows, "dom", split_axis=0, concat_axis=0, tiled=True)
    hub_z = after(hub_z.reshape(zs * half_hubs, width), out_rows)
    hub_x = jnp.concatenate(swap_blocks([hub_z] * xs, X_AXIS, num_dom))
    hub_y = jnp.concatenate(swap_blocks([hub_x] * ys, Y_AXIS, num_dom))
    own_half = lax.dynamic_slice_in_dim(node_feats, half * own_rows, own_rows, 0)
    near_table = jnp.concatenate([own_half, hub_y.reshape(hub_rows, width)])

    src = edge_src.reshape(-1)
    dst = edge_dst.reshape(-1)
    edges = src.shape[0]
    live = jnp.arange(edges, dtype=jnp.int32) < edge_count.reshape(())
    slot = src - nodes
    hub = slot - num_dom * block_rows
    is_own, is_hub = src < nodes, hub >= 0
    master = hub // hubs
    me = lax.axis_index("dom")
    far_y, far_x = (master ^ me) & (ys - 1), (master ^ me) // (ys * zs)
    master_place = (far_y * xs + far_x) * zs + (master // ys) % zs
    row = jnp.where(
        is_own,
        src % own_rows,
        jnp.where(
            is_hub,
            own_rows + master_place * half_hubs + hub % half_hubs,
            near_rows + slot // 2,
        ),
    )
    side = jnp.where(is_own, src // own_rows, jnp.where(is_hub, (hub % hubs) // half_hubs, slot % 2))
    key = (side << HALF_BIT) + (row << DST_BITS) + dst
    key = after(jnp.where(live, key, DEAD), out_rows)
    key_other = lax.ppermute(key, "edge", SWAP)
    every = jnp.concatenate([key, key_other])
    mine = jnp.where((every >> HALF_BIT) == half, every & ((1 << HALF_BIT) - 1), PAD)
    keys = lax.sort(mine).reshape(-1, CHUNK)
    every = every.reshape(-1, CHUNK)
    near_edge = keys < (near_rows << DST_BITS)
    live_edge = keys < PAD
    counts = [jnp.sum(edge.astype(jnp.int32)) for edge in (near_edge, live_edge)]
    near_low = jnp.minimum(keys[:, 0] >> DST_BITS, near_rows - 1)
    near_high = jnp.max(jnp.where(near_edge, keys, 0), axis=1) >> DST_BITS
    far_low = jnp.min(jnp.where(near_edge, PAD, keys), axis=1) >> DST_BITS
    far_low = jnp.minimum(far_low - near_rows, far_rows - 1)
    far_high = jnp.max(jnp.where(live_edge, keys, 0), axis=1) >> DST_BITS
    far_high = jnp.maximum(far_high - near_rows, 0)

    lines = keys.shape[0]
    counts = jnp.where(jnp.arange(lines) == 0, counts[0], counts[1])
    meta = jnp.stack([near_low, near_high, far_low, far_high, counts])

    near_sum, degree = near_forward(meta, every, keys, near_table, nodes)
    neigh = far_forward(meta, keys, table.reshape(far_rows, width), near_sum, near_rows)
    neigh_other = lax.ppermute(neigh, "edge", SWAP)
    layer_out, grad_sum, grad_input, grad_w = dense(
        half_scalar,
        neigh,
        neigh_other,
        degree,
        node_feats,
        cotangent,
        w_self,
        w_neigh,
        bias.reshape(1, width),
    )
    share = grad_w.shape[0] // zs
    grad_w = exchange(grad_w.reshape(zs, share, width), Z_AXIS, num_dom)
    row_grads = far_backward(meta, keys, grad_sum, near_rows, far_rows)
    row_grads, grad_w = lax.optimization_barrier((row_grads, grad_w))
    back = lax.all_to_all(
        row_grads.reshape(num_dom, slots, width), "dom", split_axis=0, concat_axis=0, tiled=True
    )
    near_grads = near_backward(meta, after(keys, row_grads), grad_sum, near_rows)

    grad_w = jnp.sum(grad_w, axis=0)
    hub_part = near_grads[own_rows:]
    for axis, parts in ((Y_AXIS, ys), (X_AXIS, xs)):
        blocks = jnp.split(hub_part, parts)
        kept = blocks[0].shape[0]
        both = pair_sum(
            swap_blocks([jnp.concatenate([block, grad_w]) for block in blocks], axis, num_dom)
        )
        hub_part, grad_w = both[:kept], both[kept:]
    hub_part = hub_part.reshape(zs, half_hubs, width)
    both = jnp.concatenate([hub_part, jnp.broadcast_to(grad_w[None], (zs,) + grad_w.shape)], axis=1)
    both = exchange(after(both, back), Z_AXIS, num_dom)
    hub_part = jnp.sum(both[:, :half_hubs], axis=0)
    grad_w = both[:, half_hubs:].reshape(zs * share, width)

    part = returned_sum(half_scalar, idx, back, near_grads, nodes)
    part_other = lax.ppermute(part, "edge", SWAP)
    small = jnp.concatenate([grad_w[:width], hub_part])
    small_other = lax.ppermute(small, "edge", SWAP)
    first = jnp.where(half == 0, small, small_other)
    second = jnp.where(half == 0, small_other, small)
    grad_self, grad_neigh, grad_bias = first[:width], second[:width], grad_w[width]
    grad_hubs = jnp.concatenate([first[width:], second[width:]])
    grad_feats = grad_input + (part + part_other)
    return (layer_out, grad_feats, grad_hubs, grad_self, grad_neigh, grad_bias)


def solution(mesh):
    placed = (
        P("dom", None),
        P("dom", None),
        P(),
        P(),
        P(),
        P("dom", None),
        P("dom", None),
        P("dom", None, None),
        P("dom", "edge", None),
        P("dom", "edge", None),
        P("dom", "edge"),
    )
    return jax.shard_map(
        body,
        mesh=mesh,
        in_specs=placed,
        out_specs=(P("dom", None), P("dom", None), P("dom", None), P(), P(), P()),
        check_vma=False,
    )
```

```python
import functools

import jax
import jax.numpy as jnp
import numpy as np
from jax import lax
from jax.experimental import pallas as pl
from jax.experimental.pallas import tpu as pltpu
from jax.sharding import PartitionSpec as P

F32 = jnp.float32
BF16 = jnp.bfloat16
I16 = jnp.int16
VMEM = pltpu.VMEM
SMEM = pltpu.SMEM
SWAP = [(0, 1), (1, 0)]
CHUNK = 256
UNROLL = 4
DST_BITS = 10
PAD = 1 << 30
DEAD = 1 << 26
HALF_BIT = 24
META = NEAR_LOW, NEAR_HIGH, FAR_LOW, FAR_HIGH, COUNTS = 0, 1, 2, 3, 4


def params(mib=40):
    return pltpu.CompilerParams(vmem_limit_bytes=mib * 1024 * 1024)


def vspec():
    return pl.BlockSpec(memory_space=VMEM)


def sspec():
    return pl.BlockSpec(memory_space=SMEM)


def columns_of(row):
    parts = []
    for at in range(0, row.shape[1], 128):
        parts.append(jnp.broadcast_to(row[:, at : at + 128], (128, 128)).T)
    return jnp.concatenate(parts, axis=0)


def onehot_of_columns(col, width):
    lane = lax.broadcasted_iota(jnp.int32, col.shape, 1).astype(I16)
    col = col.astype(I16)
    one, zero = jnp.ones((), BF16), jnp.zeros((), BF16)
    parts = [jnp.where(col == lane + I16(at), one, zero) for at in range(0, width, 128)]
    return parts[0] if len(parts) == 1 else jnp.concatenate(parts, axis=1)


def onehot_of_rows(row, height):
    sub = lax.broadcasted_iota(jnp.int32, (height, row.shape[1]), 0).astype(I16)
    return jnp.where(sub == row.astype(I16), jnp.ones((), BF16), jnp.zeros((), BF16))


def dot(a, b):
    return jnp.dot(a, b, preferred_element_type=F32)


def dot_nt(a, b):
    return lax.dot_general(a, b, (((1,), (1,)), ((), ())), preferred_element_type=F32)


def dot_tn(a, b):
    return lax.dot_general(a, b, (((0,), (0,)), ((), ())), preferred_element_type=F32)


def pick(col, wide):
    rows = wide.shape[0]
    both = dot(onehot_of_columns(jnp.where(col >= rows, col - rows, col), rows), wide)
    return jnp.where(col >= rows, both[:, 128:], both[:, :128])


def spread(row, col, values, rows):
    left = col.astype(I16) < I16(rows)
    zero = jnp.zeros((), BF16)
    pair = jnp.concatenate([jnp.where(left, values, zero), jnp.where(left, zero, values)], axis=1)
    return dot(onehot_of_rows(jnp.where(row >= rows, row - rows, row), rows), pair)


def join(refs_at):
    return jnp.concatenate(refs_at, axis=1)


def outgoing_kernel(flip_ref, count_ref, rows_ref, feat_ref, out_ref, idx_ref, wide_ref, all_ref):
    step = pl.program_id(0)
    peers, slots, width = out_ref.shape
    nodes = feat_ref.shape[0]
    lines = peers * slots // 128

    @pl.when(step == 0)
    def _():
        wide_ref[:, :width] = feat_ref[: nodes // 2, :]
        wide_ref[:, width:] = feat_ref[nodes // 2 :, :]
        count = columns_of(count_ref[...])[: rows_ref.shape[0], :]
        lane = lax.broadcasted_iota(jnp.int32, rows_ref.shape, 1)
        all_ref[...] = jnp.where(lane < count, rows_ref[...], -1)
        pairs = rows_ref.shape[0] // 2
        even = all_ref[pl.ds(0, pairs, stride=2), :]
        odd = all_ref[pl.ds(1, pairs, stride=2), :]
        low = lax.broadcasted_iota(jnp.int32, even.shape, 1) < slots
        crossed = pltpu.roll(jnp.where(low, odd, even), slots, 1)
        idx_ref[...] = jnp.where(flip_ref[0] == 0, jnp.where(low, even, odd), crossed)

    row = join([idx_ref[pl.ds(step * lines + k, 1), :] for k in range(lines)])
    out_ref[...] = pick(columns_of(row), wide_ref[...]).astype(BF16).reshape(peers, slots, width)


def outgoing(flip, count, rows, feats, step_peers=32):
    peers, slots = rows.shape[0], rows.shape[1] // 2
    nodes, width = feats.shape
    step_peers = min(step_peers, peers)
    lines = peers * slots // 128
    return pl.pallas_call(
        outgoing_kernel,
        grid=(peers // step_peers,),
        in_specs=[
            sspec(),
            pl.BlockSpec(count.shape, lambda i: (0, 0)),
            pl.BlockSpec(rows.shape, lambda i: (0, 0)),
            pl.BlockSpec(feats.shape, lambda i: (0, 0)),
        ],
        out_specs=[
            pl.BlockSpec((step_peers, slots, width), lambda i: (i, 0, 0)),
            pl.BlockSpec((lines, 128), lambda i: (0, 0)),
        ],
        out_shape=[
            pltpu.HBM((peers, slots, width), BF16),
            jax.ShapeDtypeStruct((lines, 128), jnp.int32),
        ],
        scratch_shapes=[VMEM((nodes // 2, 2 * width), BF16), VMEM(rows.shape, jnp.int32)],
        compiler_params=params(),
        name="outgoing_rows",
    )(flip, count, rows, feats)


def relative(row, base, start, window):
    return jnp.where((row >= base) & (row < start + window), row - start, -1)


def window_of(meta_ref, low_at, c, w, rows, window):
    base = meta_ref[low_at, c] // 128 * 128 + w * window
    return base, pl.multiple_of(jnp.minimum(base, rows - window), 128)


def windows_of(meta_ref, low_at, c, window):
    return (meta_ref[low_at + 1, c] - meta_ref[low_at, c] // 128 * 128) // window + 1


def keys_of(keys_ref, c, end):
    at = jnp.minimum(c, keys_ref.shape[0] - 1)
    return at, jnp.where(c < end, keys_ref[pl.ds(at, 1), :], PAD)


def gather_add(first, end, offset, window, low_at, meta_ref, keys_ref, table_ref, sum_ref, values_ref):
    half_nodes = sum_ref.shape[0]
    rows = table_ref.shape[0]
    half = window // 2

    def picked(c, w, col):
        base, start = window_of(meta_ref, low_at, c, w, rows, window)
        wide = join([table_ref[pl.ds(start, half), :], table_ref[pl.ds(start + half, half), :]])
        return pick(relative((col >> DST_BITS) - offset, base, start, window), wide)

    keys, cols = [], []
    for u in range(UNROLL):
        c, key = keys_of(keys_ref, first + u, end)
        keys.append(key)
        cols.append(columns_of(key))
        values_ref[u * CHUNK : (u + 1) * CHUNK, :] = picked(c, 0, cols[u])
    for u in range(UNROLL):
        c, key = keys_of(keys_ref, first + u, end)

        def more(w, _, c=c, key=key, u=u):
            values_ref[u * CHUNK : (u + 1) * CHUNK, :] += picked(c, w, columns_of(key))
            return 0

        lax.fori_loop(1, windows_of(meta_ref, low_at, c, window), more, 0)
    nodes = 2 * half_nodes
    sum_ref[...] += spread(
        join(keys) & (nodes - 1),
        jnp.concatenate(cols, axis=0) & (nodes - 1),
        values_ref[...].astype(BF16),
        half_nodes,
    )


def spread_add(first, end, offset, window, low_at, meta_ref, keys_ref, grad_ref, acc_ref, values_ref):
    nodes = 2 * grad_ref.shape[0]
    rows = acc_ref.shape[0]
    half = window // 2

    def add(c, w, key, col, values):
        base, start = window_of(meta_ref, low_at, c, w, rows, window)
        row, col = (
            relative((k >> DST_BITS) - offset, base, start, window) for k in (key, col)
        )
        both = spread(row, col, values, half)
        acc_ref[pl.ds(start, half), :] += both[:, :128]
        acc_ref[pl.ds(start + half, half), :] += both[:, 128:]

    keys = [keys_of(keys_ref, first + u, end) for u in range(UNROLL)]
    cols = [columns_of(key) for _, key in keys]
    values = pick(jnp.concatenate(cols, axis=0) & (nodes - 1), grad_ref[...]).astype(BF16)
    values_ref[...] = values
    for u, (c, key) in enumerate(keys):
        add(c, 0, key, cols[u], values[u * CHUNK : (u + 1) * CHUNK])
    for u in range(UNROLL):
        c, key = keys_of(keys_ref, first + u, end)

        def more(w, _, c=c, key=key, u=u):
            add(c, w, key, columns_of(key), values_ref[u * CHUNK : (u + 1) * CHUNK, :])
            return 0

        lax.fori_loop(1, windows_of(meta_ref, low_at, c, window), more, 0)


def over_chunks(first, end, visit):
    def step(i, _):
        visit(first + i * UNROLL)
        return 0

    lax.fori_loop(0, pl.cdiv(end - first, UNROLL), step, 0)


def near_forward_kernel(
    window, meta_ref, every_ref, keys_ref, table_ref, sum_ref, deg_ref, values_ref
):
    nodes = 2 * sum_ref.shape[0]
    deg_ref[...] = jnp.zeros_like(deg_ref)
    sum_ref[...] = jnp.zeros_like(sum_ref)

    def degrees(c, _):
        key = join([every_ref[pl.ds(c * UNROLL + u, 1), :] for u in range(UNROLL)])
        dst = key & (nodes - 1)
        high = jnp.where(key < DEAD, dst >> 7, deg_ref.shape[0])
        deg_ref[...] += dot_nt(
            onehot_of_rows(high, deg_ref.shape[0]), onehot_of_rows(dst & 127, 128)
        )
        return 0

    lax.fori_loop(0, every_ref.shape[0] // UNROLL, degrees, 0)
    end = pl.cdiv(meta_ref[COUNTS, 0], CHUNK)
    over_chunks(
        0,
        end,
        lambda c: gather_add(
            c, end, 0, window, NEAR_LOW, meta_ref, keys_ref, table_ref, sum_ref, values_ref
        ),
    )


def near_forward(meta, every, keys, table, nodes, window=768):
    width = table.shape[1]
    return pl.pallas_call(
        functools.partial(near_forward_kernel, min(window, table.shape[0])),
        in_specs=[sspec(), vspec(), vspec(), vspec()],
        out_specs=[vspec(), vspec()],
        out_shape=[
            jax.ShapeDtypeStruct((nodes // 2, 2 * width), F32),
            jax.ShapeDtypeStruct((16, 128), F32),
        ],
        scratch_shapes=[VMEM((UNROLL * CHUNK, width), F32)],
        compiler_params=params(),
        name="near_forward",
    )(meta, every, keys, table)


def far_forward_kernel(
    offset, window, meta_ref, keys_ref, table_ref, base_ref, sum_ref, values_ref
):
    sum_ref[...] = base_ref[...]
    end = pl.cdiv(meta_ref[COUNTS, 1], CHUNK)
    over_chunks(
        meta_ref[COUNTS, 0] // CHUNK,
        end,
        lambda c: gather_add(
            c, end, offset, window, FAR_LOW, meta_ref, keys_ref, table_ref, sum_ref, values_ref
        ),
    )


def far_forward(meta, keys, table, base, offset, window=1280):
    return pl.pallas_call(
        functools.partial(far_forward_kernel, offset, min(window, table.shape[0])),
        in_specs=[sspec(), vspec(), vspec(), vspec()],
        out_specs=vspec(),
        out_shape=jax.ShapeDtypeStruct(base.shape, F32),
        scratch_shapes=[VMEM((UNROLL * CHUNK, table.shape[1]), F32)],
        compiler_params=params(),
        name="far_forward",
    )(meta, keys, table, base)


def dense_kernel(
    half_ref,
    mine_ref,
    other_ref,
    deg_ref,
    feat_ref,
    cot_ref,
    w_self_ref,
    w_neigh_ref,
    bias_ref,
    out_ref,
    grad_sum_ref,
    pre_ref,
    grad_w_ref,
    left_ref,
):
    nodes = feat_ref.shape[0]
    grad_bias = jnp.zeros((8, 128), F32)
    for at in range(0, nodes, 128):
        span = pl.ds(at, 128)
        h = at // 128
        divisor = jnp.maximum(columns_of(deg_ref[h : h + 1, :]), 1.0)
        feats = feat_ref[span, :]
        place = (pl.ds(at % (nodes // 2), 128), pl.ds(at // (nodes // 2) * 128, 128))
        aggregate = ((mine_ref[place] + other_ref[place]) / divisor).astype(BF16)
        preact = dot(feats, w_self_ref[...]) + dot(aggregate, w_neigh_ref[...]) + bias_ref[...]
        sig = jax.nn.sigmoid(preact)
        out_ref[span, :] = (preact * sig).astype(BF16)
        slope = sig * (1.0 + preact * (1.0 - sig))
        grad_pre = (cot_ref[span, :].astype(F32) * slope).astype(BF16)
        pre_ref[span, :] = grad_pre
        grad_sum_ref[place] = (dot_nt(grad_pre, w_neigh_ref[...]) / divisor).astype(BF16)
        left_ref[span, :] = jnp.where(half_ref[0] == 0, feats.astype(F32), aggregate.astype(F32)).astype(BF16)
        wide = grad_pre.astype(F32)
        for r in range(0, 128, 8):
            grad_bias = grad_bias + wide[r : r + 8]
    grad_w_ref[:128, :] = dot_tn(left_ref[...], pre_ref[...])
    grad_w_ref[128:, :] = jnp.broadcast_to(
        jnp.sum(grad_bias, axis=0, keepdims=True), (grad_w_ref.shape[0] - 128, 128)
    )


def dense(half, mine, other, deg, feats, cot, w_self, w_neigh, bias):
    nodes, width = feats.shape
    return pl.pallas_call(
        dense_kernel,
        in_specs=[sspec()] + [vspec()] * 8,
        out_specs=[vspec()] * 4,
        out_shape=[
            jax.ShapeDtypeStruct((nodes, width), BF16),
            jax.ShapeDtypeStruct((nodes // 2, 2 * width), BF16),
            jax.ShapeDtypeStruct((nodes, width), BF16),
            jax.ShapeDtypeStruct((192, width), F32),
        ],
        scratch_shapes=[VMEM((nodes, width), BF16)],
        compiler_params=params(),
        name="dense_part",
    )(half, mine, other, deg, feats, cot, w_self, w_neigh, bias)


def far_backward_kernel(offset, window, meta_ref, keys_ref, grad_ref, out_ref, acc_ref, values_ref):
    rows = acc_ref.shape[0]
    block = out_ref.shape[0]

    @pl.when(pl.program_id(0) == 0)
    def _():
        def clear(b, _):
            span = pl.ds(pl.multiple_of(b * block, block), block)
            acc_ref[span, :] = jnp.zeros((block, acc_ref.shape[1]), F32)
            return 0

        lax.fori_loop(0, rows // block, clear, 0)
        end = pl.cdiv(meta_ref[COUNTS, 1], CHUNK)
        over_chunks(
            meta_ref[COUNTS, 0] // CHUNK,
            end,
            lambda c: spread_add(
                c, end, offset, window, FAR_LOW, meta_ref, keys_ref, grad_ref, acc_ref, values_ref
            ),
        )

    at = pl.multiple_of(pl.program_id(0) * block, block)
    out_ref[...] = acc_ref[pl.ds(at, block), :].astype(BF16)


def far_backward(meta, keys, grad_sum, offset, rows, window=1280):
    width = grad_sum.shape[1] // 2
    block = min(1024, rows)
    return pl.pallas_call(
        functools.partial(far_backward_kernel, offset, min(window, rows)),
        grid=(rows // block,),
        in_specs=[
            sspec(),
            pl.BlockSpec(keys.shape, lambda i: (0, 0)),
            pl.BlockSpec(grad_sum.shape, lambda i: (0, 0)),
        ],
        out_specs=pl.BlockSpec((block, width), lambda i: (i, 0)),
        out_shape=pltpu.HBM((rows, width), BF16),
        scratch_shapes=[VMEM((rows, width), F32), VMEM((UNROLL * CHUNK, width), BF16)],
        compiler_params=params(),
        name="far_backward",
    )(meta, keys, grad_sum)


def near_backward_kernel(
    window, half_ref, meta_ref, keys_ref, grad_ref, pre_ref, w_self_ref, out_ref, values_ref
):
    own_rows = pre_ref.shape[0] // 2
    mine = pl.ds(pl.multiple_of(half_ref[0] * own_rows, own_rows), own_rows)
    out_ref[:own_rows, :] = dot_nt(pre_ref[mine, :], w_self_ref[...])
    out_ref[own_rows:, :] = jnp.zeros((out_ref.shape[0] - own_rows, out_ref.shape[1]), F32)
    end = pl.cdiv(meta_ref[COUNTS, 0], CHUNK)
    over_chunks(
        0,
        end,
        lambda c: spread_add(
            c, end, 0, window, NEAR_LOW, meta_ref, keys_ref, grad_ref, out_ref, values_ref
        ),
    )


def near_backward(half, meta, keys, grad_sum, grad_pre, w_self, rows, window=768):
    width = grad_sum.shape[1] // 2
    return pl.pallas_call(
        functools.partial(near_backward_kernel, min(window, rows)),
        in_specs=[sspec(), sspec()] + [vspec()] * 4,
        out_specs=vspec(),
        out_shape=jax.ShapeDtypeStruct((rows, width), F32),
        scratch_shapes=[VMEM((UNROLL * CHUNK, width), BF16)],
        compiler_params=params(),
        name="near_backward",
    )(half, meta, keys, grad_sum, grad_pre, w_self)


def returned_kernel(peers_step, half_ref, idx_ref, back_ref, near_ref, part_ref, acc_ref):
    nodes = part_ref.shape[0]
    own_rows = nodes // 2
    peers, slots, width = back_ref.shape
    lines = peers_step * slots // 128
    acc_ref[...] = jnp.zeros_like(acc_ref)

    def step(s, _):
        row = join([idx_ref[pl.ds(s * lines + k, 1), :] for k in range(lines)])
        rows = back_ref[pl.ds(s * peers_step, peers_step), :, :].reshape(peers_step * slots, width)
        acc_ref[...] += spread(row, columns_of(row), rows, own_rows)
        return 0

    lax.fori_loop(0, peers // peers_step, step, 0)
    part_ref[:own_rows, :] = acc_ref[:, :width]
    part_ref[own_rows:, :] = acc_ref[:, width:]
    own_span = pl.ds(pl.multiple_of(half_ref[0] * own_rows, own_rows), own_rows)
    part_ref[own_span, :] += near_ref[:own_rows, :]


def returned_sum(half, idx, back, near, nodes):
    width = back.shape[2]
    return pl.pallas_call(
        functools.partial(returned_kernel, min(32, back.shape[0])),
        in_specs=[sspec(), vspec(), vspec(), vspec()],
        out_specs=vspec(),
        out_shape=jax.ShapeDtypeStruct((nodes, width), F32),
        scratch_shapes=[VMEM((nodes // 2, 2 * width), F32)],
        compiler_params=params(),
        name="returned_sum",
    )(half, idx, back, near)


def torus_of(size):
    side = 4 if size >= 64 else 2
    return side, size // (side * side), side


def groups_of(size, axis):
    sizes = torus_of(size)
    ids = np.arange(size).reshape(sizes)
    return np.moveaxis(ids, axis, -1).reshape(-1, sizes[axis]).tolist()


X_AXIS, Z_AXIS, Y_AXIS = 0, 1, 2


def exchange(blocks, axis, size):
    return lax.all_to_all(
        blocks, "dom", 0, 0, axis_index_groups=groups_of(size, axis), tiled=True
    )


def partners(size, axis):
    step, count = ((torus_of(size)[2] * torus_of(size)[1], torus_of(size)[0]) if axis == X_AXIS
                   else (1, torus_of(size)[2]))
    return [[(i, i ^ (step * j)) for i in range(size)] for j in range(1, count)]


def swap_blocks(blocks, axis, size):
    return [blocks[0]] + [
        lax.ppermute(block, "dom", pairs) for block, pairs in zip(blocks[1:], partners(size, axis))
    ]


def pair_sum(parts):
    while len(parts) > 1:
        parts = [parts[i] + parts[i + 1] for i in range(0, len(parts), 2)]
    return parts[0]


def split_exactly(value):
    high = lax.reduce_precision(value, 8, 7)
    middle = lax.reduce_precision(value - high, 8, 7)
    return [part.astype(BF16) for part in (high, middle, value - high - middle)]


def after(value, *earlier):
    return lax.optimization_barrier((value,) + earlier)[0]


def body(
    node_feats,
    hub_feats,
    w_self,
    w_neigh,
    bias,
    cotangent,
    send_count,
    send_rows,
    edge_src,
    edge_dst,
    edge_count,
):
    num_dom = lax.axis_size("dom")
    half = lax.axis_index("edge")
    nodes, width = node_feats.shape
    block_rows = send_rows.shape[2]
    hubs = hub_feats.shape[0]
    slots, half_hubs, own_rows = block_rows // 2, hubs // 2, nodes // 2
    half_scalar = half.astype(jnp.int32).reshape(1)
    xs, zs, ys = torus_of(num_dom)
    hub_rows = num_dom * half_hubs
    near_rows, far_rows = own_rows + hub_rows, num_dom * slots

    hub_half = lax.dynamic_slice_in_dim(hub_feats, half * half_hubs, half_hubs, 0)
    hub_z = exchange(jnp.broadcast_to(hub_half[None], (zs,) + hub_half.shape), Z_AXIS, num_dom)

    me = lax.axis_index("dom")
    counts_row = jnp.pad(send_count, ((0, 0), (0, -num_dom % 128)))
    flip = ((half ^ me) & 1).astype(jnp.int32).reshape(1)
    out_rows, idx = outgoing(flip, counts_row, send_rows[0], node_feats)
    out_rows, hub_z = lax.optimization_barrier((out_rows, hub_z))
    table = lax.all_to_all(out_rows, "dom", split_axis=0, concat_axis=0, tiled=True)
    hub_z = after(hub_z.reshape(zs * half_hubs, width), out_rows)
    hub_x = jnp.concatenate(swap_blocks([hub_z] * xs, X_AXIS, num_dom))
    hub_y = jnp.concatenate(swap_blocks([hub_x] * ys, Y_AXIS, num_dom))
    own_half = lax.dynamic_slice_in_dim(node_feats, half * own_rows, own_rows, 0)
    near_table = jnp.concatenate([own_half, hub_y.reshape(hub_rows, width)])

    src = edge_src.reshape(-1)
    dst = edge_dst.reshape(-1)
    edges = src.shape[0]
    live = jnp.arange(edges, dtype=jnp.int32) < edge_count.reshape(())
    slot = src - nodes
    hub = slot - num_dom * block_rows
    is_own, is_hub = src < nodes, hub >= 0
    master = hub // hubs
    far_y, far_x = (master ^ me) & (ys - 1), (master ^ me) // (ys * zs)
    master_place = (far_y * xs + far_x) * zs + (master // ys) % zs
    row = jnp.where(
        is_own,
        src % own_rows,
        jnp.where(
            is_hub,
            own_rows + master_place * half_hubs + hub % half_hubs,
            near_rows + slot // block_rows * slots + slot % slots,
        ),
    )
    slot_side = (slot // slots ^ slot // block_rows ^ me) & 1
    side = jnp.where(is_own, src // own_rows, jnp.where(is_hub, (hub % hubs) // half_hubs, slot_side))
    key = (side << HALF_BIT) + (row << DST_BITS) + dst
    key = after(jnp.where(live, key, DEAD), out_rows)
    key_other = lax.ppermute(key, "edge", SWAP)
    every = jnp.concatenate([key, key_other])
    mine = jnp.where((every >> HALF_BIT) == half, every & ((1 << HALF_BIT) - 1), PAD)
    keys = lax.sort(mine).reshape(-1, CHUNK)
    every = every.reshape(-1, CHUNK)
    near_edge = keys < (near_rows << DST_BITS)
    live_edge = keys < PAD
    counts = [jnp.sum(edge.astype(jnp.int32)) for edge in (near_edge, live_edge)]
    near_low = jnp.minimum(keys[:, 0] >> DST_BITS, near_rows - 1)
    near_high = jnp.max(jnp.where(near_edge, keys, 0), axis=1) >> DST_BITS
    far_low = jnp.min(jnp.where(near_edge, PAD, keys), axis=1) >> DST_BITS
    far_low = jnp.minimum(far_low - near_rows, far_rows - 1)
    far_high = jnp.max(jnp.where(live_edge, keys, 0), axis=1) >> DST_BITS
    far_high = jnp.maximum(far_high - near_rows, 0)

    lines = keys.shape[0]
    counts = jnp.where(jnp.arange(lines) == 0, counts[0], counts[1])
    meta = jnp.stack([near_low, near_high, far_low, far_high, counts])

    near_sum, degree = near_forward(meta, every, keys, near_table, nodes)
    neigh = far_forward(meta, keys, table.reshape(far_rows, width), near_sum, near_rows)
    neigh_other = lax.ppermute(neigh, "edge", SWAP)
    layer_out, grad_sum, grad_pre, grad_w = dense(
        half_scalar,
        neigh,
        neigh_other,
        degree,
        node_feats,
        cotangent,
        w_self,
        w_neigh,
        bias.reshape(1, width),
    )
    share = grad_w.shape[0] // zs
    grad_w = exchange(grad_w.reshape(zs, share, width), Z_AXIS, num_dom)
    row_grads = far_backward(meta, keys, grad_sum, near_rows, far_rows)
    row_grads, grad_w = lax.optimization_barrier((row_grads, grad_w))
    back = lax.all_to_all(
        row_grads.reshape(num_dom, slots, width), "dom", split_axis=0, concat_axis=0, tiled=True
    )
    near_grads = near_backward(
        half_scalar, meta, after(keys, row_grads), grad_sum, grad_pre, w_self, near_rows
    )

    grad_w = jnp.sum(grad_w, axis=0)
    blocks = jnp.split(near_grads[own_rows:].astype(BF16), ys)
    kept = blocks[0].shape[0]
    pieces = split_exactly(grad_w)
    both = swap_blocks([jnp.concatenate([block] + pieces) for block in blocks], Y_AXIS, num_dom)
    both = [part.astype(F32) for part in both]
    hub_part = pair_sum([part[:kept] for part in both])
    grad_w = pair_sum(
        [part[kept : kept + share] + (part[kept + share : -share] + part[-share:]) for part in both]
    )
    blocks = jnp.split(hub_part, xs)
    kept = blocks[0].shape[0]
    both = pair_sum(
        swap_blocks([jnp.concatenate([block, grad_w]) for block in blocks], X_AXIS, num_dom)
    )
    other = lax.ppermute(both, "edge", SWAP)
    first = jnp.where(half == 0, both, other)
    second = jnp.where(half == 0, other, both)
    shares = jnp.concatenate([first[kept:], second[kept:]])
    both = jnp.concatenate(
        [
            first[:kept].reshape(zs, half_hubs, width),
            second[:kept].reshape(zs, half_hubs, width),
            jnp.broadcast_to(shares[None], (zs,) + shares.shape),
        ],
        axis=1,
    )
    both = exchange(after(both, back), Z_AXIS, num_dom)
    grad_hubs = jnp.sum(both[:, :hubs], axis=0)
    first = both[:, hubs : hubs + share].reshape(zs * share, width)
    second = both[:, hubs + share :].reshape(zs * share, width)
    grad_self, grad_neigh, grad_bias = first[:width], second[:width], first[width]

    part = returned_sum(half_scalar, idx, back, near_grads, nodes)
    part_other = lax.ppermute(part, "edge", SWAP)
    grad_feats = part + part_other
    return (layer_out, grad_feats, grad_hubs, grad_self, grad_neigh, grad_bias)


def solution(mesh):
    placed = (
        P("dom", None),
        P("dom", None),
        P(),
        P(),
        P(),
        P("dom", None),
        P("dom", None),
        P("dom", None, None),
        P("dom", "edge", None),
        P("dom", "edge", None),
        P("dom", "edge"),
    )
    return jax.shard_map(
        body,
        mesh=mesh,
        in_specs=placed,
        out_specs=(P("dom", None), P("dom", None), P("dom", None), P(), P(), P()),
        check_vma=False,
    )
```

```python
import functools

import jax
import jax.numpy as jnp
import numpy as np
from jax import lax
from jax.experimental import pallas as pl
from jax.experimental.pallas import tpu as pltpu
from jax.sharding import PartitionSpec as P

F32 = jnp.float32
BF16 = jnp.bfloat16
I16 = jnp.int16
VMEM = pltpu.VMEM
SMEM = pltpu.SMEM
SWAP = [(0, 1), (1, 0)]
CHUNK = 256
UNROLL = 4
DST_BITS = 10
PAD = 1 << 30
DEAD = 1 << 26
HALF_BIT = 24
META = NEAR_LOW, NEAR_HIGH, FAR_LOW, FAR_HIGH, COUNTS = 0, 1, 2, 3, 4


def params(mib=40):
    return pltpu.CompilerParams(vmem_limit_bytes=mib * 1024 * 1024)


def vspec():
    return pl.BlockSpec(memory_space=VMEM)


def hbm_spec():
    return pl.BlockSpec(memory_space=pltpu.HBM)


def copy_now(source, target, sem):
    copy = pltpu.make_async_copy(source, target, sem)
    copy.start()
    copy.wait()


def whole(value):
    return pl.BlockSpec(value.shape, lambda i: (0,) * len(value.shape))


def sspec():
    return pl.BlockSpec(memory_space=SMEM)


def columns_of(row):
    parts = []
    for at in range(0, row.shape[1], 128):
        parts.append(jnp.broadcast_to(row[:, at : at + 128], (128, 128)).T)
    return jnp.concatenate(parts, axis=0)


def onehot_of_columns(col, width):
    lane = lax.broadcasted_iota(jnp.int32, col.shape, 1).astype(I16)
    col = col.astype(I16)
    one, zero = jnp.ones((), BF16), jnp.zeros((), BF16)
    parts = [jnp.where(col == lane + I16(at), one, zero) for at in range(0, width, 128)]
    return parts[0] if len(parts) == 1 else jnp.concatenate(parts, axis=1)


def onehot_of_rows(row, height):
    sub = lax.broadcasted_iota(jnp.int32, (height, row.shape[1]), 0).astype(I16)
    return jnp.where(sub == row.astype(I16), jnp.ones((), BF16), jnp.zeros((), BF16))


def in_hbm(value):
    return pltpu.with_memory_space_constraint(value, pltpu.HBM)


def dot(a, b):
    return jnp.dot(a, b, preferred_element_type=F32)


def dot_nt(a, b):
    return lax.dot_general(a, b, (((1,), (1,)), ((), ())), preferred_element_type=F32)


def dot_tn(a, b):
    return lax.dot_general(a, b, (((0,), (0,)), ((), ())), preferred_element_type=F32)


def pick(col, wide):
    rows = wide.shape[0]
    both = dot(onehot_of_columns(jnp.where(col >= rows, col - rows, col), rows), wide)
    return jnp.where(col >= rows, both[:, 128:], both[:, :128])


def spread(row, col, values, rows):
    left = col.astype(I16) < I16(rows)
    zero = jnp.zeros((), BF16)
    pair = jnp.concatenate([jnp.where(left, values, zero), jnp.where(left, zero, values)], axis=1)
    return dot(onehot_of_rows(jnp.where(row >= rows, row - rows, row), rows), pair)


def join(refs_at):
    return jnp.concatenate(refs_at, axis=1)


def outgoing_kernel(flip_ref, count_ref, rows_ref, feat_ref, out_ref, idx_ref, wide_ref, all_ref):
    step = pl.program_id(0)
    peers, slots, width = out_ref.shape
    nodes = feat_ref.shape[0]
    lines = peers * slots // 128

    @pl.when(step == 0)
    def _():
        wide_ref[:, :width] = feat_ref[: nodes // 2, :]
        wide_ref[:, width:] = feat_ref[nodes // 2 :, :]
        count = columns_of(count_ref[...])[: rows_ref.shape[0], :]
        lane = lax.broadcasted_iota(jnp.int32, rows_ref.shape, 1)
        all_ref[...] = jnp.where(lane < count, rows_ref[...], -1)
        pairs = rows_ref.shape[0] // 2
        even = all_ref[pl.ds(0, pairs, stride=2), :]
        odd = all_ref[pl.ds(1, pairs, stride=2), :]
        low = lax.broadcasted_iota(jnp.int32, even.shape, 1) < slots
        crossed = pltpu.roll(jnp.where(low, odd, even), slots, 1)
        idx_ref[...] = jnp.where(flip_ref[0] == 0, jnp.where(low, even, odd), crossed)

    row = join([idx_ref[pl.ds(step * lines + k, 1), :] for k in range(lines)])
    out_ref[...] = pick(columns_of(row), wide_ref[...]).astype(BF16).reshape(peers, slots, width)


def outgoing(flip, count, rows, feats, step_peers=32):
    peers, slots = rows.shape[0], rows.shape[1] // 2
    nodes, width = feats.shape
    step_peers = min(step_peers, peers)
    lines = peers * slots // 128
    return pl.pallas_call(
        outgoing_kernel,
        grid=(peers // step_peers,),
        in_specs=[
            sspec(),
            pl.BlockSpec(count.shape, lambda i: (0, 0)),
            pl.BlockSpec(rows.shape, lambda i: (0, 0)),
            pl.BlockSpec(feats.shape, lambda i: (0, 0)),
        ],
        out_specs=[
            pl.BlockSpec((step_peers, slots, width), lambda i: (i, 0, 0)),
            pl.BlockSpec((lines, 128), lambda i: (0, 0)),
        ],
        out_shape=[
            pltpu.HBM((peers, slots, width), BF16),
            jax.ShapeDtypeStruct((lines, 128), jnp.int32),
        ],
        scratch_shapes=[VMEM((nodes // 2, 2 * width), BF16), VMEM(rows.shape, jnp.int32)],
        compiler_params=params(),
        name="outgoing_rows",
    )(flip, count, rows, feats)


def relative(row, base, start, window):
    return jnp.where((row >= base) & (row < start + window), row - start, -1)


def window_of(meta_ref, low_at, c, w, rows, window):
    base = meta_ref[low_at, c] // 128 * 128 + w * window
    return base, pl.multiple_of(jnp.minimum(base, rows - window), 128)


def windows_of(meta_ref, low_at, c, window):
    return (meta_ref[low_at + 1, c] - meta_ref[low_at, c] // 128 * 128) // window + 1


def keys_of(keys_ref, c, end):
    at = jnp.minimum(c, keys_ref.shape[0] - 1)
    return at, jnp.where(c < end, keys_ref[pl.ds(at, 1), :], PAD)


def gather_add(first, end, offset, window, low_at, meta_ref, keys_ref, table_ref, sum_ref, values_ref):
    half_nodes = sum_ref.shape[0]
    rows = table_ref.shape[0]
    half = window // 2

    def picked(c, w, col):
        base, start = window_of(meta_ref, low_at, c, w, rows, window)
        wide = join([table_ref[pl.ds(start, half), :], table_ref[pl.ds(start + half, half), :]])
        return pick(relative((col >> DST_BITS) - offset, base, start, window), wide)

    keys, cols = [], []
    for u in range(UNROLL):
        c, key = keys_of(keys_ref, first + u, end)
        keys.append(key)
        cols.append(columns_of(key))
        values_ref[u * CHUNK : (u + 1) * CHUNK, :] = picked(c, 0, cols[u])
    for u in range(UNROLL):
        c, key = keys_of(keys_ref, first + u, end)

        def more(w, _, c=c, key=key, u=u):
            values_ref[u * CHUNK : (u + 1) * CHUNK, :] += picked(c, w, columns_of(key))
            return 0

        lax.fori_loop(1, windows_of(meta_ref, low_at, c, window), more, 0)
    nodes = 2 * half_nodes
    sum_ref[...] += spread(
        join(keys) & (nodes - 1),
        jnp.concatenate(cols, axis=0) & (nodes - 1),
        values_ref[...].astype(BF16),
        half_nodes,
    )


def spread_add(first, end, offset, window, low_at, meta_ref, keys_ref, grad_ref, acc_ref, values_ref):
    nodes = 2 * grad_ref.shape[0]
    rows = acc_ref.shape[0]
    half = window // 2

    def add(c, w, key, col, values):
        base, start = window_of(meta_ref, low_at, c, w, rows, window)
        row, col = (
            relative((k >> DST_BITS) - offset, base, start, window) for k in (key, col)
        )
        both = spread(row, col, values, half)
        acc_ref[pl.ds(start, half), :] += both[:, :128]
        acc_ref[pl.ds(start + half, half), :] += both[:, 128:]

    keys = [keys_of(keys_ref, first + u, end) for u in range(UNROLL)]
    cols = [columns_of(key) for _, key in keys]
    values = pick(jnp.concatenate(cols, axis=0) & (nodes - 1), grad_ref[...]).astype(BF16)
    values_ref[...] = values
    for u, (c, key) in enumerate(keys):
        add(c, 0, key, cols[u], values[u * CHUNK : (u + 1) * CHUNK])
    for u in range(UNROLL):
        c, key = keys_of(keys_ref, first + u, end)

        def more(w, _, c=c, key=key, u=u):
            add(c, w, key, columns_of(key), values_ref[u * CHUNK : (u + 1) * CHUNK, :])
            return 0

        lax.fori_loop(1, windows_of(meta_ref, low_at, c, window), more, 0)


def over_chunks(first, end, visit):
    def step(i, _):
        visit(first + i * UNROLL)
        return 0

    lax.fori_loop(0, pl.cdiv(end - first, UNROLL), step, 0)


def near_forward_kernel(
    window, meta_ref, every_ref, keys_ref, table_ref, sum_hbm, deg_hbm, sum_ref, deg_ref, values_ref, sem
):
    nodes = 2 * sum_ref.shape[0]
    deg_ref[...] = jnp.zeros_like(deg_ref)
    sum_ref[...] = jnp.zeros_like(sum_ref)

    def degrees(c, _):
        key = join([every_ref[pl.ds(c * UNROLL + u, 1), :] for u in range(UNROLL)])
        dst = key & (nodes - 1)
        high = jnp.where(key < DEAD, dst >> 7, deg_ref.shape[0])
        deg_ref[...] += dot_nt(
            onehot_of_rows(high, deg_ref.shape[0]), onehot_of_rows(dst & 127, 128)
        )
        return 0

    lax.fori_loop(0, every_ref.shape[0] // UNROLL, degrees, 0)
    end = pl.cdiv(meta_ref[COUNTS, 0], CHUNK)
    over_chunks(
        0,
        end,
        lambda c: gather_add(
            c, end, 0, window, NEAR_LOW, meta_ref, keys_ref, table_ref, sum_ref, values_ref
        ),
    )
    copy_now(sum_ref, sum_hbm, sem)
    copy_now(deg_ref, deg_hbm, sem)


def near_forward(meta, every, keys, table, nodes, window=768):
    width = table.shape[1]
    shapes = [(nodes // 2, 2 * width), (16, 128)]
    return pl.pallas_call(
        functools.partial(near_forward_kernel, min(window, table.shape[0])),
        in_specs=[sspec(), vspec(), vspec(), vspec()],
        out_specs=[hbm_spec(), hbm_spec()],
        out_shape=[pltpu.HBM(shape, F32) for shape in shapes],
        scratch_shapes=[VMEM(shape, F32) for shape in shapes]
        + [VMEM((UNROLL * CHUNK, width), F32), pltpu.SemaphoreType.DMA],
        compiler_params=params(),
        name="near_forward",
    )(meta, every, keys, table)


def far_forward_kernel(
    offset, window, meta_ref, keys_ref, table_ref, base_hbm, sum_ref, values_ref, base_ref, sem
):
    base_copy = pltpu.make_async_copy(base_hbm, base_ref, sem)
    base_copy.start()
    sum_ref[...] = jnp.zeros_like(sum_ref)
    end = pl.cdiv(meta_ref[COUNTS, 1], CHUNK)
    over_chunks(
        meta_ref[COUNTS, 0] // CHUNK,
        end,
        lambda c: gather_add(
            c, end, offset, window, FAR_LOW, meta_ref, keys_ref, table_ref, sum_ref, values_ref
        ),
    )
    base_copy.wait()
    sum_ref[...] += base_ref[...]


def far_forward(meta, keys, table, base, offset, window=1280):
    return pl.pallas_call(
        functools.partial(far_forward_kernel, offset, min(window, table.shape[0])),
        in_specs=[sspec(), vspec(), vspec(), hbm_spec()],
        out_specs=vspec(),
        out_shape=jax.ShapeDtypeStruct(base.shape, F32),
        scratch_shapes=[
            VMEM((UNROLL * CHUNK, table.shape[1]), F32),
            VMEM(base.shape, F32),
            pltpu.SemaphoreType.DMA,
        ],
        compiler_params=params(),
        name="far_forward",
    )(meta, keys, table, in_hbm(base))


def dense_kernel(
    half_ref,
    mine_ref,
    other_ref,
    deg_ref,
    feat_ref,
    cot_ref,
    w_self_ref,
    w_neigh_ref,
    bias_ref,
    out_ref,
    grad_sum_ref,
    pre_ref,
    grad_w_ref,
    left_ref,
):
    nodes = feat_ref.shape[0]
    grad_bias = jnp.zeros((8, 128), F32)
    for at in range(0, nodes, 128):
        span = pl.ds(at, 128)
        h = at // 128
        divisor = jnp.maximum(columns_of(deg_ref[h : h + 1, :]), 1.0)
        feats = feat_ref[span, :]
        place = (pl.ds(at % (nodes // 2), 128), pl.ds(at // (nodes // 2) * 128, 128))
        aggregate = ((mine_ref[place] + other_ref[place]) / divisor).astype(BF16)
        preact = dot(feats, w_self_ref[...]) + dot(aggregate, w_neigh_ref[...]) + bias_ref[...]
        sig = jax.nn.sigmoid(preact)
        out_ref[span, :] = (preact * sig).astype(BF16)
        slope = sig * (1.0 + preact * (1.0 - sig))
        grad_pre = (cot_ref[span, :].astype(F32) * slope).astype(BF16)
        pre_ref[span, :] = grad_pre
        grad_sum_ref[place] = (dot_nt(grad_pre, w_neigh_ref[...]) / divisor).astype(BF16)
        left_ref[span, :] = jnp.where(half_ref[0] == 0, feats.astype(F32), aggregate.astype(F32)).astype(BF16)
        wide = grad_pre.astype(F32)
        for r in range(0, 128, 8):
            grad_bias = grad_bias + wide[r : r + 8]
    grad_w_ref[:128, :] = dot_tn(left_ref[...], pre_ref[...])
    grad_w_ref[128:, :] = jnp.broadcast_to(
        jnp.sum(grad_bias, axis=0, keepdims=True), (grad_w_ref.shape[0] - 128, 128)
    )


def dense(half, mine, other, deg, feats, cot, w_self, w_neigh, bias):
    nodes, width = feats.shape
    outs = [
        jax.ShapeDtypeStruct((nodes, width), BF16),
        jax.ShapeDtypeStruct((nodes // 2, 2 * width), BF16),
        jax.ShapeDtypeStruct((nodes, width), BF16),
        jax.ShapeDtypeStruct((192, width), F32),
    ]
    return pl.pallas_call(
        dense_kernel,
        grid=(1,),
        in_specs=[sspec()] + [whole(x) for x in (mine, other, deg, feats, cot, w_self, w_neigh, bias)],
        out_specs=[whole(x) for x in outs],
        out_shape=outs,
        scratch_shapes=[VMEM((nodes, width), BF16)],
        compiler_params=params(),
        name="dense_part",
    )(half, mine, other, in_hbm(deg), in_hbm(feats), in_hbm(cot), in_hbm(w_self), in_hbm(w_neigh), in_hbm(bias))


def far_backward_kernel(offset, window, meta_ref, keys_ref, grad_ref, out_ref, acc_ref, values_ref):
    rows = acc_ref.shape[0]
    block = out_ref.shape[0]

    @pl.when(pl.program_id(0) == 0)
    def _():
        def clear(b, _):
            span = pl.ds(pl.multiple_of(b * block, block), block)
            acc_ref[span, :] = jnp.zeros((block, acc_ref.shape[1]), F32)
            return 0

        lax.fori_loop(0, rows // block, clear, 0)
        end = pl.cdiv(meta_ref[COUNTS, 1], CHUNK)
        over_chunks(
            meta_ref[COUNTS, 0] // CHUNK,
            end,
            lambda c: spread_add(
                c, end, offset, window, FAR_LOW, meta_ref, keys_ref, grad_ref, acc_ref, values_ref
            ),
        )

    at = pl.multiple_of(pl.program_id(0) * block, block)
    out_ref[...] = acc_ref[pl.ds(at, block), :].astype(BF16)


def far_backward(meta, keys, grad_sum, offset, rows, window=1280):
    width = grad_sum.shape[1] // 2
    block = min(2048, rows)
    return pl.pallas_call(
        functools.partial(far_backward_kernel, offset, min(window, rows)),
        grid=(rows // block,),
        in_specs=[
            sspec(),
            pl.BlockSpec(keys.shape, lambda i: (0, 0)),
            pl.BlockSpec(grad_sum.shape, lambda i: (0, 0)),
        ],
        out_specs=pl.BlockSpec((block, width), lambda i: (i, 0)),
        out_shape=pltpu.HBM((rows, width), BF16),
        scratch_shapes=[VMEM((rows, width), F32), VMEM((UNROLL * CHUNK, width), BF16)],
        compiler_params=params(),
        name="far_backward",
    )(meta, keys, grad_sum)


def near_backward_kernel(
    window, half_ref, meta_ref, keys_ref, grad_ref, pre_ref, w_self_ref, out_ref, values_ref
):
    own_rows = pre_ref.shape[0] // 2
    mine = pl.ds(pl.multiple_of(half_ref[0] * own_rows, own_rows), own_rows)
    out_ref[:own_rows, :] = dot_nt(pre_ref[mine, :], w_self_ref[...])
    out_ref[own_rows:, :] = jnp.zeros((out_ref.shape[0] - own_rows, out_ref.shape[1]), F32)
    end = pl.cdiv(meta_ref[COUNTS, 0], CHUNK)
    over_chunks(
        0,
        end,
        lambda c: spread_add(
            c, end, 0, window, NEAR_LOW, meta_ref, keys_ref, grad_ref, out_ref, values_ref
        ),
    )


def near_backward(half, meta, keys, grad_sum, grad_pre, w_self, rows, window=768):
    width = grad_sum.shape[1] // 2
    return pl.pallas_call(
        functools.partial(near_backward_kernel, min(window, rows)),
        in_specs=[sspec(), sspec()] + [vspec()] * 4,
        out_specs=vspec(),
        out_shape=jax.ShapeDtypeStruct((rows, width), F32),
        scratch_shapes=[VMEM((UNROLL * CHUNK, width), BF16)],
        compiler_params=params(),
        name="near_backward",
    )(half, meta, keys, grad_sum, grad_pre, w_self)


def returned_kernel(
    peers_step, half_ref, idx_ref, back_ref, near_ref, part_hbm, part_ref, acc_ref, sem
):
    nodes = part_ref.shape[0]
    own_rows = nodes // 2
    peers, slots, width = back_ref.shape
    lines = peers_step * slots // 128
    acc_ref[...] = jnp.zeros_like(acc_ref)

    def step(s, _):
        row = join([idx_ref[pl.ds(s * lines + k, 1), :] for k in range(lines)])
        rows = back_ref[pl.ds(s * peers_step, peers_step), :, :].reshape(peers_step * slots, width)
        acc_ref[...] += spread(row, columns_of(row), rows, own_rows)
        return 0

    lax.fori_loop(0, peers // peers_step, step, 0)
    part_ref[:own_rows, :] = acc_ref[:, :width]
    part_ref[own_rows:, :] = acc_ref[:, width:]
    own_span = pl.ds(pl.multiple_of(half_ref[0] * own_rows, own_rows), own_rows)
    part_ref[own_span, :] += near_ref[:own_rows, :]
    copy_now(part_ref, part_hbm, sem)


def returned_sum(half, idx, back, near, nodes):
    width = back.shape[2]
    return pl.pallas_call(
        functools.partial(returned_kernel, min(32, back.shape[0])),
        in_specs=[sspec(), vspec(), vspec(), vspec()],
        out_specs=hbm_spec(),
        out_shape=pltpu.HBM((nodes, width), F32),
        scratch_shapes=[
            VMEM((nodes, width), F32),
            VMEM((nodes // 2, 2 * width), F32),
            pltpu.SemaphoreType.DMA,
        ],
        compiler_params=params(),
        name="returned_sum",
    )(half, idx, back, near)


def finish_kernel(
    hubs, mine_ref, other_ref, both_ref, feats_ref, hubs_ref, self_ref, neigh_ref, bias_ref
):
    width = mine_ref.shape[1]
    places = both_ref.shape[0]
    share = (both_ref.shape[1] - hubs) // 2
    feats_ref[...] = mine_ref[...] + other_ref[...]
    hubs_ref[...] = pair_sum([both_ref[j, :hubs, :] for j in range(places)])
    for row in range(0, width, 8):
        j, at = row // share, hubs + row % share
        self_ref[row : row + 8, :] = both_ref[j, at : at + 8, :]
        neigh_ref[row : row + 8, :] = both_ref[j, at + share : at + share + 8, :]
    at = hubs + width % share
    bias_ref[...] = both_ref[width // share, at : at + 8, :]


def finish(mine, other, both, hubs):
    nodes, width = mine.shape
    outs = [
        jax.ShapeDtypeStruct(shape, F32)
        for shape in ((nodes, width), (hubs, width), (width, width), (width, width), (8, width))
    ]
    return pl.pallas_call(
        functools.partial(finish_kernel, hubs),
        grid=(1,),
        in_specs=[whole(x) for x in (mine, other, both)],
        out_specs=[whole(x) for x in outs],
        out_shape=outs,
        compiler_params=params(),
        name="finish",
    )(in_hbm(mine), in_hbm(other), in_hbm(both))


def torus_of(size):
    side = 4 if size >= 64 else 2
    return side, size // (side * side), side


def groups_of(size, axis):
    sizes = torus_of(size)
    ids = np.arange(size).reshape(sizes)
    return np.moveaxis(ids, axis, -1).reshape(-1, sizes[axis]).tolist()


X_AXIS, Z_AXIS, Y_AXIS = 0, 1, 2


def exchange(blocks, axis, size):
    return lax.all_to_all(
        blocks, "dom", 0, 0, axis_index_groups=groups_of(size, axis), tiled=True
    )


def partners(size, axis):
    sizes = torus_of(size)
    step, count = {X_AXIS: sizes[1] * sizes[2], Z_AXIS: sizes[2], Y_AXIS: 1}[axis], sizes[axis]
    return [[(i, i ^ (step * j)) for i in range(size)] for j in range(1, count)]


def swap_blocks(blocks, axis, size):
    return [blocks[0]] + [
        lax.ppermute(block, "dom", pairs) for block, pairs in zip(blocks[1:], partners(size, axis))
    ]


def pair_sum(parts):
    while len(parts) > 1:
        parts = [parts[i] + parts[i + 1] for i in range(0, len(parts), 2)]
    return parts[0]


def split_exactly(value):
    high = lax.reduce_precision(value, 8, 7)
    middle = lax.reduce_precision(value - high, 8, 7)
    return [part.astype(BF16) for part in (high, middle, value - high - middle)]


def after(value, *earlier):
    return lax.optimization_barrier((value,) + earlier)[0]


def body(
    node_feats,
    hub_feats,
    w_self,
    w_neigh,
    bias,
    cotangent,
    send_count,
    send_rows,
    edge_src,
    edge_dst,
    edge_count,
):
    num_dom = lax.axis_size("dom")
    half = lax.axis_index("edge")
    nodes, width = node_feats.shape
    block_rows = send_rows.shape[2]
    hubs = hub_feats.shape[0]
    slots, half_hubs, own_rows = block_rows // 2, hubs // 2, nodes // 2
    half_scalar = half.astype(jnp.int32).reshape(1)
    xs, zs, ys = torus_of(num_dom)
    hub_rows = num_dom * half_hubs
    near_rows, far_rows = own_rows + hub_rows, num_dom * slots

    hub_half = lax.dynamic_slice_in_dim(hub_feats, half * half_hubs, half_hubs, 0)
    hub_z = exchange(jnp.broadcast_to(hub_half[None], (zs,) + hub_half.shape), Z_AXIS, num_dom)

    me = lax.axis_index("dom")
    counts_row = jnp.pad(send_count, ((0, 0), (0, -num_dom % 128)))
    flip = ((half ^ me) & 1).astype(jnp.int32).reshape(1)
    out_rows, idx = outgoing(flip, counts_row, send_rows[0], node_feats)
    out_rows, hub_z = lax.optimization_barrier((out_rows, hub_z))
    table = lax.all_to_all(out_rows, "dom", split_axis=0, concat_axis=0, tiled=True)
    hub_z = after(hub_z.reshape(zs * half_hubs, width), out_rows)
    hub_x = jnp.concatenate(swap_blocks([hub_z] * xs, X_AXIS, num_dom))
    hub_y = jnp.concatenate(swap_blocks([hub_x] * ys, Y_AXIS, num_dom))
    own_half = lax.dynamic_slice_in_dim(node_feats, half * own_rows, own_rows, 0)
    near_table = jnp.concatenate([own_half, hub_y.reshape(hub_rows, width)])

    src = edge_src.reshape(-1)
    dst = edge_dst.reshape(-1)
    edges = src.shape[0]
    live = jnp.arange(edges, dtype=jnp.int32) < edge_count.reshape(())
    slot = src - nodes
    hub = slot - num_dom * block_rows
    is_own, is_hub = src < nodes, hub >= 0
    master = hub // hubs
    far_y, far_x = (master ^ me) & (ys - 1), (master ^ me) // (ys * zs)
    master_place = (far_y * xs + far_x) * zs + (master // ys) % zs
    row = jnp.where(
        is_own,
        src % own_rows,
        jnp.where(
            is_hub,
            own_rows + master_place * half_hubs + hub % half_hubs,
            near_rows + slot // block_rows * slots + slot % slots,
        ),
    )
    slot_side = (slot // slots ^ slot // block_rows ^ me) & 1
    side = jnp.where(is_own, src // own_rows, jnp.where(is_hub, (hub % hubs) // half_hubs, slot_side))
    key = (side << HALF_BIT) + (row << DST_BITS) + dst
    key = after(jnp.where(live, key, DEAD), out_rows)
    key_other = lax.ppermute(key, "edge", SWAP)
    every = jnp.concatenate([key, key_other])
    mine = jnp.where((every >> HALF_BIT) == half, every & ((1 << HALF_BIT) - 1), PAD)
    keys = lax.sort(mine).reshape(-1, CHUNK)
    every = every.reshape(-1, CHUNK)
    near_edge = keys < (near_rows << DST_BITS)
    live_edge = keys < PAD
    counts = [jnp.sum(edge.astype(jnp.int32)) for edge in (near_edge, live_edge)]
    near_low = jnp.minimum(keys[:, 0] >> DST_BITS, near_rows - 1)
    near_high = jnp.max(jnp.where(near_edge, keys, 0), axis=1) >> DST_BITS
    far_low = jnp.min(jnp.where(near_edge, PAD, keys), axis=1) >> DST_BITS
    far_low = jnp.minimum(far_low - near_rows, far_rows - 1)
    far_high = jnp.max(jnp.where(live_edge, keys, 0), axis=1) >> DST_BITS
    far_high = jnp.maximum(far_high - near_rows, 0)

    lines = keys.shape[0]
    counts = jnp.where(jnp.arange(lines) == 0, counts[0], counts[1])
    meta = jnp.stack([near_low, near_high, far_low, far_high, counts])

    near_sum, degree = near_forward(meta, every, keys, near_table, nodes)
    neigh = far_forward(meta, keys, table.reshape(far_rows, width), near_sum, near_rows)
    neigh_other = lax.ppermute(neigh, "edge", SWAP)
    layer_out, grad_sum, grad_pre, grad_w = dense(
        half_scalar,
        neigh,
        neigh_other,
        degree,
        node_feats,
        cotangent,
        w_self,
        w_neigh,
        bias.reshape(1, width),
    )
    share = grad_w.shape[0] // zs
    grad_w = exchange(grad_w.reshape(zs, share, width), Z_AXIS, num_dom)
    row_grads = far_backward(meta, keys, grad_sum, near_rows, far_rows)
    row_grads, grad_w = lax.optimization_barrier((row_grads, grad_w))
    back = lax.all_to_all(
        row_grads.reshape(num_dom, slots, width), "dom", split_axis=0, concat_axis=0, tiled=True
    )
    near_grads = near_backward(
        half_scalar, meta, after(keys, row_grads), grad_sum, grad_pre, w_self, near_rows
    )

    grad_w = jnp.sum(grad_w, axis=0)
    blocks = jnp.split(near_grads[own_rows:].astype(BF16), ys)
    kept = blocks[0].shape[0]
    pieces = split_exactly(grad_w)
    both = swap_blocks([jnp.concatenate([block] + pieces) for block in blocks], Y_AXIS, num_dom)
    both = [part.astype(F32) for part in both]
    hub_part = pair_sum([part[:kept] for part in both])
    grad_w = pair_sum(
        [part[kept : kept + share] + (part[kept + share : -share] + part[-share:]) for part in both]
    )
    blocks = jnp.split(hub_part, xs)
    kept = blocks[0].shape[0]
    both = pair_sum(
        swap_blocks([jnp.concatenate([block, grad_w]) for block in blocks], X_AXIS, num_dom)
    )
    other = lax.ppermute(both, "edge", SWAP)
    first = jnp.where(half == 0, both, other)
    second = jnp.where(half == 0, other, both)
    shares = jnp.concatenate([first[kept:], second[kept:]])
    both = jnp.concatenate(
        [
            first[:kept].reshape(zs, half_hubs, width),
            second[:kept].reshape(zs, half_hubs, width),
            jnp.broadcast_to(shares[None], (zs,) + shares.shape),
        ],
        axis=1,
    )
    both = exchange(after(both, back), Z_AXIS, num_dom)
    part = returned_sum(half_scalar, idx, back, near_grads, nodes)
    part_other = lax.ppermute(part, "edge", SWAP)
    grad_feats, grad_hubs, grad_self, grad_neigh, grad_bias = finish(part, part_other, both, hubs)
    return (layer_out, grad_feats, grad_hubs, grad_self, grad_neigh, grad_bias[0])


def solution(mesh):
    placed = (
        P("dom", None),
        P("dom", None),
        P(),
        P(),
        P(),
        P("dom", None),
        P("dom", None),
        P("dom", None, None),
        P("dom", "edge", None),
        P("dom", "edge", None),
        P("dom", "edge"),
    )
    return jax.shard_map(
        body,
        mesh=mesh,
        in_specs=placed,
        out_specs=(P("dom", None), P("dom", None), P("dom", None), P(), P(), P()),
        check_vma=False,
    )
```

```python
import functools

import jax
import jax.numpy as jnp
import numpy as np
from jax import lax
from jax.experimental import pallas as pl
from jax.experimental.pallas import tpu as pltpu
from jax.sharding import PartitionSpec as P

F32 = jnp.float32
BF16 = jnp.bfloat16
I16 = jnp.int16
VMEM = pltpu.VMEM
SMEM = pltpu.SMEM
SWAP = [(0, 1), (1, 0)]
CHUNK = 256
UNROLL = 6
DEGREE_LINES = 8
DST_BITS = 10
PAD = 1 << 30
DEAD = 1 << 26
HALF_BIT = 24
META = NEAR_LOW, NEAR_HIGH, FAR_LOW, FAR_HIGH, COUNTS = 0, 1, 2, 3, 4


def params(mib=40):
    return pltpu.CompilerParams(vmem_limit_bytes=mib * 1024 * 1024)


def vspec():
    return pl.BlockSpec(memory_space=VMEM)


def hbm_spec():
    return pl.BlockSpec(memory_space=pltpu.HBM)


def copy_now(source, target, sem):
    copy = pltpu.make_async_copy(source, target, sem)
    copy.start()
    copy.wait()


def whole(value):
    return pl.BlockSpec(value.shape, lambda i: (0,) * len(value.shape))


def sspec():
    return pl.BlockSpec(memory_space=SMEM)


def columns_of(row):
    parts = []
    for at in range(0, row.shape[1], 128):
        parts.append(jnp.broadcast_to(row[:, at : at + 128], (128, 128)).T)
    return jnp.concatenate(parts, axis=0)


def onehot_of_columns(col, width):
    lane = lax.broadcasted_iota(jnp.int32, col.shape, 1).astype(I16)
    col = col.astype(I16)
    one, zero = jnp.ones((), BF16), jnp.zeros((), BF16)
    parts = [jnp.where(col == lane + I16(at), one, zero) for at in range(0, width, 128)]
    return parts[0] if len(parts) == 1 else jnp.concatenate(parts, axis=1)


def onehot_of_rows(row, height):
    sub = lax.broadcasted_iota(jnp.int32, (height, row.shape[1]), 0).astype(I16)
    return jnp.where(sub == row.astype(I16), jnp.ones((), BF16), jnp.zeros((), BF16))


def in_hbm(value):
    return pltpu.with_memory_space_constraint(value, pltpu.HBM)


def dot(a, b):
    return jnp.dot(a, b, preferred_element_type=F32)


def dot_nt(a, b):
    return lax.dot_general(a, b, (((1,), (1,)), ((), ())), preferred_element_type=F32)


def dot_tn(a, b):
    return lax.dot_general(a, b, (((0,), (0,)), ((), ())), preferred_element_type=F32)


def pick(col, wide):
    rows = wide.shape[0]
    both = dot(onehot_of_columns(jnp.where(col >= rows, col - rows, col), rows), wide)
    return jnp.where(col >= rows, both[:, 128:], both[:, :128])


def spread(row, col, values, rows):
    left = col.astype(I16) < I16(rows)
    zero = jnp.zeros((), BF16)
    pair = jnp.concatenate([jnp.where(left, values, zero), jnp.where(left, zero, values)], axis=1)
    return dot(onehot_of_rows(jnp.where(row >= rows, row - rows, row), rows), pair)


def join(refs_at):
    return jnp.concatenate(refs_at, axis=1)


def outgoing_kernel(flip_ref, count_ref, rows_ref, feat_ref, out_ref, idx_ref, wide_ref, all_ref):
    step = pl.program_id(0)
    peers, slots, width = out_ref.shape
    nodes = feat_ref.shape[0]
    lines = peers * slots // 128

    @pl.when(step == 0)
    def _():
        wide_ref[:, :width] = feat_ref[: nodes // 2, :]
        wide_ref[:, width:] = feat_ref[nodes // 2 :, :]
        count = columns_of(count_ref[...])[: rows_ref.shape[0], :]
        lane = lax.broadcasted_iota(jnp.int32, rows_ref.shape, 1)
        all_ref[...] = jnp.where(lane < count, rows_ref[...], -1)
        pairs = rows_ref.shape[0] // 2
        even = all_ref[pl.ds(0, pairs, stride=2), :]
        odd = all_ref[pl.ds(1, pairs, stride=2), :]
        low = lax.broadcasted_iota(jnp.int32, even.shape, 1) < slots
        crossed = pltpu.roll(jnp.where(low, odd, even), slots, 1)
        idx_ref[...] = jnp.where(flip_ref[0] == 0, jnp.where(low, even, odd), crossed)

    row = join([idx_ref[pl.ds(step * lines + k, 1), :] for k in range(lines)])
    out_ref[...] = pick(columns_of(row), wide_ref[...]).astype(BF16).reshape(peers, slots, width)


def outgoing(flip, count, rows, feats, step_peers=32):
    peers, slots = rows.shape[0], rows.shape[1] // 2
    nodes, width = feats.shape
    step_peers = min(step_peers, peers)
    lines = peers * slots // 128
    return pl.pallas_call(
        outgoing_kernel,
        grid=(peers // step_peers,),
        in_specs=[
            sspec(),
            pl.BlockSpec(count.shape, lambda i: (0, 0)),
            pl.BlockSpec(rows.shape, lambda i: (0, 0)),
            pl.BlockSpec(feats.shape, lambda i: (0, 0)),
        ],
        out_specs=[
            pl.BlockSpec((step_peers, slots, width), lambda i: (i, 0, 0)),
            pl.BlockSpec((lines, 128), lambda i: (0, 0)),
        ],
        out_shape=[
            pltpu.HBM((peers, slots, width), BF16),
            jax.ShapeDtypeStruct((lines, 128), jnp.int32),
        ],
        scratch_shapes=[VMEM((nodes // 2, 2 * width), BF16), VMEM(rows.shape, jnp.int32)],
        compiler_params=params(),
        name="outgoing_rows",
    )(flip, in_hbm(count), in_hbm(rows), in_hbm(feats))


def relative(row, base, start, window):
    return jnp.where((row >= base) & (row < start + window), row - start, -1)


def window_of(meta_ref, low_at, c, w, rows, window):
    base = meta_ref[low_at, c] // 128 * 128 + w * window
    return base, pl.multiple_of(jnp.minimum(base, rows - window), 128)


def windows_of(meta_ref, low_at, c, window):
    return (meta_ref[low_at + 1, c] - meta_ref[low_at, c] // 128 * 128) // window + 1


def keys_of(keys_ref, c, end):
    at = jnp.minimum(c, keys_ref.shape[0] - 1)
    return at, jnp.where(c < end, keys_ref[pl.ds(at, 1), :], PAD)


def gather_add(first, end, offset, window, low_at, meta_ref, keys_ref, table_ref, sum_ref, values_ref):
    half_nodes = sum_ref.shape[0]
    rows = table_ref.shape[0]
    half = window // 2

    def picked(c, w, col):
        base, start = window_of(meta_ref, low_at, c, w, rows, window)
        wide = join([table_ref[pl.ds(start, half), :], table_ref[pl.ds(start + half, half), :]])
        return pick(relative((col >> DST_BITS) - offset, base, start, window), wide)

    keys, cols = [], []
    for u in range(UNROLL):
        c, key = keys_of(keys_ref, first + u, end)
        keys.append(key)
        cols.append(columns_of(key))
        values_ref[u * CHUNK : (u + 1) * CHUNK, :] = picked(c, 0, cols[u])
    for u in range(UNROLL):
        c, key = keys_of(keys_ref, first + u, end)

        def more(w, _, c=c, key=key, u=u):
            values_ref[u * CHUNK : (u + 1) * CHUNK, :] += picked(c, w, columns_of(key))
            return 0

        lax.fori_loop(1, windows_of(meta_ref, low_at, c, window), more, 0)
    nodes = 2 * half_nodes
    sum_ref[...] += spread(
        join(keys) & (nodes - 1),
        jnp.concatenate(cols, axis=0) & (nodes - 1),
        values_ref[...].astype(BF16),
        half_nodes,
    )


def spread_add(first, end, offset, window, low_at, meta_ref, keys_ref, grad_ref, acc_ref, values_ref):
    nodes = 2 * grad_ref.shape[0]
    rows = acc_ref.shape[0]
    half = window // 2

    def add(c, w, key, col, values):
        base, start = window_of(meta_ref, low_at, c, w, rows, window)
        row, col = (
            relative((k >> DST_BITS) - offset, base, start, window) for k in (key, col)
        )
        both = spread(row, col, values, half)
        acc_ref[pl.ds(start, half), :] += both[:, :128]
        acc_ref[pl.ds(start + half, half), :] += both[:, 128:]

    keys = [keys_of(keys_ref, first + u, end) for u in range(UNROLL)]
    cols = [columns_of(key) for _, key in keys]
    values = pick(jnp.concatenate(cols, axis=0) & (nodes - 1), grad_ref[...]).astype(BF16)
    values_ref[...] = values
    for u, (c, key) in enumerate(keys):
        add(c, 0, key, cols[u], values[u * CHUNK : (u + 1) * CHUNK])
    for u in range(UNROLL):
        c, key = keys_of(keys_ref, first + u, end)

        def more(w, _, c=c, key=key, u=u):
            add(c, w, key, columns_of(key), values_ref[u * CHUNK : (u + 1) * CHUNK, :])
            return 0

        lax.fori_loop(1, windows_of(meta_ref, low_at, c, window), more, 0)


def over_chunks(first, end, visit):
    def step(i, _):
        visit(first + i * UNROLL)
        return 0

    lax.fori_loop(0, pl.cdiv(end - first, UNROLL), step, 0)


def near_forward_kernel(
    window, meta_ref, every_ref, keys_ref, table_ref, sum_hbm, deg_hbm, sum_ref, deg_ref, values_ref, sem
):
    nodes = 2 * sum_ref.shape[0]
    deg_ref[...] = jnp.zeros_like(deg_ref)
    sum_ref[...] = jnp.zeros_like(sum_ref)

    def degrees(c, _):
        key = join([every_ref[pl.ds(c * DEGREE_LINES + u, 1), :] for u in range(DEGREE_LINES)])
        dst = key & (nodes - 1)
        high = jnp.where(key < DEAD, dst >> 7, deg_ref.shape[0])
        deg_ref[...] += dot_nt(
            onehot_of_rows(high, deg_ref.shape[0]), onehot_of_rows(dst & 127, 128)
        )
        return 0

    lax.fori_loop(0, every_ref.shape[0] // DEGREE_LINES, degrees, 0)
    end = pl.cdiv(meta_ref[COUNTS, 0], CHUNK)
    over_chunks(
        0,
        end,
        lambda c: gather_add(
            c, end, 0, window, NEAR_LOW, meta_ref, keys_ref, table_ref, sum_ref, values_ref
        ),
    )
    copy_now(sum_ref, sum_hbm, sem)
    copy_now(deg_ref, deg_hbm, sem)


def near_forward(meta, every, keys, table, nodes, window=768):
    width = table.shape[1]
    shapes = [(nodes // 2, 2 * width), (16, 128)]
    return pl.pallas_call(
        functools.partial(near_forward_kernel, min(window, table.shape[0])),
        in_specs=[sspec(), vspec(), vspec(), vspec()],
        out_specs=[hbm_spec(), hbm_spec()],
        out_shape=[pltpu.HBM(shape, F32) for shape in shapes],
        scratch_shapes=[VMEM(shape, F32) for shape in shapes]
        + [VMEM((UNROLL * CHUNK, width), F32), pltpu.SemaphoreType.DMA],
        compiler_params=params(),
        name="near_forward",
    )(meta, every, keys, table)


def far_forward_kernel(
    offset, window, meta_ref, keys_ref, table_ref, base_hbm, sum_ref, values_ref, base_ref, sem
):
    base_copy = pltpu.make_async_copy(base_hbm, base_ref, sem)
    base_copy.start()
    sum_ref[...] = jnp.zeros_like(sum_ref)
    end = pl.cdiv(meta_ref[COUNTS, 1], CHUNK)
    over_chunks(
        meta_ref[COUNTS, 0] // CHUNK,
        end,
        lambda c: gather_add(
            c, end, offset, window, FAR_LOW, meta_ref, keys_ref, table_ref, sum_ref, values_ref
        ),
    )
    base_copy.wait()
    sum_ref[...] += base_ref[...]


def far_forward(meta, keys, table, base, offset, window=1280):
    return pl.pallas_call(
        functools.partial(far_forward_kernel, offset, min(window, table.shape[0])),
        in_specs=[sspec(), vspec(), vspec(), hbm_spec()],
        out_specs=vspec(),
        out_shape=jax.ShapeDtypeStruct(base.shape, F32),
        scratch_shapes=[
            VMEM((UNROLL * CHUNK, table.shape[1]), F32),
            VMEM(base.shape, F32),
            pltpu.SemaphoreType.DMA,
        ],
        compiler_params=params(),
        name="far_forward",
    )(meta, keys, table, in_hbm(base))


def dense_kernel(
    half_ref,
    mine_ref,
    other_ref,
    deg_ref,
    feat_ref,
    cot_ref,
    w_self_ref,
    w_neigh_ref,
    bias_ref,
    out_ref,
    grad_sum_ref,
    pre_ref,
    grad_w_ref,
    left_ref,
):
    nodes = feat_ref.shape[0]
    grad_bias = jnp.zeros((8, 128), F32)
    for at in range(0, nodes, 128):
        span = pl.ds(at, 128)
        h = at // 128
        divisor = jnp.maximum(columns_of(deg_ref[h : h + 1, :]), 1.0)
        feats = feat_ref[span, :]
        place = (pl.ds(at % (nodes // 2), 128), pl.ds(at // (nodes // 2) * 128, 128))
        aggregate = ((mine_ref[place] + other_ref[place]) / divisor).astype(BF16)
        preact = dot(feats, w_self_ref[...]) + dot(aggregate, w_neigh_ref[...]) + bias_ref[...]
        sig = jax.nn.sigmoid(preact)
        out_ref[span, :] = (preact * sig).astype(BF16)
        slope = sig * (1.0 + preact * (1.0 - sig))
        grad_pre = (cot_ref[span, :].astype(F32) * slope).astype(BF16)
        pre_ref[span, :] = grad_pre
        grad_sum_ref[place] = (dot_nt(grad_pre, w_neigh_ref[...]) / divisor).astype(BF16)
        left_ref[span, :] = jnp.where(half_ref[0] == 0, feats.astype(F32), aggregate.astype(F32)).astype(BF16)
        wide = grad_pre.astype(F32)
        for r in range(0, 128, 8):
            grad_bias = grad_bias + wide[r : r + 8]
    grad_w_ref[:128, :] = dot_tn(left_ref[...], pre_ref[...])
    grad_w_ref[128:, :] = jnp.broadcast_to(
        jnp.sum(grad_bias, axis=0, keepdims=True), (grad_w_ref.shape[0] - 128, 128)
    )


def dense(half, mine, other, deg, feats, cot, w_self, w_neigh, bias):
    nodes, width = feats.shape
    outs = [
        jax.ShapeDtypeStruct((nodes, width), BF16),
        jax.ShapeDtypeStruct((nodes // 2, 2 * width), BF16),
        jax.ShapeDtypeStruct((nodes, width), BF16),
        jax.ShapeDtypeStruct((192, width), F32),
    ]
    return pl.pallas_call(
        dense_kernel,
        grid=(1,),
        in_specs=[sspec()] + [whole(x) for x in (mine, other, deg, feats, cot, w_self, w_neigh, bias)],
        out_specs=[whole(x) for x in outs],
        out_shape=outs,
        scratch_shapes=[VMEM((nodes, width), BF16)],
        compiler_params=params(),
        name="dense_part",
    )(half, mine, other, in_hbm(deg), in_hbm(feats), in_hbm(cot), in_hbm(w_self), in_hbm(w_neigh), in_hbm(bias))


def far_backward_kernel(offset, window, meta_ref, keys_ref, grad_ref, out_ref, acc_ref, values_ref):
    rows = acc_ref.shape[0]
    block = out_ref.shape[0]

    @pl.when(pl.program_id(0) == 0)
    def _():
        def clear(b, _):
            span = pl.ds(pl.multiple_of(b * block, block), block)
            acc_ref[span, :] = jnp.zeros((block, acc_ref.shape[1]), F32)
            return 0

        lax.fori_loop(0, rows // block, clear, 0)
        end = pl.cdiv(meta_ref[COUNTS, 1], CHUNK)
        over_chunks(
            meta_ref[COUNTS, 0] // CHUNK,
            end,
            lambda c: spread_add(
                c, end, offset, window, FAR_LOW, meta_ref, keys_ref, grad_ref, acc_ref, values_ref
            ),
        )

    at = pl.multiple_of(pl.program_id(0) * block, block)
    out_ref[...] = acc_ref[pl.ds(at, block), :].astype(BF16)


def far_backward(meta, keys, grad_sum, offset, rows, window=1280):
    width = grad_sum.shape[1] // 2
    block = min(2048, rows)
    return pl.pallas_call(
        functools.partial(far_backward_kernel, offset, min(window, rows)),
        grid=(rows // block,),
        in_specs=[
            sspec(),
            pl.BlockSpec(keys.shape, lambda i: (0, 0)),
            pl.BlockSpec(grad_sum.shape, lambda i: (0, 0)),
        ],
        out_specs=pl.BlockSpec((block, width), lambda i: (i, 0)),
        out_shape=pltpu.HBM((rows, width), BF16),
        scratch_shapes=[VMEM((rows, width), F32), VMEM((UNROLL * CHUNK, width), BF16)],
        compiler_params=params(),
        name="far_backward",
    )(meta, keys, grad_sum)


def near_backward_kernel(
    window, half_ref, meta_ref, keys_ref, grad_ref, pre_ref, w_self_ref, out_ref, values_ref
):
    own_rows = pre_ref.shape[0] // 2
    mine = pl.ds(pl.multiple_of(half_ref[0] * own_rows, own_rows), own_rows)
    out_ref[:own_rows, :] = dot_nt(pre_ref[mine, :], w_self_ref[...])
    out_ref[own_rows:, :] = jnp.zeros((out_ref.shape[0] - own_rows, out_ref.shape[1]), F32)
    end = pl.cdiv(meta_ref[COUNTS, 0], CHUNK)
    over_chunks(
        0,
        end,
        lambda c: spread_add(
            c, end, 0, window, NEAR_LOW, meta_ref, keys_ref, grad_ref, out_ref, values_ref
        ),
    )


def near_backward(half, meta, keys, grad_sum, grad_pre, w_self, rows, window=768):
    width = grad_sum.shape[1] // 2
    return pl.pallas_call(
        functools.partial(near_backward_kernel, min(window, rows)),
        in_specs=[sspec(), sspec()] + [vspec()] * 4,
        out_specs=vspec(),
        out_shape=jax.ShapeDtypeStruct((rows, width), F32),
        scratch_shapes=[VMEM((UNROLL * CHUNK, width), BF16)],
        compiler_params=params(),
        name="near_backward",
    )(half, meta, keys, grad_sum, grad_pre, w_self)


def returned_kernel(
    peers_step, half_ref, idx_ref, back_ref, near_ref, part_hbm, part_ref, acc_ref, sem
):
    nodes = part_ref.shape[0]
    own_rows = nodes // 2
    peers, slots, width = back_ref.shape
    lines = peers_step * slots // 128
    acc_ref[...] = jnp.zeros_like(acc_ref)

    def step(s, _):
        row = join([idx_ref[pl.ds(s * lines + k, 1), :] for k in range(lines)])
        rows = back_ref[pl.ds(s * peers_step, peers_step), :, :].reshape(peers_step * slots, width)
        acc_ref[...] += spread(row, columns_of(row), rows, own_rows)
        return 0

    lax.fori_loop(0, peers // peers_step, step, 0)
    part_ref[:own_rows, :] = acc_ref[:, :width]
    part_ref[own_rows:, :] = acc_ref[:, width:]
    own_span = pl.ds(pl.multiple_of(half_ref[0] * own_rows, own_rows), own_rows)
    part_ref[own_span, :] += near_ref[:own_rows, :]
    copy_now(part_ref, part_hbm, sem)


def returned_sum(half, idx, back, near, nodes):
    width = back.shape[2]
    return pl.pallas_call(
        functools.partial(returned_kernel, min(32, back.shape[0])),
        in_specs=[sspec(), vspec(), vspec(), vspec()],
        out_specs=hbm_spec(),
        out_shape=pltpu.HBM((nodes, width), F32),
        scratch_shapes=[
            VMEM((nodes, width), F32),
            VMEM((nodes // 2, 2 * width), F32),
            pltpu.SemaphoreType.DMA,
        ],
        compiler_params=params(),
        name="returned_sum",
    )(half, idx, back, near)


def finish_kernel(hubs, both_ref, hubs_ref, self_ref, neigh_ref, bias_ref):
    width = both_ref.shape[2]
    places = both_ref.shape[0]
    share = (both_ref.shape[1] - hubs) // 2
    hubs_ref[...] = pair_sum([both_ref[j, :hubs, :] for j in range(places)])
    for row in range(0, width, 8):
        j, at = row // share, hubs + row % share
        self_ref[row : row + 8, :] = both_ref[j, at : at + 8, :]
        neigh_ref[row : row + 8, :] = both_ref[j, at + share : at + share + 8, :]
    at = hubs + width % share
    bias_ref[...] = both_ref[width // share, at : at + 1, :]


def finish(both, hubs):
    width = both.shape[2]
    outs = [
        jax.ShapeDtypeStruct(shape, F32)
        for shape in ((hubs, width), (width, width), (width, width), (1, width))
    ]
    return pl.pallas_call(
        functools.partial(finish_kernel, hubs),
        in_specs=[vspec()],
        out_specs=[vspec()] * 4,
        out_shape=outs,
        compiler_params=params(),
        name="finish",
    )(both)


def torus_of(size):
    side = 4 if size >= 64 else 2
    return side, size // (side * side), side


def groups_of(size, axis):
    sizes = torus_of(size)
    ids = np.arange(size).reshape(sizes)
    return np.moveaxis(ids, axis, -1).reshape(-1, sizes[axis]).tolist()


X_AXIS, Z_AXIS, Y_AXIS = 0, 1, 2


def exchange(blocks, axis, size):
    return lax.all_to_all(
        blocks, "dom", 0, 0, axis_index_groups=groups_of(size, axis), tiled=True
    )


def partners(size, axis):
    sizes = torus_of(size)
    step, count = {X_AXIS: sizes[1] * sizes[2], Z_AXIS: sizes[2], Y_AXIS: 1}[axis], sizes[axis]
    return [[(i, i ^ (step * j)) for i in range(size)] for j in range(1, count)]


def swap_blocks(blocks, axis, size):
    return [blocks[0]] + [
        lax.ppermute(block, "dom", pairs) for block, pairs in zip(blocks[1:], partners(size, axis))
    ]


def pair_sum(parts):
    while len(parts) > 1:
        parts = [parts[i] + parts[i + 1] for i in range(0, len(parts), 2)]
    return parts[0]


def split_exactly(value):
    high = lax.reduce_precision(value, 8, 7)
    middle = lax.reduce_precision(value - high, 8, 7)
    return [part.astype(BF16) for part in (high, middle, value - high - middle)]


def after(value, *earlier):
    return lax.optimization_barrier((value,) + earlier)[0]


def body(
    node_feats,
    hub_feats,
    w_self,
    w_neigh,
    bias,
    cotangent,
    send_count,
    send_rows,
    edge_src,
    edge_dst,
    edge_count,
):
    num_dom = lax.axis_size("dom")
    half = lax.axis_index("edge")
    nodes, width = node_feats.shape
    block_rows = send_rows.shape[2]
    hubs = hub_feats.shape[0]
    slots, half_hubs, own_rows = block_rows // 2, hubs // 2, nodes // 2
    half_scalar = half.astype(jnp.int32).reshape(1)
    xs, zs, ys = torus_of(num_dom)
    hub_rows = num_dom * half_hubs
    near_rows, far_rows = own_rows + hub_rows, num_dom * slots

    hub_z = exchange(jnp.broadcast_to(hub_feats[None], (zs,) + hub_feats.shape), Z_AXIS, num_dom)

    me = lax.axis_index("dom")
    counts_row = jnp.pad(send_count, ((0, 0), (0, -num_dom % 128)))
    flip = ((half ^ me) & 1).astype(jnp.int32).reshape(1)
    out_rows, idx = outgoing(flip, counts_row, send_rows[0], node_feats)
    out_rows, hub_z = lax.optimization_barrier((out_rows, hub_z))
    table = lax.all_to_all(out_rows, "dom", split_axis=0, concat_axis=0, tiled=True)
    hub_z = lax.dynamic_slice_in_dim(hub_z, half * half_hubs, half_hubs, 1)
    hub_z = hub_z.reshape(zs * half_hubs, width)
    hub_x = jnp.concatenate(swap_blocks([hub_z] * xs, X_AXIS, num_dom))
    hub_y = jnp.concatenate(swap_blocks([hub_x] * ys, Y_AXIS, num_dom))
    own_half = lax.dynamic_slice_in_dim(node_feats, half * own_rows, own_rows, 0)
    near_table = jnp.concatenate([own_half, hub_y.reshape(hub_rows, width)])

    src = edge_src.reshape(-1)
    dst = edge_dst.reshape(-1)
    edges = src.shape[0]
    live = jnp.arange(edges, dtype=jnp.int32) < edge_count.reshape(())
    slot = src - nodes
    hub = slot - num_dom * block_rows
    is_own, is_hub = src < nodes, hub >= 0
    master = hub // hubs
    far_y, far_x = (master ^ me) & (ys - 1), (master ^ me) // (ys * zs)
    master_place = (far_y * xs + far_x) * zs + (master // ys) % zs
    row = jnp.where(
        is_own,
        src % own_rows,
        jnp.where(
            is_hub,
            own_rows + master_place * half_hubs + hub % half_hubs,
            near_rows + slot // block_rows * slots + slot % slots,
        ),
    )
    slot_side = (slot // slots ^ slot // block_rows ^ me) & 1
    side = jnp.where(is_own, src // own_rows, jnp.where(is_hub, (hub % hubs) // half_hubs, slot_side))
    key = (side << HALF_BIT) + (row << DST_BITS) + dst
    key = after(jnp.where(live, key, DEAD), out_rows)
    key_other = lax.ppermute(key, "edge", SWAP)
    every = jnp.concatenate([key, key_other])
    mine = jnp.where((every >> HALF_BIT) == half, every & ((1 << HALF_BIT) - 1), PAD)
    keys = lax.sort(mine).reshape(-1, CHUNK)
    every = every.reshape(-1, CHUNK)
    near_edge = keys < (near_rows << DST_BITS)
    live_edge = keys < PAD
    counts = [jnp.sum(edge.astype(jnp.int32)) for edge in (near_edge, live_edge)]
    near_low = jnp.minimum(keys[:, 0] >> DST_BITS, near_rows - 1)
    near_high = jnp.max(jnp.where(near_edge, keys, 0), axis=1) >> DST_BITS
    far_low = jnp.min(jnp.where(near_edge, PAD, keys), axis=1) >> DST_BITS
    far_low = jnp.minimum(far_low - near_rows, far_rows - 1)
    far_high = jnp.max(jnp.where(live_edge, keys, 0), axis=1) >> DST_BITS
    far_high = jnp.maximum(far_high - near_rows, 0)

    lines = keys.shape[0]
    counts = jnp.where(jnp.arange(lines) == 0, counts[0], counts[1])
    meta = jnp.stack([near_low, near_high, far_low, far_high, counts])

    near_sum, degree = near_forward(meta, every, keys, near_table, nodes)
    neigh = far_forward(meta, keys, table.reshape(far_rows, width), near_sum, near_rows)
    neigh_other = lax.ppermute(neigh, "edge", SWAP)
    layer_out, grad_sum, grad_pre, grad_w = dense(
        half_scalar,
        neigh,
        neigh_other,
        degree,
        node_feats,
        cotangent,
        w_self,
        w_neigh,
        bias.reshape(1, width),
    )
    share = grad_w.shape[0] // zs
    grad_w = exchange(grad_w.reshape(zs, share, width), Z_AXIS, num_dom)
    row_grads = far_backward(meta, keys, grad_sum, near_rows, far_rows)
    row_grads, grad_w = lax.optimization_barrier((row_grads, grad_w))
    back = lax.all_to_all(
        row_grads.reshape(num_dom, slots, width), "dom", split_axis=0, concat_axis=0, tiled=True
    )
    near_grads = near_backward(
        half_scalar, meta, after(keys, row_grads), grad_sum, grad_pre, w_self, near_rows
    )

    grad_w = jnp.sum(grad_w, axis=0)
    blocks = jnp.split(near_grads[own_rows:].astype(BF16), ys)
    kept = blocks[0].shape[0]
    pieces = split_exactly(grad_w)
    both = swap_blocks([jnp.concatenate([block] + pieces) for block in blocks], Y_AXIS, num_dom)
    both = [part.astype(F32) for part in both]
    hub_part = pair_sum([part[:kept] for part in both])
    grad_w = pair_sum(
        [part[kept : kept + share] + (part[kept + share : -share] + part[-share:]) for part in both]
    )
    blocks = jnp.split(hub_part, xs)
    kept = blocks[0].shape[0]
    both = pair_sum(
        swap_blocks([jnp.concatenate([block, grad_w]) for block in blocks], X_AXIS, num_dom)
    )
    other = lax.ppermute(both, "edge", SWAP)
    first = jnp.where(half == 0, both, other)
    second = jnp.where(half == 0, other, both)
    shares = jnp.concatenate([first[kept:], second[kept:]])
    both = jnp.concatenate(
        [
            first[:kept].reshape(zs, half_hubs, width),
            second[:kept].reshape(zs, half_hubs, width),
            jnp.broadcast_to(shares[None], (zs,) + shares.shape),
        ],
        axis=1,
    )
    both = exchange(after(both, back), Z_AXIS, num_dom)
    part = returned_sum(half_scalar, idx, back, near_grads, nodes)
    part_other = lax.ppermute(part, "edge", SWAP)
    grad_hubs, grad_self, grad_neigh, grad_bias = finish(both, hubs)
    grad_feats = part + after(part_other, grad_hubs)
    return (layer_out, grad_feats, grad_hubs, grad_self, grad_neigh, grad_bias.reshape(width))


def solution(mesh):
    placed = (
        P("dom", None),
        P("dom", None),
        P(),
        P(),
        P(),
        P("dom", None),
        P("dom", None),
        P("dom", None, None),
        P("dom", "edge", None),
        P("dom", "edge", None),
        P("dom", "edge"),
    )
    return jax.shard_map(
        body,
        mesh=mesh,
        in_specs=placed,
        out_specs=(P("dom", None), P("dom", None), P("dom", None), P(), P(), P()),
        check_vma=False,
    )
```

```python
import functools

import jax
import jax.numpy as jnp
import numpy as np
from jax import lax
from jax.experimental import pallas as pl
from jax.experimental.pallas import tpu as pltpu
from jax.sharding import PartitionSpec as P

F32 = jnp.float32
BF16 = jnp.bfloat16
I16 = jnp.int16
VMEM = pltpu.VMEM
SMEM = pltpu.SMEM
SWAP = [(0, 1), (1, 0)]
CHUNK = 256
UNROLL = 6
DEGREE_LINES = 8
DST_BITS = 10
PAD = 1 << 30
DEAD = 1 << 26
HALF_BIT = 24
META = NEAR_LOW, NEAR_HIGH, FAR_LOW, FAR_HIGH, COUNTS = 0, 1, 2, 3, 4


def params(mib=40):
    return pltpu.CompilerParams(vmem_limit_bytes=mib * 1024 * 1024)


def vspec():
    return pl.BlockSpec(memory_space=VMEM)


def hbm_spec():
    return pl.BlockSpec(memory_space=pltpu.HBM)


def copy_now(source, target, sem):
    copy = pltpu.make_async_copy(source, target, sem)
    copy.start()
    copy.wait()


def whole(value):
    return pl.BlockSpec(value.shape, lambda i: (0,) * len(value.shape))


def sspec():
    return pl.BlockSpec(memory_space=SMEM)


def columns_of(row):
    parts = []
    for at in range(0, row.shape[1], 128):
        parts.append(jnp.broadcast_to(row[:, at : at + 128], (128, 128)).T)
    return jnp.concatenate(parts, axis=0)


def onehot_of_columns(col, width):
    lane = lax.broadcasted_iota(jnp.int32, col.shape, 1).astype(I16)
    col = col.astype(I16)
    one, zero = jnp.ones((), BF16), jnp.zeros((), BF16)
    parts = [jnp.where(col == lane + I16(at), one, zero) for at in range(0, width, 128)]
    return parts[0] if len(parts) == 1 else jnp.concatenate(parts, axis=1)


def onehot_of_rows(row, height):
    sub = lax.broadcasted_iota(jnp.int32, (height, row.shape[1]), 0).astype(I16)
    return jnp.where(sub == row.astype(I16), jnp.ones((), BF16), jnp.zeros((), BF16))


def in_hbm(value):
    return pltpu.with_memory_space_constraint(value, pltpu.HBM)


def dot(a, b):
    return jnp.dot(a, b, preferred_element_type=F32)


def dot_nt(a, b):
    return lax.dot_general(a, b, (((1,), (1,)), ((), ())), preferred_element_type=F32)


def dot_tn(a, b):
    return lax.dot_general(a, b, (((0,), (0,)), ((), ())), preferred_element_type=F32)


def pick(col, wide):
    rows = wide.shape[0]
    both = dot(onehot_of_columns(jnp.where(col >= rows, col - rows, col), rows), wide)
    return jnp.where(col >= rows, both[:, 128:], both[:, :128])


def spread(row, col, values, rows):
    left = col.astype(I16) < I16(rows)
    zero = jnp.zeros((), BF16)
    pair = jnp.concatenate([jnp.where(left, values, zero), jnp.where(left, zero, values)], axis=1)
    return dot(onehot_of_rows(jnp.where(row >= rows, row - rows, row), rows), pair)


def join(refs_at):
    return jnp.concatenate(refs_at, axis=1)


def outgoing_kernel(flip_ref, count_ref, rows_ref, feat_ref, out_ref, idx_ref, wide_ref, all_ref):
    step = pl.program_id(0)
    peers, slots, width = out_ref.shape
    nodes = feat_ref.shape[0]
    lines = peers * slots // 128

    @pl.when(step == 0)
    def _():
        wide_ref[:, :width] = feat_ref[: nodes // 2, :]
        wide_ref[:, width:] = feat_ref[nodes // 2 :, :]
        count = columns_of(count_ref[...])[: rows_ref.shape[0], :]
        lane = lax.broadcasted_iota(jnp.int32, rows_ref.shape, 1)
        all_ref[...] = jnp.where(lane < count, rows_ref[...], -1)
        pairs = rows_ref.shape[0] // 2
        even = all_ref[pl.ds(0, pairs, stride=2), :]
        odd = all_ref[pl.ds(1, pairs, stride=2), :]
        low = lax.broadcasted_iota(jnp.int32, even.shape, 1) < slots
        crossed = pltpu.roll(jnp.where(low, odd, even), slots, 1)
        idx_ref[...] = jnp.where(flip_ref[0] == 0, jnp.where(low, even, odd), crossed)

    row = join([idx_ref[pl.ds(step * lines + k, 1), :] for k in range(lines)])
    out_ref[...] = pick(columns_of(row), wide_ref[...]).astype(BF16).reshape(peers, slots, width)


def outgoing(flip, count, rows, feats, step_peers=32):
    peers, slots = rows.shape[0], rows.shape[1] // 2
    nodes, width = feats.shape
    step_peers = min(step_peers, peers)
    lines = peers * slots // 128
    return pl.pallas_call(
        outgoing_kernel,
        grid=(peers // step_peers,),
        in_specs=[
            sspec(),
            pl.BlockSpec(count.shape, lambda i: (0, 0)),
            pl.BlockSpec(rows.shape, lambda i: (0, 0)),
            pl.BlockSpec(feats.shape, lambda i: (0, 0)),
        ],
        out_specs=[
            pl.BlockSpec((step_peers, slots, width), lambda i: (i, 0, 0)),
            pl.BlockSpec((lines, 128), lambda i: (0, 0)),
        ],
        out_shape=[
            pltpu.HBM((peers, slots, width), BF16),
            jax.ShapeDtypeStruct((lines, 128), jnp.int32),
        ],
        scratch_shapes=[VMEM((nodes // 2, 2 * width), BF16), VMEM(rows.shape, jnp.int32)],
        compiler_params=params(),
        name="outgoing_rows",
    )(flip, in_hbm(count), in_hbm(rows), in_hbm(feats))


def relative(row, base, start, window):
    return jnp.where((row >= base) & (row < start + window), row - start, -1)


def window_of(meta_ref, low_at, c, w, rows, window):
    base = meta_ref[low_at, c] // 128 * 128 + w * window
    return base, pl.multiple_of(jnp.minimum(base, rows - window), 128)


def windows_of(meta_ref, low_at, c, window):
    return (meta_ref[low_at + 1, c] - meta_ref[low_at, c] // 128 * 128) // window + 1


def keys_of(keys_ref, c, end):
    at = jnp.minimum(c, keys_ref.shape[0] - 1)
    return at, jnp.where(c < end, keys_ref[pl.ds(at, 1), :], PAD)


def gather_add(first, end, offset, window, low_at, meta_ref, keys_ref, table_ref, sum_ref, values_ref):
    half_nodes = sum_ref.shape[0]
    rows = table_ref.shape[0]
    half = window // 2

    def picked(c, w, col):
        base, start = window_of(meta_ref, low_at, c, w, rows, window)
        wide = join([table_ref[pl.ds(start, half), :], table_ref[pl.ds(start + half, half), :]])
        return pick(relative((col >> DST_BITS) - offset, base, start, window), wide)

    keys, cols = [], []
    for u in range(UNROLL):
        c, key = keys_of(keys_ref, first + u, end)
        keys.append(key)
        cols.append(columns_of(key))
        values_ref[u * CHUNK : (u + 1) * CHUNK, :] = picked(c, 0, cols[u])
    for u in range(UNROLL):
        c, key = keys_of(keys_ref, first + u, end)

        def more(w, _, c=c, key=key, u=u):
            values_ref[u * CHUNK : (u + 1) * CHUNK, :] += picked(c, w, columns_of(key))
            return 0

        lax.fori_loop(1, windows_of(meta_ref, low_at, c, window), more, 0)
    nodes = 2 * half_nodes
    sum_ref[...] += spread(
        join(keys) & (nodes - 1),
        jnp.concatenate(cols, axis=0) & (nodes - 1),
        values_ref[...].astype(BF16),
        half_nodes,
    )


def spread_add(first, end, offset, window, low_at, meta_ref, keys_ref, grad_ref, acc_ref, values_ref):
    nodes = 2 * grad_ref.shape[0]
    rows = acc_ref.shape[0]
    half = window // 2

    def add(c, w, key, col, values):
        base, start = window_of(meta_ref, low_at, c, w, rows, window)
        row, col = (
            relative((k >> DST_BITS) - offset, base, start, window) for k in (key, col)
        )
        both = spread(row, col, values, half)
        acc_ref[pl.ds(start, half), :] += both[:, :128]
        acc_ref[pl.ds(start + half, half), :] += both[:, 128:]

    keys = [keys_of(keys_ref, first + u, end) for u in range(UNROLL)]
    cols = [columns_of(key) for _, key in keys]
    values = pick(jnp.concatenate(cols, axis=0) & (nodes - 1), grad_ref[...]).astype(BF16)
    values_ref[...] = values
    for u, (c, key) in enumerate(keys):
        add(c, 0, key, cols[u], values[u * CHUNK : (u + 1) * CHUNK])
    for u in range(UNROLL):
        c, key = keys_of(keys_ref, first + u, end)

        def more(w, _, c=c, key=key, u=u):
            add(c, w, key, columns_of(key), values_ref[u * CHUNK : (u + 1) * CHUNK, :])
            return 0

        lax.fori_loop(1, windows_of(meta_ref, low_at, c, window), more, 0)


def over_chunks(first, end, visit):
    def step(i, _):
        visit(first + i * UNROLL)
        return 0

    lax.fori_loop(0, pl.cdiv(end - first, UNROLL), step, 0)


def near_forward_kernel(
    window, meta_ref, every_ref, keys_ref, table_ref, sum_hbm, deg_hbm, sum_ref, deg_ref, values_ref, sem
):
    nodes = 2 * sum_ref.shape[0]
    deg_ref[...] = jnp.zeros_like(deg_ref)
    sum_ref[...] = jnp.zeros_like(sum_ref)

    def degrees(c, _):
        key = join([every_ref[pl.ds(c * DEGREE_LINES + u, 1), :] for u in range(DEGREE_LINES)])
        dst = key & (nodes - 1)
        high = jnp.where(key < DEAD, dst >> 7, deg_ref.shape[0])
        deg_ref[...] += dot_nt(
            onehot_of_rows(high, deg_ref.shape[0]), onehot_of_rows(dst & 127, 128)
        )
        return 0

    lax.fori_loop(0, every_ref.shape[0] // DEGREE_LINES, degrees, 0)
    end = pl.cdiv(meta_ref[COUNTS, 0], CHUNK)
    over_chunks(
        0,
        end,
        lambda c: gather_add(
            c, end, 0, window, NEAR_LOW, meta_ref, keys_ref, table_ref, sum_ref, values_ref
        ),
    )
    copy_now(sum_ref, sum_hbm, sem)
    copy_now(deg_ref, deg_hbm, sem)


def near_forward(meta, every, keys, table, nodes, window=768):
    width = table.shape[1]
    shapes = [(nodes // 2, 2 * width), (16, 128)]
    return pl.pallas_call(
        functools.partial(near_forward_kernel, min(window, table.shape[0])),
        in_specs=[sspec(), vspec(), vspec(), vspec()],
        out_specs=[hbm_spec(), hbm_spec()],
        out_shape=[pltpu.HBM(shape, F32) for shape in shapes],
        scratch_shapes=[VMEM(shape, F32) for shape in shapes]
        + [VMEM((UNROLL * CHUNK, width), F32), pltpu.SemaphoreType.DMA],
        compiler_params=params(),
        name="near_forward",
    )(meta, every, keys, table)


def far_forward_kernel(
    offset, window, meta_ref, keys_ref, table_ref, base_hbm, sum_ref, values_ref, base_ref, sem
):
    base_copy = pltpu.make_async_copy(base_hbm, base_ref, sem)
    base_copy.start()
    sum_ref[...] = jnp.zeros_like(sum_ref)
    end = pl.cdiv(meta_ref[COUNTS, 1], CHUNK)
    over_chunks(
        meta_ref[COUNTS, 0] // CHUNK,
        end,
        lambda c: gather_add(
            c, end, offset, window, FAR_LOW, meta_ref, keys_ref, table_ref, sum_ref, values_ref
        ),
    )
    base_copy.wait()
    sum_ref[...] += base_ref[...]


def far_forward(meta, keys, table, base, offset, window=1280):
    return pl.pallas_call(
        functools.partial(far_forward_kernel, offset, min(window, table.shape[0])),
        in_specs=[sspec(), vspec(), vspec(), hbm_spec()],
        out_specs=vspec(),
        out_shape=jax.ShapeDtypeStruct(base.shape, F32),
        scratch_shapes=[
            VMEM((UNROLL * CHUNK, table.shape[1]), F32),
            VMEM(base.shape, F32),
            pltpu.SemaphoreType.DMA,
        ],
        compiler_params=params(),
        name="far_forward",
    )(meta, keys, table, in_hbm(base))


def dense_kernel(
    half_ref,
    mine_ref,
    other_ref,
    deg_ref,
    feat_ref,
    cot_ref,
    w_self_ref,
    w_neigh_ref,
    bias_ref,
    out_ref,
    grad_sum_ref,
    pre_ref,
    grad_w_ref,
    left_ref,
):
    nodes = feat_ref.shape[0]
    grad_bias = jnp.zeros((8, 128), F32)
    for at in range(0, nodes, 128):
        span = pl.ds(at, 128)
        h = at // 128
        divisor = jnp.maximum(columns_of(deg_ref[h : h + 1, :]), 1.0)
        feats = feat_ref[span, :]
        place = (pl.ds(at % (nodes // 2), 128), pl.ds(at // (nodes // 2) * 128, 128))
        aggregate = ((mine_ref[place] + other_ref[place]) / divisor).astype(BF16)
        preact = dot(feats, w_self_ref[...]) + dot(aggregate, w_neigh_ref[...]) + bias_ref[...]
        sig = jax.nn.sigmoid(preact)
        out_ref[span, :] = (preact * sig).astype(BF16)
        slope = sig * (1.0 + preact * (1.0 - sig))
        grad_pre = (cot_ref[span, :].astype(F32) * slope).astype(BF16)
        pre_ref[span, :] = grad_pre
        grad_sum_ref[place] = (dot_nt(grad_pre, w_neigh_ref[...]) / divisor).astype(BF16)
        left_ref[span, :] = jnp.where(half_ref[0] == 0, feats.astype(F32), aggregate.astype(F32)).astype(BF16)
        wide = grad_pre.astype(F32)
        for r in range(0, 128, 8):
            grad_bias = grad_bias + wide[r : r + 8]
    grad_w_ref[:128, :] = dot_tn(left_ref[...], pre_ref[...])
    grad_w_ref[128:, :] = jnp.broadcast_to(
        jnp.sum(grad_bias, axis=0, keepdims=True), (grad_w_ref.shape[0] - 128, 128)
    )


def dense(half, mine, other, deg, feats, cot, w_self, w_neigh, bias):
    nodes, width = feats.shape
    outs = [
        jax.ShapeDtypeStruct((nodes, width), BF16),
        jax.ShapeDtypeStruct((nodes // 2, 2 * width), BF16),
        jax.ShapeDtypeStruct((nodes, width), BF16),
        jax.ShapeDtypeStruct((192, width), F32),
    ]
    return pl.pallas_call(
        dense_kernel,
        grid=(1,),
        in_specs=[sspec()] + [whole(x) for x in (mine, other, deg, feats, cot, w_self, w_neigh, bias)],
        out_specs=[whole(x) for x in outs],
        out_shape=outs,
        scratch_shapes=[VMEM((nodes, width), BF16)],
        compiler_params=params(),
        name="dense_part",
    )(half, mine, other, in_hbm(deg), in_hbm(feats), in_hbm(cot), in_hbm(w_self), in_hbm(w_neigh), in_hbm(bias))


def far_backward_kernel(offset, window, meta_ref, keys_ref, grad_ref, out_ref, acc_ref, values_ref):
    rows = acc_ref.shape[0]
    block = out_ref.shape[0]

    @pl.when(pl.program_id(0) == 0)
    def _():
        def clear(b, _):
            span = pl.ds(pl.multiple_of(b * block, block), block)
            acc_ref[span, :] = jnp.zeros((block, acc_ref.shape[1]), F32)
            return 0

        lax.fori_loop(0, rows // block, clear, 0)
        end = pl.cdiv(meta_ref[COUNTS, 1], CHUNK)
        over_chunks(
            meta_ref[COUNTS, 0] // CHUNK,
            end,
            lambda c: spread_add(
                c, end, offset, window, FAR_LOW, meta_ref, keys_ref, grad_ref, acc_ref, values_ref
            ),
        )

    at = pl.multiple_of(pl.program_id(0) * block, block)
    out_ref[...] = acc_ref[pl.ds(at, block), :].astype(BF16)


def far_backward(meta, keys, grad_sum, offset, rows, window=1280):
    width = grad_sum.shape[1] // 2
    block = min(4096, rows)
    return pl.pallas_call(
        functools.partial(far_backward_kernel, offset, min(window, rows)),
        grid=(rows // block,),
        in_specs=[
            sspec(),
            pl.BlockSpec(keys.shape, lambda i: (0, 0)),
            pl.BlockSpec(grad_sum.shape, lambda i: (0, 0)),
        ],
        out_specs=pl.BlockSpec((block, width), lambda i: (i, 0)),
        out_shape=pltpu.HBM((rows, width), BF16),
        scratch_shapes=[VMEM((rows, width), F32), VMEM((UNROLL * CHUNK, width), BF16)],
        compiler_params=params(),
        name="far_backward",
    )(meta, keys, grad_sum)


def near_backward_kernel(
    window, half_ref, meta_ref, keys_ref, grad_ref, pre_ref, w_self_ref, out_ref, values_ref
):
    own_rows = pre_ref.shape[0] // 2
    mine = pl.ds(pl.multiple_of(half_ref[0] * own_rows, own_rows), own_rows)
    out_ref[:own_rows, :] = dot_nt(pre_ref[mine, :], w_self_ref[...])
    out_ref[own_rows:, :] = jnp.zeros((out_ref.shape[0] - own_rows, out_ref.shape[1]), F32)
    end = pl.cdiv(meta_ref[COUNTS, 0], CHUNK)
    over_chunks(
        0,
        end,
        lambda c: spread_add(
            c, end, 0, window, NEAR_LOW, meta_ref, keys_ref, grad_ref, out_ref, values_ref
        ),
    )


def near_backward(half, meta, keys, grad_sum, grad_pre, w_self, rows, window=768):
    width = grad_sum.shape[1] // 2
    return pl.pallas_call(
        functools.partial(near_backward_kernel, min(window, rows)),
        in_specs=[sspec(), sspec()] + [vspec()] * 4,
        out_specs=vspec(),
        out_shape=jax.ShapeDtypeStruct((rows, width), F32),
        scratch_shapes=[VMEM((UNROLL * CHUNK, width), BF16)],
        compiler_params=params(),
        name="near_backward",
    )(half, meta, keys, grad_sum, grad_pre, w_self)


def returned_kernel(peers_step, half_ref, idx_ref, back_ref, near_ref, part_ref, acc_ref):
    nodes = part_ref.shape[0]
    own_rows = nodes // 2
    peers, slots, width = back_ref.shape
    lines = peers_step * slots // 128
    acc_ref[...] = jnp.zeros_like(acc_ref)

    def step(s, _):
        row = join([idx_ref[pl.ds(s * lines + k, 1), :] for k in range(lines)])
        rows = back_ref[pl.ds(s * peers_step, peers_step), :, :].reshape(peers_step * slots, width)
        acc_ref[...] += spread(row, columns_of(row), rows, own_rows)
        return 0

    lax.fori_loop(0, peers // peers_step, step, 0)
    part_ref[:own_rows, :] = acc_ref[:, :width]
    part_ref[own_rows:, :] = acc_ref[:, width:]
    own_span = pl.ds(pl.multiple_of(half_ref[0] * own_rows, own_rows), own_rows)
    part_ref[own_span, :] += near_ref[:own_rows, :]


def returned_sum(half, idx, back, near, nodes):
    width = back.shape[2]
    return pl.pallas_call(
        functools.partial(returned_kernel, min(32, back.shape[0])),
        in_specs=[sspec(), vspec(), vspec(), vspec()],
        out_specs=vspec(),
        out_shape=jax.ShapeDtypeStruct((nodes, width), F32),
        scratch_shapes=[VMEM((nodes // 2, 2 * width), F32)],
        compiler_params=params(),
        name="returned_sum",
    )(half, idx, back, near)


def finish_kernel(hubs, both_ref, hubs_ref, self_ref, neigh_ref, bias_ref):
    width = both_ref.shape[2]
    places = both_ref.shape[0]
    share = (both_ref.shape[1] - hubs) // 2
    hubs_ref[...] = pair_sum([both_ref[j, :hubs, :] for j in range(places)])
    for row in range(0, width, 8):
        j, at = row // share, hubs + row % share
        self_ref[row : row + 8, :] = both_ref[j, at : at + 8, :]
        neigh_ref[row : row + 8, :] = both_ref[j, at + share : at + share + 8, :]
    at = hubs + width % share
    bias_ref[...] = both_ref[width // share, at : at + 1, :]


def finish(both, hubs):
    width = both.shape[2]
    outs = [
        jax.ShapeDtypeStruct(shape, F32)
        for shape in ((hubs, width), (width, width), (width, width), (1, width))
    ]
    return pl.pallas_call(
        functools.partial(finish_kernel, hubs),
        in_specs=[vspec()],
        out_specs=[vspec()] * 4,
        out_shape=outs,
        compiler_params=params(),
        name="finish",
    )(both)


def torus_of(size):
    side = 4 if size >= 64 else 2
    return side, size // (side * side), side


def groups_of(size, axis):
    sizes = torus_of(size)
    ids = np.arange(size).reshape(sizes)
    return np.moveaxis(ids, axis, -1).reshape(-1, sizes[axis]).tolist()


X_AXIS, Z_AXIS, Y_AXIS = 0, 1, 2


def exchange(blocks, axis, size):
    return lax.all_to_all(
        blocks, "dom", 0, 0, axis_index_groups=groups_of(size, axis), tiled=True
    )


def partners(size, axis):
    sizes = torus_of(size)
    step, count = {X_AXIS: sizes[1] * sizes[2], Z_AXIS: sizes[2], Y_AXIS: 1}[axis], sizes[axis]
    return [[(i, i ^ (step * j)) for i in range(size)] for j in range(1, count)]


def swap_blocks(blocks, axis, size):
    return [blocks[0]] + [
        lax.ppermute(block, "dom", pairs) for block, pairs in zip(blocks[1:], partners(size, axis))
    ]


def pair_sum(parts):
    while len(parts) > 1:
        parts = [parts[i] + parts[i + 1] for i in range(0, len(parts), 2)]
    return parts[0]


def split_exactly(value):
    high = lax.reduce_precision(value, 8, 7)
    middle = lax.reduce_precision(value - high, 8, 7)
    return [part.astype(BF16) for part in (high, middle, value - high - middle)]


def after(value, *earlier):
    return lax.optimization_barrier((value,) + earlier)[0]


def body(
    node_feats,
    hub_feats,
    w_self,
    w_neigh,
    bias,
    cotangent,
    send_count,
    send_rows,
    edge_src,
    edge_dst,
    edge_count,
):
    num_dom = lax.axis_size("dom")
    half = lax.axis_index("edge")
    nodes, width = node_feats.shape
    block_rows = send_rows.shape[2]
    hubs = hub_feats.shape[0]
    slots, half_hubs, own_rows = block_rows // 2, hubs // 2, nodes // 2
    half_scalar = half.astype(jnp.int32).reshape(1)
    xs, zs, ys = torus_of(num_dom)
    hub_rows = num_dom * half_hubs
    near_rows, far_rows = own_rows + hub_rows, num_dom * slots

    hub_z = exchange(jnp.broadcast_to(hub_feats[None], (zs,) + hub_feats.shape), Z_AXIS, num_dom)

    me = lax.axis_index("dom")
    counts_row = jnp.pad(send_count, ((0, 0), (0, -num_dom % 128)))
    flip = ((half ^ me) & 1).astype(jnp.int32).reshape(1)
    out_rows, idx = outgoing(flip, counts_row, send_rows[0], node_feats)
    out_rows, hub_z = lax.optimization_barrier((out_rows, hub_z))
    table = lax.all_to_all(out_rows, "dom", split_axis=0, concat_axis=0, tiled=True)
    hub_z = lax.dynamic_slice_in_dim(hub_z, half * half_hubs, half_hubs, 1)
    hub_z = hub_z.reshape(zs * half_hubs, width)
    hub_x = jnp.concatenate(swap_blocks([hub_z] * xs, X_AXIS, num_dom))
    hub_y = jnp.concatenate(swap_blocks([hub_x] * ys, Y_AXIS, num_dom))
    own_half = lax.dynamic_slice_in_dim(node_feats, half * own_rows, own_rows, 0)
    near_table = jnp.concatenate([own_half, hub_y.reshape(hub_rows, width)])

    src = edge_src.reshape(-1)
    dst = edge_dst.reshape(-1)
    edges = src.shape[0]
    live = jnp.arange(edges, dtype=jnp.int32) < edge_count.reshape(())
    slot = src - nodes
    hub = slot - num_dom * block_rows
    is_own, is_hub = src < nodes, hub >= 0
    master = hub // hubs
    far_y, far_x = (master ^ me) & (ys - 1), (master ^ me) // (ys * zs)
    master_place = (far_y * xs + far_x) * zs + (master // ys) % zs
    row = jnp.where(
        is_own,
        src % own_rows,
        jnp.where(
            is_hub,
            own_rows + master_place * half_hubs + hub % half_hubs,
            near_rows + slot // block_rows * slots + slot % slots,
        ),
    )
    slot_side = (slot // slots ^ slot // block_rows ^ me) & 1
    side = jnp.where(is_own, src // own_rows, jnp.where(is_hub, (hub % hubs) // half_hubs, slot_side))
    key = (side << HALF_BIT) + (row << DST_BITS) + dst
    key = after(jnp.where(live, key, DEAD), out_rows)
    key_other = lax.ppermute(key, "edge", SWAP)
    every = jnp.concatenate([key, key_other])
    mine = jnp.where((every >> HALF_BIT) == half, every & ((1 << HALF_BIT) - 1), PAD)
    keys = lax.sort(mine).reshape(-1, CHUNK)
    every = every.reshape(-1, CHUNK)
    near_edge = keys < (near_rows << DST_BITS)
    live_edge = keys < PAD
    counts = [jnp.sum(edge.astype(jnp.int32)) for edge in (near_edge, live_edge)]
    near_low = jnp.minimum(keys[:, 0] >> DST_BITS, near_rows - 1)
    near_high = jnp.max(jnp.where(near_edge, keys, 0), axis=1) >> DST_BITS
    far_low = jnp.min(jnp.where(near_edge, PAD, keys), axis=1) >> DST_BITS
    far_low = jnp.minimum(far_low - near_rows, far_rows - 1)
    far_high = jnp.max(jnp.where(live_edge, keys, 0), axis=1) >> DST_BITS
    far_high = jnp.maximum(far_high - near_rows, 0)

    lines = keys.shape[0]
    counts = jnp.where(jnp.arange(lines) == 0, counts[0], counts[1])
    meta = jnp.stack([near_low, near_high, far_low, far_high, counts])

    near_sum, degree = near_forward(meta, every, keys, near_table, nodes)
    neigh = far_forward(meta, keys, table.reshape(far_rows, width), near_sum, near_rows)
    neigh_other = lax.ppermute(neigh, "edge", SWAP)
    layer_out, grad_sum, grad_pre, grad_w = dense(
        half_scalar,
        neigh,
        neigh_other,
        degree,
        node_feats,
        cotangent,
        w_self,
        w_neigh,
        bias.reshape(1, width),
    )
    share = grad_w.shape[0] // zs
    grad_w = exchange(grad_w.reshape(zs, share, width), Z_AXIS, num_dom)
    row_grads = far_backward(meta, keys, grad_sum, near_rows, far_rows)
    row_grads, grad_w = lax.optimization_barrier((row_grads, grad_w))
    back = lax.all_to_all(
        row_grads.reshape(num_dom, slots, width), "dom", split_axis=0, concat_axis=0, tiled=True
    )
    near_grads = near_backward(
        half_scalar, meta, after(keys, row_grads), grad_sum, grad_pre, w_self, near_rows
    )

    grad_w = jnp.sum(grad_w, axis=0)
    blocks = jnp.split(near_grads[own_rows:].astype(BF16), ys)
    kept = blocks[0].shape[0]
    pieces = split_exactly(grad_w)
    both = swap_blocks([jnp.concatenate([block] + pieces) for block in blocks], Y_AXIS, num_dom)
    both = [part.astype(F32) for part in both]
    hub_part = pair_sum([part[:kept] for part in both])
    grad_w = pair_sum(
        [part[kept : kept + share] + (part[kept + share : -share] + part[-share:]) for part in both]
    )
    blocks = jnp.split(hub_part, xs)
    kept = blocks[0].shape[0]
    both = pair_sum(
        swap_blocks([jnp.concatenate([block, grad_w]) for block in blocks], X_AXIS, num_dom)
    )
    other = lax.ppermute(both, "edge", SWAP)
    first = jnp.where(half == 0, both, other)
    second = jnp.where(half == 0, other, both)
    shares = jnp.concatenate([first[kept:], second[kept:]])
    both = jnp.concatenate(
        [
            first[:kept].reshape(zs, half_hubs, width),
            second[:kept].reshape(zs, half_hubs, width),
            jnp.broadcast_to(shares[None], (zs,) + shares.shape),
        ],
        axis=1,
    )
    both = exchange(after(both, back), Z_AXIS, num_dom)
    part = returned_sum(half_scalar, idx, back, near_grads, nodes)
    part_other = lax.ppermute(part, "edge", SWAP)
    grad_feats = part + part_other
    grad_hubs, grad_self, grad_neigh, grad_bias = finish(after(both, grad_feats), hubs)
    return (layer_out, grad_feats, grad_hubs, grad_self, grad_neigh, grad_bias.reshape(width))


def solution(mesh):
    placed = (
        P("dom", None),
        P("dom", None),
        P(),
        P(),
        P(),
        P("dom", None),
        P("dom", None),
        P("dom", None, None),
        P("dom", "edge", None),
        P("dom", "edge", None),
        P("dom", "edge"),
    )
    return jax.shard_map(
        body,
        mesh=mesh,
        in_specs=placed,
        out_specs=(P("dom", None), P("dom", None), P("dom", None), P(), P(), P()),
        check_vma=False,
    )
```

```python
import functools

import jax
import jax.numpy as jnp
import numpy as np
from jax import lax
from jax.experimental import pallas as pl
from jax.experimental.pallas import tpu as pltpu
from jax.sharding import PartitionSpec as P

F32 = jnp.float32
BF16 = jnp.bfloat16
I16 = jnp.int16
VMEM = pltpu.VMEM
SMEM = pltpu.SMEM
SWAP = [(0, 1), (1, 0)]
CHUNK = 256
UNROLL = 6
DEGREE_LINES = 8
DST_BITS = 10
PAD = 1 << 30
DEAD = 1 << 26
HALF_BIT = 24
META = NEAR_LOW, NEAR_HIGH, FAR_LOW, FAR_HIGH, COUNTS = 0, 1, 2, 3, 4


def params(mib=40):
    return pltpu.CompilerParams(vmem_limit_bytes=mib * 1024 * 1024)


def vspec():
    return pl.BlockSpec(memory_space=VMEM)


def hbm_spec():
    return pl.BlockSpec(memory_space=pltpu.HBM)


def copy_now(source, target, sem):
    copy = pltpu.make_async_copy(source, target, sem)
    copy.start()
    copy.wait()


def whole(value):
    return pl.BlockSpec(value.shape, lambda i: (0,) * len(value.shape))


def sspec():
    return pl.BlockSpec(memory_space=SMEM)


def columns_of(row):
    parts = []
    for at in range(0, row.shape[1], 128):
        parts.append(jnp.broadcast_to(row[:, at : at + 128], (128, 128)).T)
    return jnp.concatenate(parts, axis=0)


def onehot_of_columns(col, width):
    lane = lax.broadcasted_iota(jnp.int32, col.shape, 1).astype(I16)
    col = col.astype(I16)
    one, zero = jnp.ones((), BF16), jnp.zeros((), BF16)
    parts = [jnp.where(col == lane + I16(at), one, zero) for at in range(0, width, 128)]
    return parts[0] if len(parts) == 1 else jnp.concatenate(parts, axis=1)


def onehot_of_rows(row, height):
    sub = lax.broadcasted_iota(jnp.int32, (height, row.shape[1]), 0).astype(I16)
    return jnp.where(sub == row.astype(I16), jnp.ones((), BF16), jnp.zeros((), BF16))


def in_hbm(value):
    return pltpu.with_memory_space_constraint(value, pltpu.HBM)


def dot(a, b):
    return jnp.dot(a, b, preferred_element_type=F32)


def dot_nt(a, b):
    return lax.dot_general(a, b, (((1,), (1,)), ((), ())), preferred_element_type=F32)


def dot_tn(a, b):
    return lax.dot_general(a, b, (((0,), (0,)), ((), ())), preferred_element_type=F32)


def pick(col, wide):
    rows = wide.shape[0]
    both = dot(onehot_of_columns(jnp.where(col >= rows, col - rows, col), rows), wide)
    return jnp.where(col >= rows, both[:, 128:], both[:, :128])


def spread(row, col, values, rows):
    left = col.astype(I16) < I16(rows)
    zero = jnp.zeros((), BF16)
    pair = jnp.concatenate([jnp.where(left, values, zero), jnp.where(left, zero, values)], axis=1)
    return dot(onehot_of_rows(jnp.where(row >= rows, row - rows, row), rows), pair)


def join(refs_at):
    return jnp.concatenate(refs_at, axis=1)


def outgoing_kernel(flip_ref, count_ref, rows_ref, feat_ref, out_ref, idx_ref, wide_ref, all_ref):
    step = pl.program_id(0)
    peers, slots, width = out_ref.shape
    nodes = feat_ref.shape[0]
    lines = peers * slots // 128

    @pl.when(step == 0)
    def _():
        wide_ref[:, :width] = feat_ref[: nodes // 2, :]
        wide_ref[:, width:] = feat_ref[nodes // 2 :, :]
        count = columns_of(count_ref[...])[: rows_ref.shape[0], :]
        lane = lax.broadcasted_iota(jnp.int32, rows_ref.shape, 1)
        all_ref[...] = jnp.where(lane < count, rows_ref[...], -1)
        pairs = rows_ref.shape[0] // 2
        even = all_ref[pl.ds(0, pairs, stride=2), :]
        odd = all_ref[pl.ds(1, pairs, stride=2), :]
        low = lax.broadcasted_iota(jnp.int32, even.shape, 1) < slots
        crossed = pltpu.roll(jnp.where(low, odd, even), slots, 1)
        idx_ref[...] = jnp.where(flip_ref[0] == 0, jnp.where(low, even, odd), crossed)

    row = join([idx_ref[pl.ds(step * lines + k, 1), :] for k in range(lines)])
    out_ref[...] = pick(columns_of(row), wide_ref[...]).astype(BF16).reshape(peers, slots, width)


def outgoing(flip, count, rows, feats, step_peers=32):
    peers, slots = rows.shape[0], rows.shape[1] // 2
    nodes, width = feats.shape
    step_peers = min(step_peers, peers)
    lines = peers * slots // 128
    return pl.pallas_call(
        outgoing_kernel,
        grid=(peers // step_peers,),
        in_specs=[
            sspec(),
            pl.BlockSpec(count.shape, lambda i: (0, 0)),
            pl.BlockSpec(rows.shape, lambda i: (0, 0)),
            pl.BlockSpec(feats.shape, lambda i: (0, 0)),
        ],
        out_specs=[
            pl.BlockSpec((step_peers, slots, width), lambda i: (i, 0, 0)),
            pl.BlockSpec((lines, 128), lambda i: (0, 0)),
        ],
        out_shape=[
            pltpu.HBM((peers, slots, width), BF16),
            jax.ShapeDtypeStruct((lines, 128), jnp.int32),
        ],
        scratch_shapes=[VMEM((nodes // 2, 2 * width), BF16), VMEM(rows.shape, jnp.int32)],
        compiler_params=params(),
        name="outgoing_rows",
    )(flip, in_hbm(count), in_hbm(rows), in_hbm(feats))


def relative(row, base, start, window):
    return jnp.where((row >= base) & (row < start + window), row - start, -1)


def window_of(meta_ref, low_at, c, w, rows, window):
    base = meta_ref[low_at, c] // 128 * 128 + w * window
    return base, pl.multiple_of(jnp.minimum(base, rows - window), 128)


def windows_of(meta_ref, low_at, c, window):
    return (meta_ref[low_at + 1, c] - meta_ref[low_at, c] // 128 * 128) // window + 1


def keys_of(keys_ref, c, end):
    at = jnp.minimum(c, keys_ref.shape[0] - 1)
    return at, jnp.where(c < end, keys_ref[pl.ds(at, 1), :], PAD)


def gather_add(first, end, offset, window, low_at, meta_ref, keys_ref, table_ref, sum_ref, values_ref):
    half_nodes = sum_ref.shape[0]
    rows = table_ref.shape[0]
    half = window // 2

    def picked(c, w, col):
        base, start = window_of(meta_ref, low_at, c, w, rows, window)
        wide = join([table_ref[pl.ds(start, half), :], table_ref[pl.ds(start + half, half), :]])
        return pick(relative((col >> DST_BITS) - offset, base, start, window), wide)

    keys, cols = [], []
    for u in range(UNROLL):
        c, key = keys_of(keys_ref, first + u, end)
        keys.append(key)
        cols.append(columns_of(key))
        values_ref[u * CHUNK : (u + 1) * CHUNK, :] = picked(c, 0, cols[u])
    for u in range(UNROLL):
        c, key = keys_of(keys_ref, first + u, end)

        def more(w, _, c=c, key=key, u=u):
            values_ref[u * CHUNK : (u + 1) * CHUNK, :] += picked(c, w, columns_of(key))
            return 0

        lax.fori_loop(1, windows_of(meta_ref, low_at, c, window), more, 0)
    nodes = 2 * half_nodes
    sum_ref[...] += spread(
        join(keys) & (nodes - 1),
        jnp.concatenate(cols, axis=0) & (nodes - 1),
        values_ref[...].astype(BF16),
        half_nodes,
    )


def spread_add(first, end, offset, window, low_at, meta_ref, keys_ref, grad_ref, acc_ref, values_ref):
    nodes = 2 * grad_ref.shape[0]
    rows = acc_ref.shape[0]
    half = window // 2

    def add(c, w, key, col, values):
        base, start = window_of(meta_ref, low_at, c, w, rows, window)
        row, col = (
            relative((k >> DST_BITS) - offset, base, start, window) for k in (key, col)
        )
        both = spread(row, col, values, half)
        acc_ref[pl.ds(start, half), :] += both[:, :128]
        acc_ref[pl.ds(start + half, half), :] += both[:, 128:]

    keys = [keys_of(keys_ref, first + u, end) for u in range(UNROLL)]
    cols = [columns_of(key) for _, key in keys]
    values = pick(jnp.concatenate(cols, axis=0) & (nodes - 1), grad_ref[...]).astype(BF16)
    values_ref[...] = values
    for u, (c, key) in enumerate(keys):
        add(c, 0, key, cols[u], values[u * CHUNK : (u + 1) * CHUNK])
    for u in range(UNROLL):
        c, key = keys_of(keys_ref, first + u, end)

        def more(w, _, c=c, key=key, u=u):
            add(c, w, key, columns_of(key), values_ref[u * CHUNK : (u + 1) * CHUNK, :])
            return 0

        lax.fori_loop(1, windows_of(meta_ref, low_at, c, window), more, 0)


def over_chunks(first, end, visit):
    def step(i, _):
        visit(first + i * UNROLL)
        return 0

    lax.fori_loop(0, pl.cdiv(end - first, UNROLL), step, 0)


def near_forward_kernel(
    window, meta_ref, every_ref, keys_ref, table_ref, sum_hbm, deg_hbm, sum_ref, deg_ref, values_ref, sem
):
    nodes = 2 * sum_ref.shape[0]
    deg_ref[...] = jnp.zeros_like(deg_ref)
    sum_ref[...] = jnp.zeros_like(sum_ref)

    def degrees(c, _):
        key = join([every_ref[pl.ds(c * DEGREE_LINES + u, 1), :] for u in range(DEGREE_LINES)])
        dst = key & (nodes - 1)
        high = jnp.where(key < DEAD, dst >> 7, deg_ref.shape[0])
        deg_ref[...] += dot_nt(
            onehot_of_rows(high, deg_ref.shape[0]), onehot_of_rows(dst & 127, 128)
        )
        return 0

    lax.fori_loop(0, every_ref.shape[0] // DEGREE_LINES, degrees, 0)
    end = pl.cdiv(meta_ref[COUNTS, 0], CHUNK)
    over_chunks(
        0,
        end,
        lambda c: gather_add(
            c, end, 0, window, NEAR_LOW, meta_ref, keys_ref, table_ref, sum_ref, values_ref
        ),
    )
    copy_now(sum_ref, sum_hbm, sem)
    copy_now(deg_ref, deg_hbm, sem)


def near_forward(meta, every, keys, table, nodes, window=768):
    width = table.shape[1]
    shapes = [(nodes // 2, 2 * width), (16, 128)]
    return pl.pallas_call(
        functools.partial(near_forward_kernel, min(window, table.shape[0])),
        in_specs=[sspec(), vspec(), vspec(), vspec()],
        out_specs=[hbm_spec(), hbm_spec()],
        out_shape=[pltpu.HBM(shape, F32) for shape in shapes],
        scratch_shapes=[VMEM(shape, F32) for shape in shapes]
        + [VMEM((UNROLL * CHUNK, width), F32), pltpu.SemaphoreType.DMA],
        compiler_params=params(),
        name="near_forward",
    )(meta, every, keys, table)


def far_forward_kernel(
    offset, window, meta_ref, keys_ref, table_ref, base_hbm, sum_ref, values_ref, base_ref, sem
):
    base_copy = pltpu.make_async_copy(base_hbm, base_ref, sem)
    base_copy.start()
    sum_ref[...] = jnp.zeros_like(sum_ref)
    end = pl.cdiv(meta_ref[COUNTS, 1], CHUNK)
    over_chunks(
        meta_ref[COUNTS, 0] // CHUNK,
        end,
        lambda c: gather_add(
            c, end, offset, window, FAR_LOW, meta_ref, keys_ref, table_ref, sum_ref, values_ref
        ),
    )
    base_copy.wait()
    sum_ref[...] += base_ref[...]


def far_forward(meta, keys, table, base, offset, window=1280):
    return pl.pallas_call(
        functools.partial(far_forward_kernel, offset, min(window, table.shape[0])),
        in_specs=[sspec(), vspec(), vspec(), hbm_spec()],
        out_specs=vspec(),
        out_shape=jax.ShapeDtypeStruct(base.shape, F32),
        scratch_shapes=[
            VMEM((UNROLL * CHUNK, table.shape[1]), F32),
            VMEM(base.shape, F32),
            pltpu.SemaphoreType.DMA,
        ],
        compiler_params=params(),
        name="far_forward",
    )(meta, keys, table, in_hbm(base))


def dense_kernel(
    half_ref,
    mine_ref,
    other_ref,
    deg_ref,
    feat_ref,
    cot_ref,
    w_self_ref,
    w_neigh_ref,
    bias_ref,
    out_ref,
    grad_sum_ref,
    pre_ref,
    grad_w_ref,
    left_ref,
):
    nodes = feat_ref.shape[0]
    grad_bias = jnp.zeros((8, 128), F32)
    for at in range(0, nodes, 128):
        span = pl.ds(at, 128)
        h = at // 128
        divisor = jnp.maximum(columns_of(deg_ref[h : h + 1, :]), 1.0)
        feats = feat_ref[span, :]
        place = (pl.ds(at % (nodes // 2), 128), pl.ds(at // (nodes // 2) * 128, 128))
        aggregate = ((mine_ref[place] + other_ref[place]) / divisor).astype(BF16)
        preact = dot(feats, w_self_ref[...]) + dot(aggregate, w_neigh_ref[...]) + bias_ref[...]
        sig = jax.nn.sigmoid(preact)
        out_ref[span, :] = (preact * sig).astype(BF16)
        slope = sig * (1.0 + preact * (1.0 - sig))
        grad_pre = (cot_ref[span, :].astype(F32) * slope).astype(BF16)
        pre_ref[span, :] = grad_pre
        grad_sum_ref[place] = (dot_nt(grad_pre, w_neigh_ref[...]) / divisor).astype(BF16)
        left_ref[span, :] = jnp.where(half_ref[0] == 0, feats.astype(F32), aggregate.astype(F32)).astype(BF16)
        wide = grad_pre.astype(F32)
        for r in range(0, 128, 8):
            grad_bias = grad_bias + wide[r : r + 8]
    grad_w_ref[:128, :] = dot_tn(left_ref[...], pre_ref[...])
    grad_w_ref[128:, :] = jnp.broadcast_to(
        jnp.sum(grad_bias, axis=0, keepdims=True), (grad_w_ref.shape[0] - 128, 128)
    )


def dense(half, mine, other, deg, feats, cot, w_self, w_neigh, bias):
    nodes, width = feats.shape
    outs = [
        jax.ShapeDtypeStruct((nodes, width), BF16),
        jax.ShapeDtypeStruct((nodes // 2, 2 * width), BF16),
        jax.ShapeDtypeStruct((nodes, width), BF16),
        jax.ShapeDtypeStruct((192, width), F32),
    ]
    return pl.pallas_call(
        dense_kernel,
        grid=(1,),
        in_specs=[sspec()] + [whole(x) for x in (mine, other, deg, feats, cot, w_self, w_neigh, bias)],
        out_specs=[whole(x) for x in outs],
        out_shape=outs,
        scratch_shapes=[VMEM((nodes, width), BF16)],
        compiler_params=params(),
        name="dense_part",
    )(half, mine, other, in_hbm(deg), in_hbm(feats), in_hbm(cot), in_hbm(w_self), in_hbm(w_neigh), in_hbm(bias))


def far_backward_kernel(offset, window, meta_ref, keys_ref, grad_ref, out_ref, acc_ref, values_ref):
    rows = acc_ref.shape[0]
    block = out_ref.shape[0]

    @pl.when(pl.program_id(0) == 0)
    def _():
        def clear(b, _):
            span = pl.ds(pl.multiple_of(b * block, block), block)
            acc_ref[span, :] = jnp.zeros((block, acc_ref.shape[1]), F32)
            return 0

        lax.fori_loop(0, rows // block, clear, 0)
        end = pl.cdiv(meta_ref[COUNTS, 1], CHUNK)
        over_chunks(
            meta_ref[COUNTS, 0] // CHUNK,
            end,
            lambda c: spread_add(
                c, end, offset, window, FAR_LOW, meta_ref, keys_ref, grad_ref, acc_ref, values_ref
            ),
        )

    at = pl.multiple_of(pl.program_id(0) * block, block)
    out_ref[...] = acc_ref[pl.ds(at, block), :].astype(BF16)


def far_backward(meta, keys, grad_sum, offset, rows, window=1280):
    width = grad_sum.shape[1] // 2
    block = min(4096, rows)
    return pl.pallas_call(
        functools.partial(far_backward_kernel, offset, min(window, rows)),
        grid=(rows // block,),
        in_specs=[
            sspec(),
            pl.BlockSpec(keys.shape, lambda i: (0, 0)),
            pl.BlockSpec(grad_sum.shape, lambda i: (0, 0)),
        ],
        out_specs=pl.BlockSpec((block, width), lambda i: (i, 0)),
        out_shape=pltpu.HBM((rows, width), BF16),
        scratch_shapes=[VMEM((rows, width), F32), VMEM((UNROLL * CHUNK, width), BF16)],
        compiler_params=params(),
        name="far_backward",
    )(meta, keys, grad_sum)


def near_backward_kernel(
    window, half_ref, meta_ref, keys_ref, grad_ref, pre_ref, w_self_ref, out_ref, values_ref
):
    own_rows = pre_ref.shape[0] // 2
    mine = pl.ds(pl.multiple_of(half_ref[0] * own_rows, own_rows), own_rows)
    out_ref[:own_rows, :] = dot_nt(pre_ref[mine, :], w_self_ref[...])
    out_ref[own_rows:, :] = jnp.zeros((out_ref.shape[0] - own_rows, out_ref.shape[1]), F32)
    end = pl.cdiv(meta_ref[COUNTS, 0], CHUNK)
    over_chunks(
        0,
        end,
        lambda c: spread_add(
            c, end, 0, window, NEAR_LOW, meta_ref, keys_ref, grad_ref, out_ref, values_ref
        ),
    )


def near_backward(half, meta, keys, grad_sum, grad_pre, w_self, rows, window=768):
    width = grad_sum.shape[1] // 2
    return pl.pallas_call(
        functools.partial(near_backward_kernel, min(window, rows)),
        in_specs=[sspec(), sspec()] + [vspec()] * 4,
        out_specs=vspec(),
        out_shape=jax.ShapeDtypeStruct((rows, width), F32),
        scratch_shapes=[VMEM((UNROLL * CHUNK, width), BF16)],
        compiler_params=params(),
        name="near_backward",
    )(half, meta, keys, grad_sum, grad_pre, w_self)


def returned_kernel(peers_step, half_ref, idx_ref, back_ref, near_ref, part_ref, acc_ref):
    nodes = part_ref.shape[0]
    own_rows = nodes // 2
    peers, slots, width = back_ref.shape
    lines = peers_step * slots // 128
    acc_ref[...] = jnp.zeros_like(acc_ref)

    def step(s, _):
        row = join([idx_ref[pl.ds(s * lines + k, 1), :] for k in range(lines)])
        rows = back_ref[pl.ds(s * peers_step, peers_step), :, :].reshape(peers_step * slots, width)
        acc_ref[...] += spread(row, columns_of(row), rows, own_rows)
        return 0

    lax.fori_loop(0, peers // peers_step, step, 0)
    part_ref[:own_rows, :] = acc_ref[:, :width]
    part_ref[own_rows:, :] = acc_ref[:, width:]
    own_span = pl.ds(pl.multiple_of(half_ref[0] * own_rows, own_rows), own_rows)
    part_ref[own_span, :] += near_ref[:own_rows, :]


def returned_sum(half, idx, back, near, nodes):
    width = back.shape[2]
    return pl.pallas_call(
        functools.partial(returned_kernel, min(32, back.shape[0])),
        in_specs=[sspec(), vspec(), vspec(), vspec()],
        out_specs=vspec(),
        out_shape=jax.ShapeDtypeStruct((nodes, width), F32),
        scratch_shapes=[VMEM((nodes // 2, 2 * width), F32)],
        compiler_params=params(),
        name="returned_sum",
    )(half, idx, back, near)


def finish_kernel(hubs, z_ref, *refs):
    parts = refs[:-4]
    hubs_ref, self_ref, neigh_ref, bias_ref = refs[-4:]
    width = hubs_ref.shape[1]
    share = (parts[0].shape[0] - hubs) // 2
    hubs_ref[...] = pair_sum([part[:hubs, :] for part in parts])
    for j, part in enumerate(parts):
        for at in range(0, share, 8):
            row = (z_ref[0] ^ j) * share + at
            first = part[hubs + at : hubs + at + 8, :]
            second = part[hubs + share + at : hubs + share + at + 8, :]

            @pl.when(row < width)
            def _(row=row, first=first, second=second):
                rows = pl.ds(pl.multiple_of(row, 8), 8)
                self_ref[rows, :] = first
                neigh_ref[rows, :] = second

            @pl.when(row == width)
            def _(first=first):
                bias_ref[...] = first[:1, :]


def finish(z, parts, hubs):
    width = parts[0].shape[1]
    outs = [
        jax.ShapeDtypeStruct(shape, F32)
        for shape in ((hubs, width), (width, width), (width, width), (1, width))
    ]
    return pl.pallas_call(
        functools.partial(finish_kernel, hubs),
        in_specs=[sspec()] + [vspec()] * len(parts),
        out_specs=[vspec()] * 4,
        out_shape=outs,
        compiler_params=params(),
        name="finish",
    )(z, *parts)


def torus_of(size):
    side = 4 if size >= 64 else 2
    return side, size // (side * side), side


def groups_of(size, axis):
    sizes = torus_of(size)
    ids = np.arange(size).reshape(sizes)
    return np.moveaxis(ids, axis, -1).reshape(-1, sizes[axis]).tolist()


X_AXIS, Z_AXIS, Y_AXIS = 0, 1, 2


def exchange(blocks, axis, size):
    return lax.all_to_all(
        blocks, "dom", 0, 0, axis_index_groups=groups_of(size, axis), tiled=True
    )


def partners(size, axis):
    sizes = torus_of(size)
    step, count = {X_AXIS: sizes[1] * sizes[2], Z_AXIS: sizes[2], Y_AXIS: 1}[axis], sizes[axis]
    return [[(i, i ^ (step * j)) for i in range(size)] for j in range(1, count)]


def swap_blocks(blocks, axis, size):
    return [blocks[0]] + [
        lax.ppermute(block, "dom", pairs) for block, pairs in zip(blocks[1:], partners(size, axis))
    ]


def pair_sum(parts):
    while len(parts) > 1:
        parts = [parts[i] + parts[i + 1] for i in range(0, len(parts), 2)]
    return parts[0]


def split_exactly(value):
    high = lax.reduce_precision(value, 8, 7)
    middle = lax.reduce_precision(value - high, 8, 7)
    return [part.astype(BF16) for part in (high, middle, value - high - middle)]


def after(value, *earlier):
    return lax.optimization_barrier((value,) + earlier)[0]


def body(
    node_feats,
    hub_feats,
    w_self,
    w_neigh,
    bias,
    cotangent,
    send_count,
    send_rows,
    edge_src,
    edge_dst,
    edge_count,
):
    num_dom = lax.axis_size("dom")
    half = lax.axis_index("edge")
    nodes, width = node_feats.shape
    block_rows = send_rows.shape[2]
    hubs = hub_feats.shape[0]
    slots, half_hubs, own_rows = block_rows // 2, hubs // 2, nodes // 2
    half_scalar = half.astype(jnp.int32).reshape(1)
    xs, zs, ys = torus_of(num_dom)
    hub_rows = num_dom * half_hubs
    near_rows, far_rows = own_rows + hub_rows, num_dom * slots

    hub_z = exchange(jnp.broadcast_to(hub_feats[None], (zs,) + hub_feats.shape), Z_AXIS, num_dom)

    me = lax.axis_index("dom")
    counts_row = jnp.pad(send_count, ((0, 0), (0, -num_dom % 128)))
    flip = ((half ^ me) & 1).astype(jnp.int32).reshape(1)
    out_rows, idx = outgoing(flip, counts_row, send_rows[0], node_feats)
    out_rows, hub_z = lax.optimization_barrier((out_rows, hub_z))
    table = lax.all_to_all(out_rows, "dom", split_axis=0, concat_axis=0, tiled=True)
    hub_z = lax.dynamic_slice_in_dim(hub_z, half * half_hubs, half_hubs, 1)
    hub_z = hub_z.reshape(zs * half_hubs, width)
    hub_x = jnp.concatenate(swap_blocks([hub_z] * xs, X_AXIS, num_dom))
    hub_y = jnp.concatenate(swap_blocks([hub_x] * ys, Y_AXIS, num_dom))
    own_half = lax.dynamic_slice_in_dim(node_feats, half * own_rows, own_rows, 0)
    near_table = jnp.concatenate([own_half, hub_y.reshape(hub_rows, width)])

    src = edge_src.reshape(-1)
    dst = edge_dst.reshape(-1)
    edges = src.shape[0]
    live = jnp.arange(edges, dtype=jnp.int32) < edge_count.reshape(())
    slot = src - nodes
    hub = slot - num_dom * block_rows
    is_own, is_hub = src < nodes, hub >= 0
    master = hub // hubs
    far_y, far_x = (master ^ me) & (ys - 1), (master ^ me) // (ys * zs)
    master_place = (far_y * xs + far_x) * zs + (master // ys) % zs
    row = jnp.where(
        is_own,
        src % own_rows,
        jnp.where(
            is_hub,
            own_rows + master_place * half_hubs + hub % half_hubs,
            near_rows + slot // block_rows * slots + slot % slots,
        ),
    )
    slot_side = (slot // slots ^ slot // block_rows ^ me) & 1
    side = jnp.where(is_own, src // own_rows, jnp.where(is_hub, (hub % hubs) // half_hubs, slot_side))
    key = (side << HALF_BIT) + (row << DST_BITS) + dst
    key = after(jnp.where(live, key, DEAD), out_rows)
    key_other = lax.ppermute(key, "edge", SWAP)
    every = jnp.concatenate([key, key_other])
    mine = jnp.where((every >> HALF_BIT) == half, every & ((1 << HALF_BIT) - 1), PAD)
    keys = lax.sort(mine).reshape(-1, CHUNK)
    every = every.reshape(-1, CHUNK)
    near_edge = keys < (near_rows << DST_BITS)
    live_edge = keys < PAD
    counts = [jnp.sum(edge.astype(jnp.int32)) for edge in (near_edge, live_edge)]
    near_low = jnp.minimum(keys[:, 0] >> DST_BITS, near_rows - 1)
    near_high = jnp.max(jnp.where(near_edge, keys, 0), axis=1) >> DST_BITS
    far_low = jnp.min(jnp.where(near_edge, PAD, keys), axis=1) >> DST_BITS
    far_low = jnp.minimum(far_low - near_rows, far_rows - 1)
    far_high = jnp.max(jnp.where(live_edge, keys, 0), axis=1) >> DST_BITS
    far_high = jnp.maximum(far_high - near_rows, 0)

    lines = keys.shape[0]
    counts = jnp.where(jnp.arange(lines) == 0, counts[0], counts[1])
    meta = jnp.stack([near_low, near_high, far_low, far_high, counts])

    near_sum, degree = near_forward(meta, every, keys, near_table, nodes)
    neigh = far_forward(meta, keys, table.reshape(far_rows, width), near_sum, near_rows)
    neigh_other = lax.ppermute(neigh, "edge", SWAP)
    layer_out, grad_sum, grad_pre, grad_w = dense(
        half_scalar,
        neigh,
        neigh_other,
        degree,
        node_feats,
        cotangent,
        w_self,
        w_neigh,
        bias.reshape(1, width),
    )
    share = grad_w.shape[0] // zs
    grad_w = exchange(grad_w.reshape(zs, share, width), Z_AXIS, num_dom)
    row_grads = far_backward(meta, keys, grad_sum, near_rows, far_rows)
    row_grads, grad_w = lax.optimization_barrier((row_grads, grad_w))
    back = lax.all_to_all(
        row_grads.reshape(num_dom, slots, width), "dom", split_axis=0, concat_axis=0, tiled=True
    )
    near_grads = near_backward(
        half_scalar, meta, after(keys, row_grads), grad_sum, grad_pre, w_self, near_rows
    )

    grad_w = jnp.sum(grad_w, axis=0)
    blocks = jnp.split(near_grads[own_rows:].astype(BF16), ys)
    kept = blocks[0].shape[0]
    pieces = split_exactly(grad_w)
    both = swap_blocks([jnp.concatenate([block] + pieces) for block in blocks], Y_AXIS, num_dom)
    both = [part.astype(F32) for part in both]
    hub_part = pair_sum([part[:kept] for part in both])
    grad_w = pair_sum(
        [part[kept : kept + share] + (part[kept + share : -share] + part[-share:]) for part in both]
    )
    blocks = jnp.split(hub_part, xs)
    kept = blocks[0].shape[0]
    both = pair_sum(
        swap_blocks([jnp.concatenate([block, grad_w]) for block in blocks], X_AXIS, num_dom)
    )
    other = lax.ppermute(both, "edge", SWAP)
    first = jnp.where(half == 0, both, other)
    second = jnp.where(half == 0, other, both)
    shares = jnp.concatenate([first[kept:], second[kept:]])
    z = (me // ys) % zs
    hub_blocks = jnp.concatenate(
        [half_part[:kept].reshape(zs, half_hubs, width) for half_part in (first, second)], axis=1
    )
    blocks = [
        jnp.concatenate([lax.dynamic_index_in_dim(hub_blocks, z ^ j, keepdims=False), shares])
        for j in range(zs)
    ]
    blocks = swap_blocks(blocks, Z_AXIS, num_dom)
    back, *blocks = lax.optimization_barrier((back, *blocks))
    part = returned_sum(half_scalar, idx, back, near_grads, nodes)
    part_other = lax.ppermute(part, "edge", SWAP)
    grad_feats = part + part_other
    grad_hubs, grad_self, grad_neigh, grad_bias = finish(
        z.astype(jnp.int32).reshape(1), blocks, hubs
    )
    return (layer_out, grad_feats, grad_hubs, grad_self, grad_neigh, grad_bias.reshape(width))


def solution(mesh):
    placed = (
        P("dom", None),
        P("dom", None),
        P(),
        P(),
        P(),
        P("dom", None),
        P("dom", None),
        P("dom", None, None),
        P("dom", "edge", None),
        P("dom", "edge", None),
        P("dom", "edge"),
    )
    return jax.shard_map(
        body,
        mesh=mesh,
        in_specs=placed,
        out_specs=(P("dom", None), P("dom", None), P("dom", None), P(), P(), P()),
        check_vma=False,
    )
```
